32 devices in a mesh: gx: 4 (over x, core), gy: 8 (over z, y).
Axes of the slice: x: 2, y: 2, z: 4, core: 2. Of those that a mesh axis runs over, the one named last changes fastest.
Arguments:
- particles: float32 [16, 262144], P(None, ('gx', 'gy')), may hold values from -10 to 10
- migrant_index: int32 [128, 512], P(('gx', 'gy')), may hold values from 0 to 8191, as said below
- migrant_count: int32 [32, 4], P(('gx', 'gy')), may hold values from 170 to 512, as said below
- migrated_slot_cell: int32 [327680], P(('gx', 'gy')), may hold values from 0 to 12287
- source_tile_size: int32 [32, 256], P(('gx', 'gy')), may hold values from 1 to 64, 12288 in all within a row
- tile_owner: int32 [8192, 1], P(('gx', 'gy')), may hold values from 0 to 31; in each aligned block of 256 rows (0 to 255, 256 to 511, ...) at most 16 rows name the same one
- tile_offset: int32 [8192], P(('gx', 'gy')), may hold values from 0 to 8128, as said below
- closure: float32 [8, 16], replicated, may hold values from -1.5 to 1.5
- damping: float32 [8], replicated, may hold values from 0.5 to 1.5
Outputs:
- drag_field: bfloat16 [8, 32, 64, 128], P(None, 'gx', 'gy')
- particle_force: float32 [8, 327680], P(None, ('gx', 'gy'))
The draws below stay inside these ranges and needn't reach their ends.
Inputs may be any that keep to these rules, and one draw needn't show every extreme that they name: `migrant_index`: on each device the first migrant_count entries of its four rows name distinct particles of that device. `migrant_count`: some device's count reaches 512. `source_tile_size`: the sizes of one device sum to 12288. `tile_owner`: among the tiles of one device no owner is named more than 16 times, a bound that some block reaches. Every tile lies in one vertical column of its owner's block: tile_offset % 128 + 64 <= 128.
All inputs are finite; a program needn't handle non-finite values.
Results may differ from the reference program's by a relative error of at most 0.0053.
Values may be sent and summed in bfloat16 or wider, within the bound.
No kernel may reach another device: no remote copies, remote signals or barrier semaphores. Data moves between devices by JAX's collectives and lax.ppermute only.
A program may use at most 64 MiB of HBM per device.

```python
import math
import jax
import jax.numpy as jnp
import numpy as np
from jax import lax

CHANNELS = 16
DRAG_CH = 8
PART_DEV = 8192
MIGRANTS = 512
SOURCE_TILES = 256
MAX_TILE_CELLS = 64
FX = 8
FY = 8
FZ = 128
PARTICLE_CELLS = 12288
CAP = 16
TILES = 8192
PARTICLES = 262144
MIGRATED_SLOTS = 327680
N_GX = 4
N_GY = 8


def draw_migrant_index(key, part):
    devices = N_GX * N_GY
    keys = jax.random.split(key, devices)

    def choose(single):
        return jax.random.permutation(single, PART_DEV)[:4 * MIGRANTS]
    picked = jax.vmap(choose)(keys)
    return picked.reshape(devices * 4, MIGRANTS).astype(jnp.int32)


def draw_migrant_count(key, part):
    devices = N_GX * N_GY
    counts = jax.random.randint(key, (devices, 4), MIGRANTS // 3, MIGRANTS + 1)
    return counts.at[0, 0].set(MIGRANTS).astype(jnp.int32)


def draw_tile_offset(key, part):
    first_key = jax.random.fold_in(key, 11)
    second_key = jax.random.fold_in(key, 23)
    total_tiles = SOURCE_TILES * N_GX * N_GY
    column = jax.random.randint(first_key, (total_tiles,), 0, FX * FY)
    height = jax.random.randint(second_key, (total_tiles,), 0, FZ - MAX_TILE_CELLS + 1)
    return (column * FZ + height).astype(jnp.int32)


def place_ends(result, stream_key, smallest, largest):
    spot = [jax.random.randint(jax.random.fold_in(stream_key, axis), (), 0, length) for axis, length in enumerate(result.shape)]
    widest = result.shape.index(max(result.shape))
    next_to = spot[:widest] + [(spot[widest] + 1) % result.shape[widest]] + spot[widest + 1:]
    return result.at[tuple(spot)].set(smallest).at[tuple(next_to)].set(largest)


def levels(stream_key, extent, pieces, low, high):
    def one(position, blocks):
        heights = jax.random.uniform(jax.random.fold_in(jax.random.fold_in(stream_key, 6), position), (blocks,), jnp.float32, low / len(pieces), high / len(pieces))
        return jnp.repeat(jnp.exp(heights), extent[position] // blocks).reshape((-1,) + (1,) * (len(extent) - position - 1))

    loudness = one(*pieces[0])
    for cut in pieces[1:]:
        loudness = loudness * one(*cut)
    return loudness


def profile(count, total, reach, lean):
    loads = [(1 << 20) // math.isqrt(standing ** lean) + 1 for standing in range(2, count + 1)]
    spare, given = total - reach - (count - 1), [1] * (count - 1)
    while spare > 0:
        free = [i for i in range(count - 1) if given[i] < reach]
        mass, budget = sum([loads[i] for i in free]), spare
        for i in free:
            extra = min(reach - given[i], max(1, budget * loads[i] // mass), spare)
            given[i] = given[i] + extra
            spare = spare - extra
    return np.array([reach] + given)


def ragged_sizes(key, number_of, total, most, slope):
    if number_of == 2:
        one = jax.random.randint(key, (), max(1, total - most), min(most, total - 1) + 1)
        return jnp.stack([one, total - one])
    tallies = jnp.asarray(profile(number_of, total, most, slope), jnp.int32)
    twos = (number_of - 1) // 2
    giver, receiver = tallies[1:1 + 2 * twos:2], tallies[2:2 + 2 * twos:2]
    slack = jnp.minimum(giver - 1, most - receiver)
    moved = jax.random.randint(jax.random.fold_in(key, 1), (twos,), 0, 1 << 20) % (slack + 1)
    tallies = tallies.at[1:1 + 2 * twos:2].set(giver - moved).at[2:2 + 2 * twos:2].set(receiver + moved)
    return tallies[jax.random.permutation(jax.random.fold_in(key, 2), number_of)]


def shared_out(rng, own, number, rows, count, top, limit, slope):
    ranking = jax.random.permutation(rng, count)
    heavy_load, ordinary = load_shares(count, rows * top, limit, slope, True), load_shares(count, rows * top, limit, slope, False)
    places = jnp.arange(count)

    def named(sizes, turn):
        used = int((sizes > 0).sum())
        fixed = max(1, used // 4)
        shifted = fixed + (places - fixed + turn * (used - fixed)) % max(1, count - fixed)
        return jnp.zeros((count,), jnp.int32).at[ranking[jnp.where(places < fixed, places, shifted)]].set(jnp.asarray(sizes, jnp.int32))

    sizes = jnp.where(number % 4 == 0, named(heavy_load, number // 4), named(ordinary, number - number // 4 - 1))
    mixed = jax.random.permutation(jax.random.fold_in(own, 3), count)
    source_of, taker = mixed[0:count // 2 * 2:2], mixed[1:count // 2 * 2:2]
    room = jnp.minimum(sizes[source_of] - 1, limit - sizes[taker]) // 2
    room = jnp.where((source_of == ranking[0]) | (taker == ranking[0]) | (sizes[taker] == 0), 0, jnp.maximum(room, 0))
    shifted = jax.random.randint(jax.random.fold_in(own, 4), (count // 2,), 0, 1 << 20) % (room + 1)
    sizes = sizes.at[source_of].add(-shifted).at[taker].add(shifted)
    items = jnp.searchsorted(jnp.cumsum(sizes), jnp.arange(rows * top), side="right").astype(jnp.int32)
    listing = items.reshape(top, rows).T
    listing = listing[jax.random.permutation(jax.random.fold_in(own, 1), rows)]
    turn = jax.random.randint(jax.random.fold_in(own, 2), (rows, 1), 0, top)
    return jnp.take_along_axis(listing, (jnp.arange(top)[None, :] + turn) % top, axis=1)


def load_shares(number_of, total, limit, slope, full):
    loads = [(1 << 20) // math.isqrt(standing ** slope) + 1 for standing in range(1, number_of + 1)]
    largest = limit if full else min(limit, max(-(-total // number_of), total * loads[0] // sum(loads)))
    least = 1 if total - largest >= number_of - 1 else 0
    given, rest = [largest] + [least] * (number_of - 1), total - largest - least * (number_of - 1)
    while rest > 0:
        candidates = [i for i in range(1, number_of) if given[i] < largest] or [i for i in range(1, number_of) if given[i] < limit]
        pool, budget = sum([loads[i] for i in candidates]), rest
        for i in candidates:
            more = min(limit - given[i], max(1, budget * loads[i] // pool), rest)
            given[i] = given[i] + more
            rest = rest - more
    return np.array(given)


def noise(key, dims, spread, bound, shards=(), held_as=jnp.bfloat16):
    result = jax.random.normal(key, dims, jnp.float32) * spread
    if len(shards) > 0:
        result = levels(key, dims, shards, -0.22, 0.18) * result
    return jnp.clip(result, min=-bound, max=bound).astype(held_as)


def setup_inputs(seed: int = 0) -> dict:
    arg_keys = jax.random.split(jax.random.key(seed), 10)
    particles = noise(arg_keys[0], (CHANNELS, PARTICLES), 2.0, 10.0, ((1, 32),), jnp.float32)
    migrant_index = draw_migrant_index(jax.random.fold_in(arg_keys[9], 71), 0)
    migrant_count = draw_migrant_count(jax.random.fold_in(arg_keys[9], 71), 0)
    migrated_slot_cell = place_ends(jax.random.randint(arg_keys[3], (MIGRATED_SLOTS,), 0, PARTICLE_CELLS), jax.random.fold_in(arg_keys[3], 1), 0, PARTICLE_CELLS - 1).astype(jnp.int32)
    source_tile_size = jax.vmap(lambda own: ragged_sizes(own, SOURCE_TILES, PARTICLE_CELLS, MAX_TILE_CELLS, 1))(jax.random.split(arg_keys[4], (N_GX * N_GY))).reshape((N_GX * N_GY, SOURCE_TILES)).astype(jnp.int32)
    tile_owner_keys = jax.random.split(jax.random.fold_in(arg_keys[5], 1), TILES // SOURCE_TILES)
    tile_owner_turns = jax.random.permutation(jax.random.fold_in(arg_keys[5], 3), TILES // SOURCE_TILES)
    tile_owner = jax.vmap(lambda own, number: shared_out(jax.random.fold_in(arg_keys[5], 2), own, number, SOURCE_TILES, N_GX * N_GY, 1, CAP, 2))(tile_owner_keys, tile_owner_turns).reshape((TILES, 1))
    tile_offset = draw_tile_offset(jax.random.fold_in(arg_keys[9], 71), 0)
    closure = noise(arg_keys[7], (DRAG_CH, CHANNELS), CHANNELS ** -0.5, 1.5, (), jnp.float32)
    damping = jnp.clip(1.0 + 0.1 * jax.random.normal(arg_keys[8], (DRAG_CH,), jnp.float32), 0.5, 1.5)
    return {"particles": particles, "migrant_index": migrant_index, "migrant_count": migrant_count, "migrated_slot_cell": migrated_slot_cell, "source_tile_size": source_tile_size, "tile_owner": tile_owner, "tile_offset": tile_offset, "closure": closure, "damping": damping}


def reference(particles, migrant_index, migrant_count, migrated_slot_cell, source_tile_size, tile_owner, tile_offset, closure, damping):
    devices = N_GX * N_GY
    channel_count = particles.shape[0]
    drag_row_values = closure.shape[0]
    slots_dev = PART_DEV + 4 * MIGRANTS
    fluid_cells = FX * FY * FZ
    per_dev = particles.reshape(channel_count, devices, PART_DEV).transpose(1, 0, 2)
    lists = migrant_index.reshape(devices, 4, MIGRANTS).astype(jnp.int32)
    valid_rows = jnp.arange(MIGRANTS, dtype=jnp.int32)[None, None, :] < migrant_count[:, :, None]
    leaving = jnp.where(valid_rows, lists, PART_DEV).astype(jnp.int32)

    def clear_rows(rows):
        return jnp.ones((PART_DEV,), jnp.float32).at[rows.reshape(-1)].set(0.0, mode="drop")

    resident_live = jax.vmap(clear_rows)(leaving)
    picked = jax.vmap(lambda block, rows: block[:, rows])(per_dev, lists)
    outgoing = jnp.where(valid_rows[:, :, None, :], picked.transpose(0, 2, 1, 3), 0.0)
    sent_live = valid_rows.astype(jnp.float32)

    def arrive(cell_values):
        grid = cell_values.reshape((N_GX, N_GY) + cell_values.shape[1:])
        moved = jnp.stack([jnp.roll(grid[:, :, 0], 1, axis=0), jnp.roll(grid[:, :, 1], -1, axis=0),
                           jnp.roll(grid[:, :, 2], 1, axis=1), jnp.roll(grid[:, :, 3], -1, axis=1)], axis=2)
        return moved.reshape((devices,) + cell_values.shape[1:])

    arrived_state = arrive(outgoing).transpose(0, 2, 1, 3).reshape(devices, channel_count, 4 * MIGRANTS)
    arrived_live = arrive(sent_live).reshape(devices, 4 * MIGRANTS)
    slot_state = jnp.concatenate([per_dev, arrived_state], axis=2)
    slot_live = jnp.concatenate([resident_live, arrived_live], axis=1)
    deposit = (slot_state * slot_live[:, None, :]).astype(jnp.bfloat16)
    cell_rows = migrated_slot_cell.reshape(devices, slots_dev)

    def deposit_one(cell_values, cell_index_list):
        return jax.ops.segment_sum(cell_values.T.astype(jnp.float32), cell_index_list, num_segments=PARTICLE_CELLS)

    source_field = jax.vmap(deposit_one)(deposit, cell_rows)
    sizes = source_tile_size.astype(jnp.int32)
    tile_starts = jnp.cumsum(sizes, axis=1).astype(jnp.int32) - sizes

    def tile_ids(tile_sizes_row):
        return jnp.repeat(jnp.arange(SOURCE_TILES, dtype=jnp.int32), tile_sizes_row, total_repeat_length=PARTICLE_CELLS)

    cell_tile_index = jax.vmap(tile_ids)(sizes).astype(jnp.int32)
    within_tile_mask = jnp.arange(PARTICLE_CELLS, dtype=jnp.int32)[None, :] - jnp.take_along_axis(tile_starts, cell_tile_index, axis=1)
    owners = tile_owner.reshape(devices, SOURCE_TILES).astype(jnp.int32)
    offsets = tile_offset.reshape(devices, SOURCE_TILES).astype(jnp.int32)
    target_cells = (jnp.take_along_axis(owners, cell_tile_index, axis=1) * fluid_cells
              + jnp.take_along_axis(offsets, cell_tile_index, axis=1) + within_tile_mask).astype(jnp.int32)
    gas_flat = jnp.zeros((devices * fluid_cells, channel_count), jnp.float32).at[target_cells.reshape(-1)].add(
        source_field.reshape(-1, channel_count))
    gas_source = gas_flat.reshape(N_GX, N_GY, FX, FY, FZ, channel_count).transpose(5, 0, 2, 1, 3, 4).reshape(
        channel_count, N_GX * FX, N_GY * FY, FZ)
    weights = (1.0, 2.0, 1.0)
    smoothed = jnp.zeros_like(gas_source)
    for first in range(3):
        for second in range(3):
            moved = jnp.roll(jnp.roll(gas_source, 1 - first, axis=1), 1 - second, axis=2)
            smoothed = smoothed + (weights[first] * weights[second] / 16.0) * moved
    mixed = jnp.einsum("rf,fxyz->rxyz", closure, smoothed, precision=lax.Precision.HIGHEST)
    drag_field = (mixed / (1.0 + smoothed[0] * smoothed[0])).astype(jnp.bfloat16)
    flattened_drag = drag_field.reshape(drag_row_values, N_GX, FX, N_GY, FY, FZ).transpose(1, 3, 2, 4, 5, 0).reshape(
        devices * fluid_cells, drag_row_values)
    particle_drag = flattened_drag[target_cells]
    looked_values = jax.vmap(lambda lookup_table, cell_index_list: lookup_table[cell_index_list])(particle_drag, cell_rows).astype(jnp.float32)
    slip = slot_state[:, :drag_row_values, :].transpose(0, 2, 1)
    force = slot_live[:, :, None] * (looked_values - damping[None, None, :] * slip)
    particle_force = force.transpose(2, 0, 1).reshape(drag_row_values, devices * slots_dev)
    return drag_field, particle_force
```

```python
import functools

import jax
import jax.numpy as jnp
from jax import lax
from jax.experimental import pallas as pl
from jax.experimental.pallas import tpu as pltpu
from jax.sharding import PartitionSpec as P

TILE = 64
FX = 8
FY = 8
FZ = 128
COLS = FX * FY
LANES = 128
GROUP = 256
CHUNK = 1024
VMEM = 48 * 1024 * 1024

NT = (((1,), (1,)), ((), ()))
TN = (((0,), (0,)), ((), ()))


def iota(shape, dim):
    return lax.broadcasted_iota(jnp.int32, shape, dim)


def dot(a, b, dims=(((1,), (0,)), ((), ()))):
    return lax.dot_general(a, b, dims, preferred_element_type=jnp.float32)


def one_hot(mask):
    return jnp.where(mask, 1.0, 0.0).astype(jnp.bfloat16)


def pick_kernel(part_ref, index_ref, count_ref, *out_refs):
    channels, parts = part_ref.shape
    migr = index_ref.shape[1]
    groups = parts // GROUP
    table = jnp.concatenate(
        [part_ref[:, g * GROUP : (g + 1) * GROUP].astype(jnp.bfloat16) for g in range(groups)], axis=0
    )
    for row in range(4):
        index = index_ref[row : row + 1, :]
        count = count_ref[0, row]
        low = one_hot(iota((GROUP, migr), 0) == index % GROUP)
        rows = dot(table, low)
        high = index // GROUP
        high = jnp.where(iota((1, migr), 1) < count, high, groups)
        picked = jnp.zeros((channels, migr), jnp.float32)
        for g in range(groups):
            picked = picked + jnp.where(high == g, rows[g * channels : (g + 1) * channels], 0.0)
        out_refs[row][:, :migr] = picked.astype(jnp.bfloat16)
        digits = jnp.where(iota((channels, LANES), 0) == 0, count // GROUP, count % GROUP)
        out_refs[row][:, migr:] = digits.astype(jnp.float32).astype(jnp.bfloat16)


def mix(closure_ref, state):
    state = state.astype(jnp.float32)
    mixed = closure_ref[:, 0:1] * state[0:1]
    for f in range(1, state.shape[0]):
        mixed = mixed + closure_ref[:, f : f + 1] * state[f : f + 1]
    return mixed, state[0:1]


def spread(mixed, first, place, width):
    hit = iota((TILE, width), 0) == place
    rows = [
        jnp.where(hit, mixed[r : r + 1], 0.0).astype(jnp.bfloat16) for r in range(mixed.shape[0])
    ]
    rows.append(jnp.where(hit, first, 0.0).astype(jnp.bfloat16))
    return jnp.concatenate(rows, axis=0)


def deposit_kernel(
    capacity, part_ref, index_ref, count_ref, cell_ref, size_ref, owner_ref, offset_ref, closure_ref,
    sum_ref, live_ref, code_ref, slot_ref, columns_ref,
):
    channels, parts = part_ref.shape
    migr = index_ref.shape[1]
    slots = cell_ref.shape[1]
    tiles = size_ref.shape[1]
    groups = parts // GROUP

    square = (tiles, tiles)
    below, across = iota(square, 0), iota(square, 1)
    same = below == across

    def column(row):
        return jnp.sum(jnp.where(same, row, 0), axis=1, keepdims=True)

    sizes = size_ref[...]
    owners = owner_ref[...]
    start = jnp.sum(jnp.where(across < below, sizes, 0), axis=1, keepdims=True)
    end = start + column(sizes)
    height = column(offset_ref[...] % FZ)
    code = iota((tiles, 1), 0) * TILE + (height - start) % TILE
    earlier = (column(owners) == owners) & (below < across)
    rank = jnp.sum(jnp.where(earlier, 1, 0), axis=0, keepdims=True)
    slot_ref[...] = owners * capacity + rank
    columns_ref[0] = jnp.broadcast_to(start, (tiles, LANES))
    columns_ref[1] = jnp.broadcast_to(end, (tiles, LANES))
    columns_ref[2] = jnp.broadcast_to(code, (tiles, LANES))

    hits = jnp.zeros((groups, GROUP), jnp.float32)
    for row in range(4):
        index = index_ref[row : row + 1, :]
        valid = iota((1, migr), 1) < count_ref[0, row]
        high = one_hot(iota((groups, migr), 0) == jnp.where(valid, index // GROUP, groups))
        low = one_hot(iota((GROUP, migr), 0) == index % GROUP)
        hits = hits + dot(high, low, NT)
    for g in range(groups):
        live_ref[:, g * GROUP : (g + 1) * GROUP] = 1.0 - hits[g : g + 1]

    def member(cell):
        def wide(k):
            return jnp.concatenate([columns_ref[k]] * (CHUNK // LANES), axis=1)

        inside = (cell >= wide(0)) & (cell < wide(1))
        found = jnp.sum(jnp.where(inside, wide(2), 0), axis=0, keepdims=True)
        place = (found + cell) % TILE
        return inside, found // TILE * TILE + place, place

    sum_ref[...] = jnp.zeros_like(sum_ref)

    @pl.loop(0, parts // CHUNK)
    def _(step):
        where = pl.ds(pl.multiple_of(step * CHUNK, CHUNK), CHUNK)
        inside, full, place = member(cell_ref[:, where])
        code_ref[:, where] = full
        state = (part_ref[:, where] * live_ref[:, where]).astype(jnp.bfloat16)
        mixed, first = mix(closure_ref, state)
        sum_ref[...] += dot(spread(mixed, first, place, CHUNK), one_hot(inside), NT)

    @pl.loop(parts // CHUNK, slots // CHUNK)
    def _(step):
        where = pl.ds(pl.multiple_of(step * CHUNK, CHUNK), CHUNK)
        _, full, _ = member(cell_ref[:, where])
        code_ref[:, where] = full


def pack_kernel(sum_ref, code_ref, slot_ref, offset_ref, closure_ref, *refs):
    state_refs, out_ref = refs[:4], refs[4]
    tiles = slot_ref.shape[1]
    migr = code_ref.shape[1] // 4
    total = sum_ref[...]
    for row in range(4):
        code = code_ref[:, row * migr : (row + 1) * migr]
        inside = iota((tiles, migr), 0) == code // TILE
        mixed, first = mix(closure_ref, state_refs[row][:, :migr])
        total = total + dot(spread(mixed, first, code % TILE, migr), one_hot(inside), NT)
    offset = offset_ref[...]
    spare = out_ref.shape[1] - total.shape[0]
    rows = iota((spare, tiles), 0)
    marks = jnp.where(rows == 0, offset // FZ, jnp.where(rows == 1, offset % FZ, 0))
    table = jnp.concatenate(
        [total.astype(jnp.bfloat16), marks.astype(jnp.float32).astype(jnp.bfloat16)], axis=0
    )
    match = one_hot(iota((out_ref.shape[0], tiles), 0) == slot_ref[...])
    out_ref[...] = dot(match, table, NT).astype(jnp.bfloat16)


def place_kernel(tile_ref, gas_ref, xlow_ref, xhigh_ref, ylow_ref, yhigh_ref):
    count, lanes = tile_ref.shape
    width = gas_ref.shape[1] // 2
    marks = tile_ref[:, lanes - LANES :].astype(jnp.float32)
    column = marks[:, width % LANES : width % LANES + 1]
    height = marks[:, width % LANES + 1 : width % LANES + 2]
    lane = iota((1, LANES), 1)
    target = jnp.where(
        lane < COLS,
        lane,
        jnp.where(
            lane < COLS + FX,
            (lane - COLS) * FY,
            jnp.where(lane < COLS + 2 * FX, (lane - COLS - FX) * FY + FY - 1, -1),
        ),
    )
    hot = one_hot(column == target.astype(jnp.float32))
    place = (iota((1, width), 1) % TILE).astype(jnp.float32)
    values = tile_ref[:, :width].astype(jnp.float32)
    for half, mask in enumerate((place >= height, place < height)):
        total = dot(hot, jnp.where(mask, values, 0.0).astype(jnp.bfloat16), TN)
        where = slice(half * width, (half + 1) * width)
        gas_ref[:, where] = total[:COLS]
        xlow_ref[:, where] = total[:FY]
        xhigh_ref[:, where] = total[COLS - FY : COLS]
        ylow_ref[:, where] = total[COLS : COLS + FX]
        yhigh_ref[:, where] = total[COLS + FX : COLS + 2 * FX]


def drag_kernel(mark_ref, gas_ref, xm_ref, xp_ref, ym_ref, yp_ref, drag_ref, back_ref):
    rows = drag_ref.shape[0]
    width = gas_ref.shape[1] // 2
    lanes = rows * TILE
    blocks = [xm_ref[...]] + [gas_ref[x * FY : (x + 1) * FY, :] for x in range(FX)] + [xp_ref[...]]
    along = [blocks[x] + 2.0 * blocks[x + 1] + blocks[x + 2] for x in range(FX)]

    def edge(ref):
        return ref[0:FX, :] + 2.0 * ref[1 : FX + 1, :] + ref[2 : FX + 2, :]

    before, after = edge(ym_ref), edge(yp_ref)
    smooth = []
    for x in range(FX):
        padded = jnp.concatenate([before[x : x + 1], along[x], after[x : x + 1]], axis=0)
        smooth.append((padded[0:FY] + 2.0 * padded[1 : FY + 1] + padded[2 : FY + 2]) / 16.0)
    smooth = jnp.concatenate(smooth, axis=0)
    halves = []
    for half in range(2):
        base = half * width
        density = smooth[:, base + lanes : base + lanes + TILE]
        below = 1.0 + density * density
        below = jnp.concatenate([below] * rows, axis=1)
        halves.append(smooth[:, base : base + lanes] / below)
    for r in range(rows):
        where = slice(r * TILE, (r + 1) * TILE)
        both = jnp.concatenate([halves[0][:, where], halves[1][:, where]], axis=1)
        drag_ref[r] = both.reshape(FX, FY, FZ).astype(jnp.bfloat16)
    mark = width % LANES
    marks = mark_ref[...].astype(jnp.float32)
    column, height = marks[:, mark : mark + 1], marks[:, mark + 1 : mark + 2]
    hot = one_hot(column == iota((1, COLS), 1).astype(jnp.float32))
    place = (iota((1, lanes), 1) % TILE).astype(jnp.float32)
    low = dot(hot, halves[0].astype(jnp.bfloat16))
    high = dot(hot, halves[1].astype(jnp.bfloat16))
    back_ref[...] = jnp.where(place >= height, low, high).astype(jnp.bfloat16)


def force_kernel(back_ref, slot_ref, code_ref, live_ref, part_ref, damping_ref, *refs):
    state_refs, out_ref, table_ref = refs[:4], refs[4], refs[5]
    rows, slots = out_ref.shape
    parts = part_ref.shape[1]
    tiles = slot_ref.shape[1]
    migr = (slots - parts) // 4
    match = one_hot(iota((back_ref.shape[0], tiles), 0) == slot_ref[...])
    table_ref[...] = dot(back_ref[...], match, TN).astype(jnp.bfloat16)
    damping = damping_ref[...]

    def look(code, width):
        inside = one_hot(iota((tiles, width), 0) == code // TILE)
        values = dot(table_ref[...], inside)
        hit = iota((TILE, width), 0) == code % TILE
        return jnp.concatenate(
            [
                jnp.sum(jnp.where(hit, values[r * TILE : (r + 1) * TILE], 0.0), axis=0, keepdims=True)
                for r in range(rows)
            ],
            axis=0,
        )

    @pl.loop(0, parts // CHUNK)
    def _(step):
        where = pl.ds(pl.multiple_of(step * CHUNK, CHUNK), CHUNK)
        drag = look(code_ref[:, where], CHUNK)
        out_ref[:, where] = live_ref[:, where] * (drag - damping * part_ref[:, where])

    for row in range(4):
        begin = parts + row * migr
        drag = look(code_ref[:, begin : begin + migr], migr)
        arrived = state_refs[row][:, :].astype(jnp.float32)
        count = arrived[0:1, migr : migr + 1] * GROUP + arrived[1:2, migr : migr + 1]
        live = iota((1, migr), 1).astype(jnp.float32) < count
        force = drag - damping * arrived[:rows, :migr]
        out_ref[:, begin : begin + migr] = jnp.where(live, force, 0.0)


def call(kernel, shapes, *operands, smem=(), scratch=()):
    in_specs = [
        pl.BlockSpec(memory_space=pltpu.SMEM if i in smem else pltpu.VMEM)
        for i in range(len(operands))
    ]
    return pl.pallas_call(
        kernel,
        out_shape=shapes,
        in_specs=in_specs,
        out_specs=[pl.BlockSpec(memory_space=pltpu.VMEM) for _ in shapes],
        scratch_shapes=scratch,
        compiler_params=pltpu.CompilerParams(vmem_limit_bytes=VMEM),
    )(*operands)


def shift(block, axis, step):
    size = lax.axis_size(axis)
    return lax.ppermute(block, axis, [(i, (i + step) % size) for i in range(size)])


def per_device(
    particles,
    migrant_index,
    migrant_count,
    migrated_slot_cell,
    source_tile_size,
    tile_owner,
    tile_offset,
    closure,
    damping,
):
    f32, bf16 = jnp.float32, jnp.bfloat16
    shape = jax.ShapeDtypeStruct
    channels, parts = particles.shape
    rows = closure.shape[0]
    migr = migrant_index.shape[1]
    slots = migrated_slot_cell.shape[0]
    tiles = source_tile_size.shape[1]
    devices = lax.axis_size("gx") * lax.axis_size("gy")
    capacity = max(2, 2 * tiles // devices)
    count = devices * capacity
    width = (rows + 1) * TILE
    lanes = (width + LANES) // LANES * LANES
    cells = migrated_slot_cell.reshape(1, slots)
    owners = tile_owner.reshape(1, tiles)
    offsets = tile_offset.reshape(1, tiles)

    leaving = call(
        pick_kernel, [shape((channels, migr + LANES), bf16)] * 4,
        particles, migrant_index, migrant_count, smem=(2,),
    )
    arrived = [
        shift(block, axis, step)
        for block, (axis, step) in zip(leaving, (("gx", 1), ("gx", -1), ("gy", 1), ("gy", -1)))
    ]
    sums, live, code, slot = call(
        functools.partial(deposit_kernel, capacity),
        [shape((width, tiles), f32), shape((1, parts), f32), shape((1, slots), jnp.int32),
         shape((1, tiles), jnp.int32)],
        particles, migrant_index, migrant_count, cells, source_tile_size, owners, offsets, closure,
        smem=(2,), scratch=[pltpu.VMEM((3, tiles, LANES), jnp.int32)],
    )
    (payload,) = call(
        pack_kernel, [shape((count, lanes), bf16)],
        sums, code[:, parts:], slot, offsets, closure, *arrived,
    )
    received = lax.all_to_all(
        payload.reshape(devices, capacity, lanes), ("gx", "gy"), split_axis=0, concat_axis=0, tiled=True
    ).reshape(count, lanes)
    edge = shape((FX, 2 * width), f32)
    gas, xlow, xhigh, ylow, yhigh = call(
        place_kernel, [shape((COLS, 2 * width), f32), edge, edge, edge, edge], received
    )
    xm, xp = shift(xhigh, "gx", 1), shift(xlow, "gx", -1)
    high = jnp.concatenate([xm[FY - 1 :], yhigh, xp[FY - 1 :]], axis=0)
    low = jnp.concatenate([xm[:1], ylow, xp[:1]], axis=0)
    ym, yp = shift(high, "gy", 1), shift(low, "gy", -1)
    drag, back = call(
        drag_kernel,
        [shape((rows, FX, FY, FZ), bf16), shape((count, rows * TILE), bf16)],
        received[:, lanes - LANES :], gas, xm, xp, ym, yp,
    )
    returned = lax.all_to_all(
        back.reshape(devices, capacity, rows * TILE), ("gx", "gy"), split_axis=0, concat_axis=0, tiled=True
    ).reshape(count, rows * TILE)
    (force,) = call(
        force_kernel, [shape((rows, slots), f32)],
        returned, slot, code, live, particles[:rows], damping.reshape(rows, 1), *arrived,
        scratch=[pltpu.VMEM((rows * TILE, tiles), bf16)],
    )
    return drag, force


def solution(mesh):
    both = ("gx", "gy")
    in_specs = (
        P(None, both),
        P(both, None),
        P(both, None),
        P(both),
        P(both, None),
        P(both, None),
        P(both),
        P(),
        P(),
    )
    out_specs = (P(None, "gx", "gy", None), P(None, both))
    return jax.shard_map(
        per_device, mesh=mesh, in_specs=in_specs, out_specs=out_specs, check_vma=False
    )
```

```python
import functools

import jax
import jax.numpy as jnp
from jax import lax
from jax.experimental import pallas as pl
from jax.experimental.pallas import tpu as pltpu
from jax.sharding import PartitionSpec as P

TILE = 64
FX = 8
FY = 8
FZ = 128
COLS = FX * FY
LANES = 128
GROUP = 256
CHUNK = 2048
VMEM = 48 * 1024 * 1024

NT = (((1,), (1,)), ((), ()))
TN = (((0,), (0,)), ((), ()))


def iota(shape, dim):
    return lax.broadcasted_iota(jnp.int32, shape, dim)


def dot(a, b, dims=(((1,), (0,)), ((), ()))):
    return lax.dot_general(a, b, dims, preferred_element_type=jnp.float32)


def one_hot(mask):
    return jnp.where(mask, 1.0, 0.0).astype(jnp.bfloat16)


def fetch(sources, targets, sems):
    copies = [
        pltpu.make_async_copy(source, target, sems.at[i])
        for i, (source, target) in enumerate(zip(sources, targets))
    ]
    for copy in copies:
        copy.start()
    return copies


def pick_kernel(part_hbm, index_hbm, count_hbm, *refs):
    out_refs, (part_ref, index_ref, count_ref, sems) = refs[:4], refs[4:]
    channels, parts = part_ref.shape
    migr = index_ref.shape[1]
    groups = parts // GROUP
    piece = parts // 4
    sources, targets = [index_hbm, count_hbm], [index_ref, count_ref]
    for k in range(4):
        sources.append(part_hbm.at[:, k * piece : (k + 1) * piece])
        targets.append(part_ref.at[:, k * piece : (k + 1) * piece])
    copies = fetch(sources, targets, sems)
    for copy in copies[:2]:
        copy.wait()
    lows = [one_hot(iota((GROUP, migr), 0) == index_ref[r : r + 1, :] % GROUP) for r in range(4)]
    low = jnp.concatenate(lows, axis=1)
    lane = iota((1, migr), 1)
    highs = [
        jnp.where(lane < count_ref[0, r], index_ref[r : r + 1, :] // GROUP, groups) for r in range(4)
    ]
    high = jnp.concatenate(highs, axis=1)
    for copy in copies[2:]:
        copy.wait()
    table = jnp.concatenate(
        [part_ref[:, g * GROUP : (g + 1) * GROUP].astype(jnp.bfloat16) for g in range(groups)], axis=0
    )
    rows = dot(table, low)
    picked = jnp.zeros((channels, 4 * migr), jnp.float32)
    for g in range(groups):
        picked = jnp.where(high == g, rows[g * channels : (g + 1) * channels], picked)
    for r in range(4):
        count = count_ref[0, r]
        out_refs[r][:, :migr] = picked[:, r * migr : (r + 1) * migr].astype(jnp.bfloat16)
        digits = jnp.where(iota((channels, LANES), 0) == 0, count // GROUP, count % GROUP)
        out_refs[r][:, migr:] = digits.astype(jnp.float32).astype(jnp.bfloat16)


def mix(closure_ref, state):
    state = state.astype(jnp.float32)
    mixed = closure_ref[:, 0:1] * state[0:1]
    for f in range(1, state.shape[0]):
        mixed = mixed + closure_ref[:, f : f + 1] * state[f : f + 1]
    return mixed, state[0:1]


def equal(rows, row):
    numbers = iota((rows, row.shape[1]), 0).astype(jnp.float32).astype(jnp.bfloat16)
    return numbers == row.astype(jnp.float32).astype(jnp.bfloat16)


def ones(mask):
    return jnp.where(mask, jnp.bfloat16(1), jnp.bfloat16(0))


def spread(mixed, first, place):
    hit = equal(TILE, place)
    values = jnp.concatenate([mixed, first], axis=0).astype(jnp.bfloat16)
    return jnp.concatenate(
        [jnp.where(hit, values[r : r + 1], jnp.bfloat16(0)) for r in range(values.shape[0])], axis=0
    )


def deposit_kernel(
    capacity, part_ref, index_ref, count_ref, cell_ref, size_hbm, owner_hbm, offset_hbm, closure_hbm,
    sum_ref, live_ref, code_ref, slot_ref, size_ref, owner_ref, offset_ref, closure_ref, columns_ref, sems,
):
    channels, parts = part_ref.shape
    migr = index_ref.shape[1]
    slots = cell_ref.shape[1]
    tiles = size_ref.shape[1]
    groups = parts // GROUP
    copies = fetch(
        (size_hbm, owner_hbm, offset_hbm, closure_hbm), (size_ref, owner_ref, offset_ref, closure_ref), sems
    )

    highs, lows = [], []
    for row in range(4):
        index = index_ref[row : row + 1, :]
        valid = iota((1, migr), 1) < count_ref[0, row]
        highs.append(jnp.where(valid, index // GROUP, groups))
        lows.append(index % GROUP)
    high, low = jnp.concatenate(highs, axis=1), jnp.concatenate(lows, axis=1)
    hits = dot(ones(equal(groups, high)), ones(equal(GROUP, low)), NT)
    for g in range(groups):
        live_ref[:, g * GROUP : (g + 1) * GROUP] = 1.0 - hits[g : g + 1]

    for copy in copies:
        copy.wait()

    square = (tiles, tiles)
    below, across = iota(square, 0), iota(square, 1)

    def column(row):
        return jnp.sum(jnp.where(below == across, row, 0), axis=1, keepdims=True)

    sizes = size_ref[...]
    owners = owner_ref[...]
    start = jnp.sum(jnp.where(across < below, sizes, 0), axis=1, keepdims=True)
    height = column(offset_ref[...] % FZ)
    code = iota((tiles, 1), 0) * TILE + (height - start) % TILE
    code_step = code - jnp.concatenate([jnp.zeros((1, 1), jnp.int32), code[: tiles - 1]], axis=0)
    earlier = (column(owners) == owners) & (below < across)
    rank = jnp.sum(jnp.where(earlier, 1, 0), axis=0, keepdims=True)
    slot_ref[...] = owners * capacity + rank
    columns_ref[0] = jnp.broadcast_to(start, (tiles, LANES))
    columns_ref[1] = jnp.broadcast_to(code_step, (tiles, LANES))

    def find(cell):
        width = cell.shape[1]
        starts = jnp.concatenate([columns_ref[0]] * (width // LANES), axis=1)
        steps = jnp.concatenate([columns_ref[1]] * (width // LANES), axis=1)
        found = jnp.sum(jnp.where(cell >= starts, steps, 0), axis=0, keepdims=True)
        return found // TILE, (found + cell) % TILE

    for begin in range(parts, slots, CHUNK):
        tile, place = find(cell_ref[:, begin : begin + CHUNK])
        code_ref[:, begin : begin + CHUNK] = tile * TILE + place
    for begin in range(0, parts, CHUNK):
        tile, place = find(cell_ref[:, begin : begin + CHUNK])
        code_ref[:, begin : begin + CHUNK] = tile * TILE + place
        state = part_ref[:, begin : begin + CHUNK] * live_ref[:, begin : begin + CHUNK]
        mixed, first = mix(closure_ref, state.astype(jnp.bfloat16))
        added = dot(spread(mixed, first, place), ones(equal(tiles, tile)), NT)
        if begin == 0:
            sum_ref[...] = added
        else:
            sum_ref[...] += added


def pack_kernel(sum_ref, code_ref, slot_ref, offset_ref, closure_ref, *refs):
    state_refs, out_ref = refs[:4], refs[4]
    tiles = slot_ref.shape[1]
    migr = code_ref.shape[1] // 4
    code = code_ref[...]
    state = jnp.concatenate([ref[:, :migr] for ref in state_refs], axis=1)
    mixed, first = mix(closure_ref, state)
    total = sum_ref[...] + dot(spread(mixed, first, code % TILE), ones(equal(tiles, code // TILE)), NT)
    offset = offset_ref[...]
    spare = out_ref.shape[1] - total.shape[0]
    rows = iota((spare, tiles), 0)
    marks = jnp.where(rows == 0, offset // FZ, jnp.where(rows == 1, offset % FZ, 0))
    table = jnp.concatenate(
        [total.astype(jnp.bfloat16), marks.astype(jnp.float32).astype(jnp.bfloat16)], axis=0
    )
    match = one_hot(iota((out_ref.shape[0], tiles), 0) == slot_ref[...])
    out_ref[...] = dot(match, table, NT).astype(jnp.bfloat16)


def place_kernel(tile_ref, gas_ref, xlow_ref, xhigh_ref):
    count, lanes = tile_ref.shape
    width = gas_ref.shape[1] // 2
    marks = tile_ref[:, lanes - LANES :].astype(jnp.float32)
    column = marks[:, width % LANES : width % LANES + 1]
    height = marks[:, width % LANES + 1 : width % LANES + 2]
    lane = iota((1, LANES), 1)
    hot = one_hot(column == lane.astype(jnp.float32))
    place = (iota((1, width), 1) % TILE).astype(jnp.float32)
    values = tile_ref[:, :width].astype(jnp.float32)
    for half, mask in enumerate((place >= height, place < height)):
        total = dot(hot, jnp.where(mask, values, 0.0).astype(jnp.bfloat16), TN)
        where = slice(half * width, (half + 1) * width)
        gas_ref[:, where] = total[:COLS]
        xlow_ref[:, where] = total[:FY]
        xhigh_ref[:, where] = total[COLS - FY : COLS]


def along_kernel(gas_ref, xm_ref, xp_ref, out_ref, ylow_ref, yhigh_ref):
    blocks = [xm_ref[...]] + [gas_ref[x * FY : (x + 1) * FY, :] for x in range(FX)] + [xp_ref[...]]
    along = [blocks[x] + 2.0 * blocks[x + 1] + blocks[x + 2] for x in range(FX)]
    for x in range(FX):
        out_ref[x * FY : (x + 1) * FY, :] = along[x]
    ylow_ref[...] = jnp.concatenate([along[x][:1] for x in range(FX)], axis=0)
    yhigh_ref[...] = jnp.concatenate([along[x][FY - 1 :] for x in range(FX)], axis=0)


def drag_kernel(mark_ref, along_ref, ym_ref, yp_ref, drag_ref, back_ref):
    rows = drag_ref.shape[0]
    width = along_ref.shape[1] // 2
    lanes = rows * TILE
    before, after = ym_ref[...], yp_ref[...]
    smooth = []
    for x in range(FX):
        block = along_ref[x * FY : (x + 1) * FY, :]
        padded = jnp.concatenate([before[x : x + 1], block, after[x : x + 1]], axis=0)
        smooth.append((padded[0:FY] + 2.0 * block + padded[2 : FY + 2]) / 16.0)
    smooth = jnp.concatenate(smooth, axis=0)
    halves = []
    for half in range(2):
        base = half * width
        density = smooth[:, base + lanes : base + lanes + TILE]
        below = 1.0 + density * density
        below = jnp.concatenate([below] * rows, axis=1)
        halves.append(smooth[:, base : base + lanes] / below)
    for r in range(rows):
        where = slice(r * TILE, (r + 1) * TILE)
        both = jnp.concatenate([halves[0][:, where], halves[1][:, where]], axis=1)
        drag_ref[r] = both.reshape(FX, FY, FZ).astype(jnp.bfloat16)
    mark = width % LANES
    marks = mark_ref[...].astype(jnp.float32)
    column, height = marks[:, mark : mark + 1], marks[:, mark + 1 : mark + 2]
    hot = one_hot(column == iota((1, COLS), 1).astype(jnp.float32))
    place = (iota((1, lanes), 1) % TILE).astype(jnp.float32)
    low = dot(hot, halves[0].astype(jnp.bfloat16))
    high = dot(hot, halves[1].astype(jnp.bfloat16))
    back_ref[...] = jnp.where(place >= height, low, high).astype(jnp.bfloat16)


def force_kernel(back_ref, slot_ref, code_ref, live_ref, part_ref, damping_ref, *refs):
    state_refs, out_ref, table_ref = refs[:4], refs[4], refs[5]
    rows, slots = out_ref.shape
    parts = part_ref.shape[1]
    tiles = slot_ref.shape[1]
    migr = (slots - parts) // 4
    match = one_hot(iota((back_ref.shape[0], tiles), 0) == slot_ref[...])
    table_ref[...] = dot(back_ref[...], match, TN).astype(jnp.bfloat16)
    damping = damping_ref[...]

    def look(code):
        values = dot(table_ref[...], ones(equal(tiles, code // TILE))).astype(jnp.bfloat16)
        hit = equal(TILE, code % TILE)
        found = []
        for r in range(rows):
            picked = jnp.where(hit, values[r * TILE : (r + 1) * TILE], jnp.bfloat16(0))
            while picked.shape[0] > 16:
                half = picked.shape[0] // 2
                picked = picked[:half] + picked[half:]
            found.append(jnp.sum(picked.astype(jnp.float32), axis=0, keepdims=True))
        return jnp.concatenate(found, axis=0)

    for begin in range(0, parts, CHUNK):
        where = slice(begin, begin + CHUNK)
        out_ref[:, where] = live_ref[:, where] * (look(code_ref[:, where]) - damping * part_ref[:, where])
    drag = look(code_ref[:, parts:])
    for row in range(4):
        begin = parts + row * migr
        arrived = state_refs[row][:, :].astype(jnp.float32)
        count = arrived[0:1, migr : migr + 1] * GROUP + arrived[1:2, migr : migr + 1]
        live = iota((1, migr), 1).astype(jnp.float32) < count
        force = drag[:, row * migr : (row + 1) * migr] - damping * arrived[:rows, :migr]
        out_ref[:, begin : begin + migr] = jnp.where(live, force, 0.0)


def call(kernel, shapes, *operands, smem=(), hbm=(), scratch=()):
    def space(i):
        return pltpu.SMEM if i in smem else pltpu.HBM if i in hbm else pltpu.VMEM

    return pl.pallas_call(
        kernel,
        out_shape=shapes,
        in_specs=[pl.BlockSpec(memory_space=space(i)) for i in range(len(operands))],
        out_specs=[pl.BlockSpec(memory_space=pltpu.VMEM) for _ in shapes],
        scratch_shapes=scratch,
        compiler_params=pltpu.CompilerParams(vmem_limit_bytes=VMEM),
    )(*operands)


def shift(block, axis, step):
    size = lax.axis_size(axis)
    return lax.ppermute(block, axis, [(i, (i + step) % size) for i in range(size)])


def per_device(
    particles,
    migrant_index,
    migrant_count,
    migrated_slot_cell,
    source_tile_size,
    tile_owner,
    tile_offset,
    closure,
    damping,
):
    f32, bf16 = jnp.float32, jnp.bfloat16
    shape = jax.ShapeDtypeStruct
    channels, parts = particles.shape
    rows = closure.shape[0]
    migr = migrant_index.shape[1]
    slots = migrated_slot_cell.shape[0]
    tiles = source_tile_size.shape[1]
    devices = lax.axis_size("gx") * lax.axis_size("gy")
    capacity = max(2, 2 * tiles // devices)
    count = devices * capacity
    width = (rows + 1) * TILE
    lanes = (width + LANES) // LANES * LANES
    cells = migrated_slot_cell.reshape(1, slots)
    owners = tile_owner.reshape(1, tiles)
    offsets = tile_offset.reshape(1, tiles)

    leaving = call(
        pick_kernel, [shape((channels, migr + LANES), bf16)] * 4,
        particles, migrant_index, migrant_count, hbm=(0, 1, 2),
        scratch=[pltpu.VMEM(particles.shape, f32), pltpu.VMEM(migrant_index.shape, jnp.int32),
                 pltpu.SMEM(migrant_count.shape, jnp.int32), pltpu.SemaphoreType.DMA((6,))],
    )
    arrived = [
        shift(block, axis, step)
        for block, (axis, step) in zip(leaving, (("gx", 1), ("gx", -1), ("gy", 1), ("gy", -1)))
    ]
    sums, live, code, slot = call(
        functools.partial(deposit_kernel, capacity),
        [shape((width, tiles), f32), shape((1, parts), f32), shape((1, slots), jnp.int32),
         shape((1, tiles), jnp.int32)],
        particles, migrant_index, migrant_count, cells, source_tile_size, owners, offsets, closure,
        smem=(2,), hbm=(4, 5, 6, 7),
        scratch=[pltpu.VMEM((1, tiles), jnp.int32)] * 3
        + [pltpu.VMEM(closure.shape, f32), pltpu.VMEM((2, tiles, LANES), jnp.int32),
           pltpu.SemaphoreType.DMA((4,))],
    )
    (payload,) = call(
        pack_kernel, [shape((count, lanes), bf16)],
        sums, code[:, parts:], slot, offsets, closure, *arrived,
    )
    received = lax.all_to_all(
        payload.reshape(devices, capacity, lanes), ("gx", "gy"), split_axis=0, concat_axis=0, tiled=True
    ).reshape(count, lanes)
    grid, edge = shape((COLS, 2 * width), f32), shape((FX, 2 * width), f32)
    gas, xlow, xhigh = call(place_kernel, [grid, edge, edge], received)
    xm, xp = shift(xhigh, "gx", 1), shift(xlow, "gx", -1)
    along, ylow, yhigh = call(along_kernel, [grid, edge, edge], gas, xm, xp)
    ym, yp = shift(yhigh, "gy", 1), shift(ylow, "gy", -1)
    drag, back = call(
        drag_kernel,
        [shape((rows, FX, FY, FZ), bf16), shape((count, rows * TILE), bf16)],
        received[:, lanes - LANES :], along, ym, yp,
    )
    returned = lax.all_to_all(
        back.reshape(devices, capacity, rows * TILE), ("gx", "gy"), split_axis=0, concat_axis=0, tiled=True
    ).reshape(count, rows * TILE)
    (force,) = call(
        force_kernel, [shape((rows, slots), f32)],
        returned, slot, code, live, particles[:rows], damping.reshape(rows, 1), *arrived,
        scratch=[pltpu.VMEM((rows * TILE, tiles), bf16)],
    )
    return drag, force


def solution(mesh):
    both = ("gx", "gy")
    in_specs = (
        P(None, both),
        P(both, None),
        P(both, None),
        P(both),
        P(both, None),
        P(both, None),
        P(both),
        P(),
        P(),
    )
    out_specs = (P(None, "gx", "gy", None), P(None, both))
    return jax.shard_map(
        per_device, mesh=mesh, in_specs=in_specs, out_specs=out_specs, check_vma=False
    )
```

```python
import functools

import jax
import jax.numpy as jnp
from jax import lax
from jax.experimental import pallas as pl
from jax.experimental.pallas import tpu as pltpu
from jax.sharding import PartitionSpec as P

TILE = 64
FX = 8
FY = 8
FZ = 128
COLS = FX * FY
LANES = 128
GROUP = 256
CHUNK = 2048
VMEM = 48 * 1024 * 1024
LARGE = 63 * 1024 * 1024

NT = (((1,), (1,)), ((), ()))
TN = (((0,), (0,)), ((), ()))


def iota(shape, dim):
    return lax.broadcasted_iota(jnp.int32, shape, dim)


def dot(a, b, dims=(((1,), (0,)), ((), ()))):
    return lax.dot_general(a, b, dims, preferred_element_type=jnp.float32)


def one_hot(mask):
    return jnp.where(mask, 1.0, 0.0).astype(jnp.bfloat16)


def equal(rows, row):
    numbers = iota((rows, row.shape[1]), 0).astype(jnp.float32).astype(jnp.bfloat16)
    return numbers == row.astype(jnp.float32).astype(jnp.bfloat16)


def ones(mask):
    return jnp.where(mask, jnp.bfloat16(1), jnp.bfloat16(0))


def fetch(sources, targets, sems):
    copies = [
        pltpu.make_async_copy(source, target, sems.at[i])
        for i, (source, target) in enumerate(zip(sources, targets))
    ]
    for copy in copies:
        copy.start()
    return copies


def leaving_rows(index_ref, count_ref, groups):
    migr = index_ref.shape[1]
    lane = iota((1, migr), 1)
    index = jnp.concatenate([index_ref[r : r + 1, :] for r in range(4)], axis=1)
    leaves = jnp.concatenate([lane < count_ref[0, r] for r in range(4)], axis=1)
    return jnp.where(leaves, index // GROUP, groups), index % GROUP


def pick_kernel(
    part_hbm, index_hbm, count_hbm, size_hbm, owner_hbm, offset_hbm, closure_hbm, damping_hbm, *refs
):
    out_refs, small_ref, refs = refs[:4], refs[4], refs[5:]
    part_ref, index_ref, count_ref, size_ref, owner_ref, offset_ref, closure_ref, damping_ref, sems = refs
    channels, parts = part_ref.shape
    migr = index_ref.shape[1]
    groups = parts // GROUP
    piece = parts // 4
    sources, targets = [index_hbm, count_hbm], [index_ref, count_ref]
    for k in range(4):
        sources.append(part_hbm.at[:, k * piece : (k + 1) * piece])
        targets.append(part_ref.at[:, k * piece : (k + 1) * piece])
    sources += [size_hbm, owner_hbm, offset_hbm, closure_hbm, damping_hbm]
    targets += [size_ref, owner_ref, offset_ref, closure_ref, damping_ref]
    copies = fetch(sources, targets, sems)
    for copy in copies[:2]:
        copy.wait()
    high, low = leaving_rows(index_ref, count_ref, groups)
    low = ones(equal(GROUP, low))
    for copy in copies[2:]:
        copy.wait()
    for row, ref in enumerate((size_ref, owner_ref, offset_ref)):
        small_ref[row : row + 1, :] = ref[...].astype(jnp.float32)
    rows, width = closure_ref.shape
    small_ref[rows : 2 * rows, :width] = closure_ref[...]
    diagonal = iota((rows, rows), 0) == iota((rows, rows), 1)
    damping = jnp.sum(jnp.where(diagonal, damping_ref[...], 0.0), axis=1, keepdims=True)
    small_ref[rows : 2 * rows, width : width + 1] = damping
    table = jnp.concatenate(
        [part_ref[:, g * GROUP : (g + 1) * GROUP].astype(jnp.bfloat16) for g in range(groups)], axis=0
    )
    rows = dot(table, low)
    picked = jnp.zeros((channels, 4 * migr), jnp.float32)
    for g in range(groups):
        picked = jnp.where(high == g, rows[g * channels : (g + 1) * channels], picked)
    for r in range(4):
        count = count_ref[0, r]
        out_refs[r][:, :migr] = picked[:, r * migr : (r + 1) * migr].astype(jnp.bfloat16)
        digits = jnp.where(iota((channels, LANES), 0) == 0, count // GROUP, count % GROUP)
        out_refs[r][:, migr:] = digits.astype(jnp.float32).astype(jnp.bfloat16)


def mix(small_ref, state):
    state = state.astype(jnp.float32)
    closure = small_ref[small_ref.shape[0] // 2 :, :]
    mixed = closure[:, 0:1] * state[0:1]
    for f in range(1, state.shape[0]):
        mixed = mixed + closure[:, f : f + 1] * state[f : f + 1]
    return mixed, state[0:1]


def spread(mixed, first, place):
    hit = equal(TILE, place)
    values = jnp.concatenate([mixed, first], axis=0).astype(jnp.bfloat16)
    return jnp.concatenate(
        [jnp.where(hit, values[r : r + 1], jnp.bfloat16(0)) for r in range(values.shape[0])], axis=0
    )


def deposit_kernel(
    capacity, part_ref, index_ref, count_ref, cell_ref, small_ref,
    sum_ref, live_ref, code_ref, slot_ref, mark_ref, columns_ref,
):
    channels, parts = part_ref.shape
    slots = cell_ref.shape[1]
    tiles = slot_ref.shape[1]
    groups = parts // GROUP

    high, low = leaving_rows(index_ref, count_ref, groups)
    hits = dot(ones(equal(groups, high)), ones(equal(GROUP, low)), NT)
    for g in range(groups):
        live_ref[:, g * GROUP : (g + 1) * GROUP] = 1.0 - hits[g : g + 1]

    square = (tiles, tiles)
    below, across = iota(square, 0), iota(square, 1)

    def column(row):
        return jnp.sum(jnp.where(below == across, row, 0), axis=1, keepdims=True)

    sizes, owners, offset = [small_ref[row : row + 1, :].astype(jnp.int32) for row in range(3)]
    start = jnp.sum(jnp.where(across < below, sizes, 0), axis=1, keepdims=True)
    height = column(offset % FZ)
    code = iota((tiles, 1), 0) * TILE + (height - start) % TILE
    code_step = code - jnp.concatenate([jnp.zeros((1, 1), jnp.int32), code[: tiles - 1]], axis=0)
    earlier = (column(owners) == owners) & (below < across)
    rank = jnp.sum(jnp.where(earlier, 1, 0), axis=0, keepdims=True)
    slot_ref[...] = owners * capacity + rank
    columns_ref[0] = jnp.broadcast_to(start, (tiles, LANES))
    columns_ref[1] = jnp.broadcast_to(code_step, (tiles, LANES))
    rows = iota(mark_ref.shape, 0)
    marks = jnp.where(rows == 0, offset // FZ, jnp.where(rows == 1, offset % FZ, 0))
    mark_ref[...] = marks.astype(jnp.float32).astype(jnp.bfloat16)

    def find(cell):
        width = cell.shape[1]
        starts = jnp.concatenate([columns_ref[0]] * (width // LANES), axis=1)
        steps = jnp.concatenate([columns_ref[1]] * (width // LANES), axis=1)
        found = jnp.sum(jnp.where(cell >= starts, steps, 0), axis=0, keepdims=True)
        return found // TILE, (found + cell) % TILE

    for begin in range(parts, slots, CHUNK):
        tile, place = find(cell_ref[:, begin : begin + CHUNK])
        code_ref[:, begin : begin + CHUNK] = tile * TILE + place
    for begin in range(0, parts, CHUNK):
        tile, place = find(cell_ref[:, begin : begin + CHUNK])
        code_ref[:, begin : begin + CHUNK] = tile * TILE + place
        state = part_ref[:, begin : begin + CHUNK] * live_ref[:, begin : begin + CHUNK]
        mixed, first = mix(small_ref, state.astype(jnp.bfloat16))
        added = dot(spread(mixed, first, place), ones(equal(tiles, tile)), NT)
        if begin == 0:
            sum_ref[...] = added
        else:
            sum_ref[...] += added


def pack_kernel(sum_ref, code_ref, slot_ref, mark_ref, small_ref, *refs):
    state_refs, out_ref = refs[:4], refs[4]
    tiles = slot_ref.shape[1]
    migr = state_refs[0].shape[1] - LANES
    code = code_ref[:, code_ref.shape[1] - 4 * migr :]
    state = jnp.concatenate([ref[:, :migr] for ref in state_refs], axis=1)
    mixed, first = mix(small_ref, state)
    total = sum_ref[...] + dot(spread(mixed, first, code % TILE), ones(equal(tiles, code // TILE)), NT)
    table = jnp.concatenate([total.astype(jnp.bfloat16), mark_ref[...]], axis=0)
    match = one_hot(iota((out_ref.shape[0], tiles), 0) == slot_ref[...])
    out_ref[...] = dot(match, table, NT).astype(jnp.bfloat16)


def place_kernel(tile_ref, gas_ref, xlow_ref, xhigh_ref):
    count, lanes = tile_ref.shape
    width = gas_ref.shape[1] // 2
    marks = tile_ref[:, lanes - LANES :].astype(jnp.float32)
    column = marks[:, width % LANES : width % LANES + 1]
    height = marks[:, width % LANES + 1 : width % LANES + 2]
    lane = iota((1, LANES), 1)
    hot = one_hot(column == lane.astype(jnp.float32))
    place = (iota((1, width), 1) % TILE).astype(jnp.float32)
    values = tile_ref[:, :width].astype(jnp.float32)
    for half, mask in enumerate((place >= height, place < height)):
        total = dot(hot, jnp.where(mask, values, 0.0).astype(jnp.bfloat16), TN)
        where = slice(half * width, (half + 1) * width)
        gas_ref[:, where] = total[:COLS]
        rows = slice(half * FY, (half + 1) * FY)
        xlow_ref[rows, :] = total[:FY].astype(jnp.bfloat16)
        xhigh_ref[rows, :] = total[COLS - FY : COLS].astype(jnp.bfloat16)


def unfold(ref):
    edge = ref[...].astype(jnp.float32)
    half = edge.shape[0] // 2
    return jnp.concatenate([edge[:half], edge[half:]], axis=1)


def along_kernel(gas_ref, xm_ref, xp_ref, out_ref, ylow_ref, yhigh_ref):
    blocks = [unfold(xm_ref)] + [gas_ref[x * FY : (x + 1) * FY, :] for x in range(FX)] + [unfold(xp_ref)]
    along = [blocks[x] + 2.0 * blocks[x + 1] + blocks[x + 2] for x in range(FX)]
    for x in range(FX):
        out_ref[x * FY : (x + 1) * FY, :] = along[x]
    width = ylow_ref.shape[1]
    for ref, row in ((ylow_ref, 0), (yhigh_ref, FY - 1)):
        edge = jnp.concatenate([along[x][row : row + 1] for x in range(FX)], axis=0)
        edge = jnp.concatenate([edge[:, :width], edge[:, width:]], axis=0)
        ref[...] = edge.astype(jnp.bfloat16)


def drag_kernel(mark_ref, along_ref, ym_ref, yp_ref, drag_ref, back_ref):
    rows = drag_ref.shape[0]
    width = along_ref.shape[1] // 2
    lanes = rows * TILE
    before, after = unfold(ym_ref), unfold(yp_ref)
    smooth = []
    for x in range(FX):
        block = along_ref[x * FY : (x + 1) * FY, :]
        padded = jnp.concatenate([before[x : x + 1], block, after[x : x + 1]], axis=0)
        smooth.append((padded[0:FY] + 2.0 * block + padded[2 : FY + 2]) / 16.0)
    smooth = jnp.concatenate(smooth, axis=0)
    halves = []
    for half in range(2):
        base = half * width
        density = smooth[:, base + lanes : base + lanes + TILE]
        below = 1.0 + density * density
        below = jnp.concatenate([below] * rows, axis=1)
        halves.append(smooth[:, base : base + lanes] / below)
    for r in range(rows):
        where = slice(r * TILE, (r + 1) * TILE)
        both = jnp.concatenate([halves[0][:, where], halves[1][:, where]], axis=1)
        drag_ref[r] = both.reshape(FX, FY, FZ).astype(jnp.bfloat16)
    mark = width % LANES
    marks = mark_ref[...].astype(jnp.float32)
    column, height = marks[:, mark : mark + 1], marks[:, mark + 1 : mark + 2]
    hot = one_hot(column == iota((1, COLS), 1).astype(jnp.float32))
    place = (iota((1, lanes), 1) % TILE).astype(jnp.float32)
    low = dot(hot, halves[0].astype(jnp.bfloat16))
    high = dot(hot, halves[1].astype(jnp.bfloat16))
    back_ref[...] = jnp.where(place >= height, low, high).astype(jnp.bfloat16)


def force_kernel(back_ref, slot_ref, code_ref, live_ref, part_ref, small_ref, *refs):
    state_refs, out_ref, table_ref = refs[:4], refs[4], refs[5]
    rows, slots = out_ref.shape
    parts = part_ref.shape[1]
    tiles = slot_ref.shape[1]
    migr = (slots - parts) // 4
    match = one_hot(iota((back_ref.shape[0], tiles), 0) == slot_ref[...])
    table_ref[...] = dot(back_ref[...], match, TN).astype(jnp.bfloat16)
    channels = part_ref.shape[0]
    damping = small_ref[rows:, channels : channels + 1]

    def look(code):
        values = dot(table_ref[...], ones(equal(tiles, code // TILE))).astype(jnp.bfloat16)
        hit = equal(TILE, code % TILE)
        found = []
        for r in range(rows):
            picked = jnp.where(hit, values[r * TILE : (r + 1) * TILE], jnp.bfloat16(0))
            while picked.shape[0] > 16:
                half = picked.shape[0] // 2
                picked = picked[:half] + picked[half:]
            found.append(jnp.sum(picked.astype(jnp.float32), axis=0, keepdims=True))
        return jnp.concatenate(found, axis=0)

    for begin in range(0, parts, CHUNK):
        where = slice(begin, begin + CHUNK)
        out_ref[:, where] = live_ref[:, where] * (look(code_ref[:, where]) - damping * part_ref[:rows, where])
    drag = look(code_ref[:, parts:])
    for row in range(4):
        begin = parts + row * migr
        arrived = state_refs[row][:, :].astype(jnp.float32)
        count = arrived[0:1, migr : migr + 1] * GROUP + arrived[1:2, migr : migr + 1]
        live = iota((1, migr), 1).astype(jnp.float32) < count
        force = drag[:, row * migr : (row + 1) * migr] - damping * arrived[:rows, :migr]
        out_ref[:, begin : begin + migr] = jnp.where(live, force, 0.0)


def call(kernel, shapes, *operands, smem=(), hbm=(), scratch=(), vmem=VMEM):
    def space(i):
        return pltpu.SMEM if i in smem else pltpu.HBM if i in hbm else pltpu.VMEM

    return pl.pallas_call(
        kernel,
        out_shape=shapes,
        in_specs=[pl.BlockSpec(memory_space=space(i)) for i in range(len(operands))],
        out_specs=[pl.BlockSpec(memory_space=pltpu.VMEM) for _ in shapes],
        scratch_shapes=scratch,
        compiler_params=pltpu.CompilerParams(vmem_limit_bytes=vmem),
    )(*operands)


def shift(block, axis, step):
    size = lax.axis_size(axis)
    return lax.ppermute(block, axis, [(i, (i + step) % size) for i in range(size)])


def per_device(
    particles,
    migrant_index,
    migrant_count,
    migrated_slot_cell,
    source_tile_size,
    tile_owner,
    tile_offset,
    closure,
    damping,
):
    f32, bf16, i32 = jnp.float32, jnp.bfloat16, jnp.int32
    shape = jax.ShapeDtypeStruct
    channels, parts = particles.shape
    rows = closure.shape[0]
    migr = migrant_index.shape[1]
    slots = migrated_slot_cell.shape[0]
    tiles = source_tile_size.shape[1]
    devices = lax.axis_size("gx") * lax.axis_size("gy")
    capacity = max(2, 2 * tiles // devices)
    count = devices * capacity
    width = (rows + 1) * TILE
    lanes = (width + LANES) // LANES * LANES
    *leaving, small = call(
        pick_kernel,
        [shape((channels, migr + LANES), bf16)] * 4 + [shape((2 * rows, tiles), f32)],
        particles, migrant_index, migrant_count, source_tile_size, tile_owner.reshape(1, tiles),
        tile_offset.reshape(1, tiles), closure, damping.reshape(1, rows),
        hbm=range(8), vmem=LARGE,
        scratch=[pltpu.VMEM(particles.shape, f32), pltpu.VMEM(migrant_index.shape, i32),
                 pltpu.SMEM(migrant_count.shape, i32)]
        + [pltpu.VMEM((1, tiles), i32)] * 3
        + [pltpu.VMEM(closure.shape, f32), pltpu.VMEM((1, rows), f32), pltpu.SemaphoreType.DMA((11,))],
    )
    arrived = [
        shift(block, axis, step)
        for block, (axis, step) in zip(leaving, (("gx", 1), ("gx", -1), ("gy", 1), ("gy", -1)))
    ]
    sums, live, code, slot, marks = call(
        functools.partial(deposit_kernel, capacity),
        [shape((width, tiles), f32), shape((1, parts), f32), shape((1, slots), i32), shape((1, tiles), i32),
         shape((lanes - width, tiles), bf16)],
        particles, migrant_index, migrant_count, migrated_slot_cell.reshape(1, slots), small,
        smem=(2,), scratch=[pltpu.VMEM((2, tiles, LANES), i32)],
    )
    (payload,) = call(
        pack_kernel, [shape((count, lanes), bf16)], sums, code, slot, marks, small, *arrived
    )
    received = lax.all_to_all(
        payload.reshape(devices, capacity, lanes), ("gx", "gy"), split_axis=0, concat_axis=0, tiled=True
    ).reshape(count, lanes)
    grid, edge = shape((COLS, 2 * width), f32), shape((2 * FX, width), bf16)
    gas, xlow, xhigh = call(place_kernel, [grid, edge, edge], received)
    xm, xp = shift(xhigh, "gx", 1), shift(xlow, "gx", -1)
    along, ylow, yhigh = call(along_kernel, [grid, edge, edge], gas, xm, xp)
    ym, yp = shift(yhigh, "gy", 1), shift(ylow, "gy", -1)
    drag, back = call(
        drag_kernel,
        [shape((rows, FX, FY, FZ), bf16), shape((count, rows * TILE), bf16)],
        received[:, lanes - LANES :], along, ym, yp,
    )
    returned = lax.all_to_all(
        back.reshape(devices, capacity, rows * TILE), ("gx", "gy"), split_axis=0, concat_axis=0, tiled=True
    ).reshape(count, rows * TILE)
    (force,) = call(
        force_kernel, [shape((rows, slots), f32)],
        returned, slot, code, live, particles, small, *arrived,
        scratch=[pltpu.VMEM((rows * TILE, tiles), bf16)],
    )
    return drag, force


def solution(mesh):
    both = ("gx", "gy")
    in_specs = (
        P(None, both),
        P(both, None),
        P(both, None),
        P(both),
        P(both, None),
        P(both, None),
        P(both),
        P(),
        P(),
    )
    out_specs = (P(None, "gx", "gy", None), P(None, both))
    return jax.shard_map(
        per_device, mesh=mesh, in_specs=in_specs, out_specs=out_specs, check_vma=False
    )
```

```python
import functools

import jax
import jax.numpy as jnp
from jax import lax
from jax.experimental import pallas as pl
from jax.experimental.pallas import tpu as pltpu
from jax.sharding import PartitionSpec as P

TILE = 64
FX = 8
FY = 8
FZ = 128
COLS = FX * FY
LANES = 128
GROUP = 256
CHUNK = 2048
VMEM = 48 * 1024 * 1024
LARGE = 63 * 1024 * 1024

NT = (((1,), (1,)), ((), ()))
TN = (((0,), (0,)), ((), ()))


def iota(shape, dim):
    return lax.broadcasted_iota(jnp.int32, shape, dim)


def dot(a, b, dims=(((1,), (0,)), ((), ()))):
    return lax.dot_general(a, b, dims, preferred_element_type=jnp.float32)


def one_hot(mask):
    return jnp.where(mask, 1.0, 0.0).astype(jnp.bfloat16)


def equal(rows, row):
    numbers = iota((rows, row.shape[1]), 0).astype(jnp.float32).astype(jnp.bfloat16)
    return numbers == row.astype(jnp.float32).astype(jnp.bfloat16)


def ones(mask):
    return jnp.where(mask, jnp.bfloat16(1), jnp.bfloat16(0))


def fetch(sources, targets, sems):
    copies = [
        pltpu.make_async_copy(source, target, sems.at[i])
        for i, (source, target) in enumerate(zip(sources, targets))
    ]
    for copy in copies:
        copy.start()
    return copies


def pieces(hbm, vmem):
    width = hbm.shape[1] // 4
    cuts = [slice(k * width, (k + 1) * width) for k in range(4)]
    return [hbm.at[:, cut] for cut in cuts], [vmem.at[:, cut] for cut in cuts]


def leaving_row(index_ref, count_ref, parts):
    migr = index_ref.shape[1]
    lane = iota((1, migr), 1)
    rows = [jnp.where(lane < count_ref[0, r], index_ref[r : r + 1, :], parts) for r in range(4)]
    return jnp.concatenate(rows, axis=1)


def small_rows(rows, groups, slots):
    live = 2 * rows
    cells = live + groups
    return rows, live, cells, cells + slots // GROUP


def pick_kernel(
    part_hbm, index_hbm, count_hbm, size_hbm, owner_hbm, offset_hbm, closure_hbm, damping_hbm, cell_hbm, *refs
):
    out_refs, small_ref, refs = refs[:4], refs[4], refs[5:]
    part_ref, index_ref, count_ref, size_ref, owner_ref, offset_ref = refs[:6]
    closure_ref, damping_ref, cell_ref, sems = refs[6:]
    channels, parts = part_ref.shape
    migr = index_ref.shape[1]
    slots = cell_ref.shape[1]
    groups = parts // GROUP
    rows, width = closure_ref.shape
    closure_row, live_row, cell_row, _ = small_rows(rows, groups, slots)
    sources, targets = pieces(part_hbm, part_ref)
    copies = fetch(
        [index_hbm, count_hbm, size_hbm, owner_hbm, offset_hbm, closure_hbm, damping_hbm, cell_hbm] + sources,
        [index_ref, count_ref, size_ref, owner_ref, offset_ref, closure_ref, damping_ref, cell_ref] + targets,
        sems,
    )
    for copy in copies[:8]:
        copy.wait()
    for row, ref in enumerate((size_ref, owner_ref, offset_ref)):
        small_ref[row : row + 1, :] = ref[...].astype(jnp.float32)
    small_ref[closure_row:live_row, :width] = closure_ref[...]
    diagonal = iota((rows, rows), 0) == iota((rows, rows), 1)
    damping = jnp.sum(jnp.where(diagonal, damping_ref[...], 0.0), axis=1, keepdims=True)
    small_ref[closure_row:live_row, width : width + 1] = damping
    for k in range(slots // GROUP):
        row = cell_ref[:, k * GROUP : (k + 1) * GROUP]
        small_ref[cell_row + k : cell_row + k + 1, :] = row.astype(jnp.float32)
    leave = leaving_row(index_ref, count_ref, parts)
    high = leave // GROUP
    low = ones(equal(GROUP, leave % GROUP))
    small_ref[live_row:cell_row, :] = 1.0 - dot(ones(equal(groups, high)), low, NT)
    for copy in copies[8:]:
        copy.wait()
    table = jnp.concatenate(
        [part_ref[:, g * GROUP : (g + 1) * GROUP].astype(jnp.bfloat16) for g in range(groups)], axis=0
    )
    rows = dot(table, low)
    picked = jnp.zeros((channels, 4 * migr), jnp.float32)
    for g in range(groups):
        picked = jnp.where(high == g, rows[g * channels : (g + 1) * channels], picked)
    live = jnp.where(leave < parts, 1.0, 0.0)
    for r in range(4):
        out_refs[r][:, :migr] = picked[:, r * migr : (r + 1) * migr].astype(jnp.bfloat16)
        flags = [live[:, k : k + LANES] for k in range(r * migr, (r + 1) * migr, LANES)]
        flags.append(jnp.zeros((channels - len(flags), LANES), jnp.float32))
        out_refs[r][:, migr:] = jnp.concatenate(flags, axis=0).astype(jnp.bfloat16)


def mix(closure, state):
    state = state.astype(jnp.float32)
    mixed = closure[:, 0:1] * state[0:1]
    for f in range(1, state.shape[0]):
        mixed = mixed + closure[:, f : f + 1] * state[f : f + 1]
    return mixed, state[0:1]


def side_by_side(ref, first, begin, width):
    first = first + begin // GROUP
    rows = [ref[r : r + 1, :] for r in range(first, first + width // GROUP)]
    return jnp.concatenate(rows, axis=1)


def spread(mixed, first, place):
    hit = equal(TILE, place)
    values = jnp.concatenate([mixed, first], axis=0).astype(jnp.bfloat16)
    return jnp.concatenate(
        [jnp.where(hit, values[r : r + 1], jnp.bfloat16(0)) for r in range(values.shape[0])], axis=0
    )


def deposit_kernel(
    capacity, rows, part_ref, small_ref, sum_ref, code_ref, slot_ref, mark_ref, columns_ref,
):
    channels, parts = part_ref.shape
    slots = code_ref.shape[1]
    tiles = slot_ref.shape[1]
    closure_row, live_row, cell_row, _ = small_rows(rows, parts // GROUP, slots)
    closure = small_ref[closure_row:live_row, :channels]

    square = (tiles, tiles)
    below, across = iota(square, 0), iota(square, 1)

    def column(row):
        return jnp.sum(jnp.where(below == across, row, 0), axis=1, keepdims=True)

    sizes, owners, offset = [small_ref[r : r + 1, :].astype(jnp.int32) for r in range(3)]
    start = jnp.sum(jnp.where(across < below, sizes, 0), axis=1, keepdims=True)
    height = column(offset % FZ)
    code = iota((tiles, 1), 0) * TILE + (height - start) % TILE
    code_step = code - jnp.concatenate([jnp.zeros((1, 1), jnp.int32), code[: tiles - 1]], axis=0)
    earlier = (column(owners) == owners) & (below < across)
    rank = jnp.sum(jnp.where(earlier, 1, 0), axis=0, keepdims=True)
    slot_ref[...] = owners * capacity + rank
    columns_ref[0] = jnp.broadcast_to(start, (tiles, LANES))
    columns_ref[1] = jnp.broadcast_to(code_step, (tiles, LANES))
    rows = iota(mark_ref.shape, 0)
    marks = jnp.where(rows == 0, offset // FZ, jnp.where(rows == 1, offset % FZ, 0))
    mark_ref[...] = marks.astype(jnp.float32).astype(jnp.bfloat16)

    def find(begin):
        cell = side_by_side(small_ref, cell_row, begin, CHUNK).astype(jnp.int32)
        starts = jnp.concatenate([columns_ref[0]] * (CHUNK // LANES), axis=1)
        steps = jnp.concatenate([columns_ref[1]] * (CHUNK // LANES), axis=1)
        found = jnp.sum(jnp.where(cell >= starts, steps, 0), axis=0, keepdims=True)
        return found // TILE, (found + cell) % TILE

    for begin in range(parts, slots, CHUNK):
        tile, place = find(begin)
        code_ref[:, begin : begin + CHUNK] = tile * TILE + place
    for begin in range(0, parts, CHUNK):
        tile, place = find(begin)
        code_ref[:, begin : begin + CHUNK] = tile * TILE + place
        live = side_by_side(small_ref, live_row, begin, CHUNK)
        state = part_ref[:, begin : begin + CHUNK] * live
        mixed, first = mix(closure, state.astype(jnp.bfloat16))
        added = dot(spread(mixed, first, place), ones(equal(tiles, tile)), NT)
        if begin == 0:
            sum_ref[...] = added
        else:
            sum_ref[...] += added


def pack_kernel(rows, sum_ref, code_ref, slot_ref, mark_ref, small_ref, *refs):
    state_refs, out_ref = refs[:4], refs[4]
    channels, tiles = state_refs[0].shape[0], slot_ref.shape[1]
    closure = small_ref[rows : 2 * rows, :channels]
    migr = state_refs[0].shape[1] - LANES
    code = code_ref[:, code_ref.shape[1] - 4 * migr :]
    state = jnp.concatenate([ref[:, :migr] for ref in state_refs], axis=1)
    mixed, first = mix(closure, state)
    total = sum_ref[...] + dot(spread(mixed, first, code % TILE), ones(equal(tiles, code // TILE)), NT)
    table = jnp.concatenate([total.astype(jnp.bfloat16), mark_ref[...]], axis=0)
    match = one_hot(iota((out_ref.shape[0], tiles), 0) == slot_ref[...])
    out_ref[...] = dot(match, table, NT).astype(jnp.bfloat16)


def is_even(axis):
    return lax.axis_index(axis) % 2 == 0


def exchange(block_a, block_b, axis):
    size = lax.axis_size(axis)
    blocks = []
    for odd, block in enumerate((block_a, block_b)):
        pairs = [(i, (i + 1) % size if i % 2 == odd else (i - 1) % size) for i in range(size)]
        blocks.append(lax.ppermute(block, axis, pairs))
    return blocks


def place_kernel(tile_ref, gas_ref, xa_ref, xb_ref):
    even = is_even("gx")
    count, lanes = tile_ref.shape
    width = gas_ref.shape[1] // 2
    marks = tile_ref[:, lanes - LANES :].astype(jnp.float32)
    column = marks[:, width % LANES : width % LANES + 1]
    height = marks[:, width % LANES + 1 : width % LANES + 2]
    lane = iota((1, LANES), 1)
    hot = one_hot(column == lane.astype(jnp.float32))
    place = (iota((1, width), 1) % TILE).astype(jnp.float32)
    values = tile_ref[:, :width].astype(jnp.float32)
    for half, mask in enumerate((place >= height, place < height)):
        total = dot(hot, jnp.where(mask, values, 0.0).astype(jnp.bfloat16), TN)
        where = slice(half * width, (half + 1) * width)
        gas_ref[:, where] = total[:COLS]
        rows = slice(half * FY, (half + 1) * FY)
        low, high = total[:FY], total[COLS - FY : COLS]
        xa_ref[rows, :] = jnp.where(even, high, low).astype(jnp.bfloat16)
        xb_ref[rows, :] = jnp.where(even, low, high).astype(jnp.bfloat16)


def unfold(ref):
    edge = ref[...].astype(jnp.float32)
    half = edge.shape[0] // 2
    return jnp.concatenate([edge[:half], edge[half:]], axis=1)


def along_kernel(gas_ref, xa_ref, xb_ref, out_ref, ya_ref, yb_ref):
    even = is_even("gx")
    xa, xb = unfold(xa_ref), unfold(xb_ref)
    blocks = [gas_ref[x * FY : (x + 1) * FY, :] for x in range(FX)]
    blocks = [jnp.where(even, xb, xa)] + blocks + [jnp.where(even, xa, xb)]
    along = [blocks[x] + 2.0 * blocks[x + 1] + blocks[x + 2] for x in range(FX)]
    for x in range(FX):
        out_ref[x * FY : (x + 1) * FY, :] = along[x]
    width = ya_ref.shape[1]
    edges = []
    for row in (0, FY - 1):
        edge = jnp.concatenate([along[x][row : row + 1] for x in range(FX)], axis=0)
        edges.append(jnp.concatenate([edge[:, :width], edge[:, width:]], axis=0))
    even = is_even("gy")
    ya_ref[...] = jnp.where(even, edges[1], edges[0]).astype(jnp.bfloat16)
    yb_ref[...] = jnp.where(even, edges[0], edges[1]).astype(jnp.bfloat16)


def drag_kernel(mark_ref, along_ref, ya_ref, yb_ref, drag_ref, back_ref):
    rows = drag_ref.shape[0]
    width = along_ref.shape[1] // 2
    lanes = rows * TILE
    even = is_even("gy")
    ya, yb = unfold(ya_ref), unfold(yb_ref)
    before, after = jnp.where(even, yb, ya), jnp.where(even, ya, yb)
    smooth = []
    for x in range(FX):
        block = along_ref[x * FY : (x + 1) * FY, :]
        padded = jnp.concatenate([before[x : x + 1], block, after[x : x + 1]], axis=0)
        smooth.append((padded[0:FY] + 2.0 * block + padded[2 : FY + 2]) / 16.0)
    smooth = jnp.concatenate(smooth, axis=0)
    halves = []
    for half in range(2):
        base = half * width
        density = smooth[:, base + lanes : base + lanes + TILE]
        below = 1.0 + density * density
        below = jnp.concatenate([below] * rows, axis=1)
        halves.append(smooth[:, base : base + lanes] / below)
    for r in range(rows):
        where = slice(r * TILE, (r + 1) * TILE)
        both = jnp.concatenate([halves[0][:, where], halves[1][:, where]], axis=1)
        drag_ref[r] = both.reshape(FX, FY, FZ).astype(jnp.bfloat16)
    mark = width % LANES
    marks = mark_ref[...].astype(jnp.float32)
    column, height = marks[:, mark : mark + 1], marks[:, mark + 1 : mark + 2]
    hot = one_hot(column == iota((1, COLS), 1).astype(jnp.float32))
    place = (iota((1, lanes), 1) % TILE).astype(jnp.float32)
    low = dot(hot, halves[0].astype(jnp.bfloat16))
    high = dot(hot, halves[1].astype(jnp.bfloat16))
    back_ref[...] = jnp.where(place >= height, low, high).astype(jnp.bfloat16)


def force_kernel(back_ref, slot_ref, code_ref, part_ref, small_ref, *refs):
    state_refs, out_ref, table_ref = refs[:4], refs[4], refs[5]
    rows, slots = out_ref.shape
    parts = part_ref.shape[1]
    tiles = slot_ref.shape[1]
    migr = (slots - parts) // 4
    match = one_hot(iota((back_ref.shape[0], tiles), 0) == slot_ref[...])
    table_ref[...] = dot(back_ref[...], match, TN).astype(jnp.bfloat16)
    channels = part_ref.shape[0]
    closure_row, live_row, _, _ = small_rows(rows, parts // GROUP, slots)
    damping = small_ref[closure_row:live_row, channels : channels + 1]

    def look(code):
        values = dot(table_ref[...], ones(equal(tiles, code // TILE))).astype(jnp.bfloat16)
        hit = equal(TILE, code % TILE)
        found = []
        for r in range(rows):
            picked = jnp.where(hit, values[r * TILE : (r + 1) * TILE], jnp.bfloat16(0))
            while picked.shape[0] > 16:
                half = picked.shape[0] // 2
                picked = picked[:half] + picked[half:]
            found.append(jnp.sum(picked.astype(jnp.float32), axis=0, keepdims=True))
        return jnp.concatenate(found, axis=0)

    for begin in range(0, parts, CHUNK):
        where = slice(begin, begin + CHUNK)
        live = side_by_side(small_ref, live_row, begin, CHUNK)
        out_ref[:, where] = live * (look(code_ref[:, where]) - damping * part_ref[:rows, where])
    drag = look(code_ref[:, parts:])
    for row in range(4):
        begin = parts + row * migr
        arrived = state_refs[row][:, :].astype(jnp.float32)
        live = jnp.concatenate([arrived[k : k + 1, migr:] for k in range(migr // LANES)], axis=1)
        force = drag[:, row * migr : (row + 1) * migr] - damping * arrived[:rows, :migr]
        out_ref[:, begin : begin + migr] = live * force


def call(kernel, shapes, *operands, limit=None, scratch=()):
    vmem = pl.BlockSpec(memory_space=pltpu.VMEM)
    operand = pl.BlockSpec(memory_space=pltpu.HBM) if limit else vmem
    return pl.pallas_call(
        kernel,
        out_shape=shapes,
        in_specs=[operand] * len(operands),
        out_specs=[vmem] * len(shapes),
        scratch_shapes=scratch,
        compiler_params=pltpu.CompilerParams(vmem_limit_bytes=limit or VMEM),
    )(*operands)


def shift(block, axis, step):
    size = lax.axis_size(axis)
    return lax.ppermute(block, axis, [(i, (i + step) % size) for i in range(size)])


def per_device(
    particles,
    migrant_index,
    migrant_count,
    migrated_slot_cell,
    source_tile_size,
    tile_owner,
    tile_offset,
    closure,
    damping,
):
    f32, bf16, i32 = jnp.float32, jnp.bfloat16, jnp.int32
    shape = jax.ShapeDtypeStruct
    channels, parts = particles.shape
    rows = closure.shape[0]
    migr = migrant_index.shape[1]
    slots = migrated_slot_cell.shape[0]
    tiles = source_tile_size.shape[1]
    devices = lax.axis_size("gx") * lax.axis_size("gy")
    capacity = max(2, 2 * tiles // devices)
    count = devices * capacity
    width = (rows + 1) * TILE
    lanes = (width + LANES) // LANES * LANES
    small_count = small_rows(rows, parts // GROUP, slots)[-1]
    operands = (
        particles, migrant_index, migrant_count, source_tile_size, tile_owner.reshape(1, tiles),
        tile_offset.reshape(1, tiles), closure, damping.reshape(1, rows), migrated_slot_cell.reshape(1, slots),
    )
    *leaving, small = call(
        pick_kernel,
        [shape((channels, migr + LANES), bf16)] * 4 + [shape((small_count, GROUP), f32)],
        *operands, limit=LARGE,
        scratch=[(pltpu.SMEM if i == 2 else pltpu.VMEM)(x.shape, x.dtype) for i, x in enumerate(operands)]
        + [pltpu.SemaphoreType.DMA((12,))],
    )
    arrived = [
        shift(block, axis, step)
        for block, (axis, step) in zip(leaving, (("gx", 1), ("gx", -1), ("gy", 1), ("gy", -1)))
    ]
    sums, code, slot, marks = call(
        functools.partial(deposit_kernel, capacity, rows),
        [shape((width, tiles), f32), shape((1, slots), i32), shape((1, tiles), i32),
         shape((lanes - width, tiles), bf16)],
        particles, small, scratch=[pltpu.VMEM((2, tiles, LANES), i32)],
    )
    (payload,) = call(
        functools.partial(pack_kernel, rows), [shape((count, lanes), bf16)],
        sums, code, slot, marks, small, *arrived,
    )
    received = lax.all_to_all(
        payload.reshape(devices, capacity, lanes), ("gx", "gy"), split_axis=0, concat_axis=0, tiled=True
    ).reshape(count, lanes)
    grid, edge = shape((COLS, 2 * width), f32), shape((2 * FX, width), bf16)
    gas, xa, xb = call(place_kernel, [grid, edge, edge], received)
    xa, xb = exchange(xa, xb, "gx")
    along, ya, yb = call(along_kernel, [grid, edge, edge], gas, xa, xb)
    ya, yb = exchange(ya, yb, "gy")
    drag, back = call(
        drag_kernel,
        [shape((rows, FX, FY, FZ), bf16), shape((count, rows * TILE), bf16)],
        received[:, lanes - LANES :], along, ya, yb,
    )
    returned = lax.all_to_all(
        back.reshape(devices, capacity, rows * TILE), ("gx", "gy"), split_axis=0, concat_axis=0, tiled=True
    ).reshape(count, rows * TILE)
    (force,) = call(
        force_kernel, [shape((rows, slots), f32)],
        returned, slot, code, particles, small, *arrived,
        scratch=[pltpu.VMEM((rows * TILE, tiles), bf16)],
    )
    return drag, force


def solution(mesh):
    both = ("gx", "gy")
    in_specs = (
        P(None, both),
        P(both, None),
        P(both, None),
        P(both),
        P(both, None),
        P(both, None),
        P(both),
        P(),
        P(),
    )
    out_specs = (P(None, "gx", "gy", None), P(None, both))
    return jax.shard_map(
        per_device, mesh=mesh, in_specs=in_specs, out_specs=out_specs, check_vma=False
    )
```

```python
import functools

import jax
import jax.numpy as jnp
from jax import lax
from jax.experimental import pallas as pl
from jax.experimental.pallas import tpu as pltpu
from jax.sharding import PartitionSpec as P

TILE = 64
FX = 8
FY = 8
FZ = 128
COLS = FX * FY
LANES = 128
GROUP = 256
CHUNK = 2048
VMEM = 48 * 1024 * 1024
LARGE = 63 * 1024 * 1024

NT = (((1,), (1,)), ((), ()))
TN = (((0,), (0,)), ((), ()))


def iota(shape, dim):
    return lax.broadcasted_iota(jnp.int32, shape, dim)


def dot(a, b, dims=(((1,), (0,)), ((), ()))):
    return lax.dot_general(a, b, dims, preferred_element_type=jnp.float32)


def one_hot(mask):
    return jnp.where(mask, 1.0, 0.0).astype(jnp.bfloat16)


def equal(rows, row):
    numbers = iota((rows, row.shape[1]), 0).astype(jnp.float32).astype(jnp.bfloat16)
    return numbers == row.astype(jnp.float32).astype(jnp.bfloat16)


def ones(mask):
    return jnp.where(mask, jnp.bfloat16(1), jnp.bfloat16(0))


def fetch(sources, targets, sems):
    copies = [
        pltpu.make_async_copy(source, target, sems.at[i])
        for i, (source, target) in enumerate(zip(sources, targets))
    ]
    for copy in copies:
        copy.start()
    return copies


def pieces(hbm, vmem):
    width = hbm.shape[1] // 4
    cuts = [slice(k * width, (k + 1) * width) for k in range(4)]
    return [hbm.at[:, cut] for cut in cuts], [vmem.at[:, cut] for cut in cuts]


def leaving_row(index_ref, count_ref, parts):
    migr = index_ref.shape[1]
    lane = iota((1, migr), 1)
    rows = [jnp.where(lane < count_ref[0, r], index_ref[r : r + 1, :], parts) for r in range(4)]
    return jnp.concatenate(rows, axis=1)


def small_rows(rows, groups, slots):
    live = 2 * rows
    cells = live + groups
    return rows, live, cells, cells + slots // GROUP


def pick_kernel(
    part_hbm, index_hbm, count_hbm, size_hbm, owner_hbm, offset_hbm, closure_hbm, damping_hbm, cell_hbm, *refs
):
    out_hbm, small_hbm, refs = refs[:4], refs[4], refs[5:]
    part_ref, index_ref, count_ref, size_ref, owner_ref, offset_ref = refs[:6]
    closure_ref, damping_ref, cell_ref, out_ref, small_ref, sems, out_sems = refs[6:]
    channels, parts = part_ref.shape
    migr = index_ref.shape[1]
    slots = cell_ref.shape[1]
    groups = parts // GROUP
    rows, width = closure_ref.shape
    closure_row, live_row, cell_row, _ = small_rows(rows, groups, slots)
    sources, targets = pieces(part_hbm, part_ref)
    copies = fetch(
        [index_hbm, count_hbm, size_hbm, owner_hbm, offset_hbm, closure_hbm, damping_hbm, cell_hbm] + sources,
        [index_ref, count_ref, size_ref, owner_ref, offset_ref, closure_ref, damping_ref, cell_ref] + targets,
        sems,
    )
    copies[0].wait()
    copies[1].wait()
    leave = leaving_row(index_ref, count_ref, parts)
    high = leave // GROUP
    low = ones(equal(GROUP, leave % GROUP))
    small_ref[live_row:cell_row, :] = 1.0 - dot(ones(equal(groups, high)), low, NT)
    for copy in copies[2:8]:
        copy.wait()
    for row, ref in enumerate((size_ref, owner_ref, offset_ref)):
        small_ref[row : row + 1, :] = ref[...].astype(jnp.float32)
    small_ref[closure_row:live_row, :width] = closure_ref[...]
    diagonal = iota((rows, rows), 0) == iota((rows, rows), 1)
    damping = jnp.sum(jnp.where(diagonal, damping_ref[...], 0.0), axis=1, keepdims=True)
    small_ref[closure_row:live_row, width : width + 1] = damping
    for k in range(slots // GROUP):
        row = cell_ref[:, k * GROUP : (k + 1) * GROUP]
        small_ref[cell_row + k : cell_row + k + 1, :] = row.astype(jnp.float32)
    stores = [pltpu.make_async_copy(small_ref, small_hbm, out_sems.at[4])]
    stores[0].start()
    for copy in copies[8:]:
        copy.wait()
    table = jnp.concatenate(
        [part_ref[:, g * GROUP : (g + 1) * GROUP].astype(jnp.bfloat16) for g in range(groups)], axis=0
    )
    rows = dot(table, low)
    picked = jnp.zeros((channels, 4 * migr), jnp.float32)
    for g in range(groups):
        picked = jnp.where(high == g, rows[g * channels : (g + 1) * channels], picked)
    live = jnp.where(leave < parts, 1.0, 0.0)
    for r in range(4):
        out_ref[r, :, :migr] = picked[:, r * migr : (r + 1) * migr].astype(jnp.bfloat16)
        flags = [live[:, k : k + LANES] for k in range(r * migr, (r + 1) * migr, LANES)]
        flags.append(jnp.zeros((channels - len(flags), LANES), jnp.float32))
        out_ref[r, :, migr:] = jnp.concatenate(flags, axis=0).astype(jnp.bfloat16)
        stores.append(pltpu.make_async_copy(out_ref.at[r], out_hbm[r], out_sems.at[r]))
        stores[-1].start()
    for store in stores:
        store.wait()


def mix(closure, state):
    state = state.astype(jnp.float32)
    mixed = closure[:, 0:1] * state[0:1]
    for f in range(1, state.shape[0]):
        mixed = mixed + closure[:, f : f + 1] * state[f : f + 1]
    return mixed, state[0:1]


def side_by_side(ref, first, begin, width):
    first = first + begin // GROUP
    rows = [ref[r : r + 1, :] for r in range(first, first + width // GROUP)]
    return jnp.concatenate(rows, axis=1)


def spread(mixed, first, place):
    hit = equal(TILE, place)
    values = jnp.concatenate([mixed, first], axis=0).astype(jnp.bfloat16)
    return jnp.concatenate(
        [jnp.where(hit, values[r : r + 1], jnp.bfloat16(0)) for r in range(values.shape[0])], axis=0
    )


def deposit_kernel(
    capacity, rows, part_ref, small_ref, sum_ref, code_ref, slot_ref, mark_ref, columns_ref,
):
    channels, parts = part_ref.shape
    slots = code_ref.shape[1]
    tiles = slot_ref.shape[1]
    closure_row, live_row, cell_row, _ = small_rows(rows, parts // GROUP, slots)
    closure = small_ref[closure_row:live_row, :channels]

    square = (tiles, tiles)
    below, across = iota(square, 0), iota(square, 1)

    def column(row):
        return jnp.sum(jnp.where(below == across, row, 0), axis=1, keepdims=True)

    sizes, owners, offset = [small_ref[r : r + 1, :].astype(jnp.int32) for r in range(3)]
    start = jnp.sum(jnp.where(across < below, sizes, 0), axis=1, keepdims=True)
    height = column(offset % FZ)
    code = iota((tiles, 1), 0) * TILE + (height - start) % TILE
    code_step = code - jnp.concatenate([jnp.zeros((1, 1), jnp.int32), code[: tiles - 1]], axis=0)
    earlier = (column(owners) == owners) & (below < across)
    rank = jnp.sum(jnp.where(earlier, 1, 0), axis=0, keepdims=True)
    slot_ref[...] = owners * capacity + rank
    columns_ref[0] = jnp.broadcast_to(start, (tiles, LANES))
    columns_ref[1] = jnp.broadcast_to(code_step, (tiles, LANES))
    rows = iota(mark_ref.shape, 0)
    marks = jnp.where(rows == 0, offset // FZ, jnp.where(rows == 1, offset % FZ, 0))
    mark_ref[...] = marks.astype(jnp.float32).astype(jnp.bfloat16)

    def find(begin):
        cell = side_by_side(small_ref, cell_row, begin, CHUNK).astype(jnp.int32)
        starts = jnp.concatenate([columns_ref[0]] * (CHUNK // LANES), axis=1)
        steps = jnp.concatenate([columns_ref[1]] * (CHUNK // LANES), axis=1)
        found = jnp.sum(jnp.where(cell >= starts, steps, 0), axis=0, keepdims=True)
        return found // TILE, (found + cell) % TILE

    for begin in range(parts, slots, CHUNK):
        tile, place = find(begin)
        code_ref[:, begin : begin + CHUNK] = tile * TILE + place
    for begin in range(0, parts, CHUNK):
        tile, place = find(begin)
        code_ref[:, begin : begin + CHUNK] = tile * TILE + place
        live = side_by_side(small_ref, live_row, begin, CHUNK)
        state = part_ref[:, begin : begin + CHUNK] * live
        mixed, first = mix(closure, state.astype(jnp.bfloat16))
        added = dot(spread(mixed, first, place), ones(equal(tiles, tile)), NT)
        if begin == 0:
            sum_ref[...] = added
        else:
            sum_ref[...] += added


def pack_kernel(rows, sum_ref, code_ref, slot_ref, mark_ref, small_ref, *refs):
    state_refs, out_ref = refs[:4], refs[4]
    channels, tiles = state_refs[0].shape[0], slot_ref.shape[1]
    closure = small_ref[rows : 2 * rows, :channels]
    migr = state_refs[0].shape[1] - LANES
    code = code_ref[:, code_ref.shape[1] - 4 * migr :]
    state = jnp.concatenate([ref[:, :migr] for ref in state_refs], axis=1)
    mixed, first = mix(closure, state)
    total = sum_ref[...] + dot(spread(mixed, first, code % TILE), ones(equal(tiles, code // TILE)), NT)
    table = jnp.concatenate([total.astype(jnp.bfloat16), mark_ref[...]], axis=0)
    match = one_hot(iota((out_ref.shape[0], tiles), 0) == slot_ref[...])
    out_ref[...] = dot(match, table, NT).astype(jnp.bfloat16)


def is_even(axis):
    return lax.axis_index(axis) % 2 == 0


def exchange(block_a, block_b, axis):
    size = lax.axis_size(axis)
    blocks = {}
    for odd, block in ((1, block_b), (0, block_a)):
        pairs = [(i, (i + 1) % size if i % 2 == odd else (i - 1) % size) for i in range(size)]
        blocks[odd] = lax.ppermute(block, axis, pairs)
    return blocks[0], blocks[1]


def place_kernel(tile_ref, gas_ref, xa_ref, xb_ref):
    even = is_even("gx")
    count, lanes = tile_ref.shape
    width = gas_ref.shape[1] // 2
    marks = tile_ref[:, lanes - LANES :].astype(jnp.float32)
    column = marks[:, width % LANES : width % LANES + 1]
    height = marks[:, width % LANES + 1 : width % LANES + 2]
    lane = iota((1, LANES), 1)
    hot = one_hot(column == lane.astype(jnp.float32))
    place = (iota((1, width), 1) % TILE).astype(jnp.float32)
    values = tile_ref[:, :width].astype(jnp.float32)
    for half, mask in enumerate((place >= height, place < height)):
        total = dot(hot, jnp.where(mask, values, 0.0).astype(jnp.bfloat16), TN)
        where = slice(half * width, (half + 1) * width)
        gas_ref[:, where] = total[:COLS]
        rows = slice(half * FY, (half + 1) * FY)
        low, high = total[:FY], total[COLS - FY : COLS]
        xa_ref[rows, :] = jnp.where(even, high, low).astype(jnp.bfloat16)
        xb_ref[rows, :] = jnp.where(even, low, high).astype(jnp.bfloat16)


def unfold(ref):
    edge = ref[...].astype(jnp.float32)
    half = edge.shape[0] // 2
    return jnp.concatenate([edge[:half], edge[half:]], axis=1)


def along_kernel(gas_ref, xa_ref, xb_ref, out_ref, ya_ref, yb_ref):
    even = is_even("gx")
    xa, xb = unfold(xa_ref), unfold(xb_ref)
    blocks = [gas_ref[x * FY : (x + 1) * FY, :] for x in range(FX)]
    blocks = [jnp.where(even, xb, xa)] + blocks + [jnp.where(even, xa, xb)]
    along = [blocks[x] + 2.0 * blocks[x + 1] + blocks[x + 2] for x in range(FX)]
    for x in range(FX):
        out_ref[x * FY : (x + 1) * FY, :] = along[x]
    width = ya_ref.shape[1]
    edges = []
    for row in (0, FY - 1):
        edge = jnp.concatenate([along[x][row : row + 1] for x in range(FX)], axis=0)
        edges.append(jnp.concatenate([edge[:, :width], edge[:, width:]], axis=0))
    even = is_even("gy")
    ya_ref[...] = jnp.where(even, edges[1], edges[0]).astype(jnp.bfloat16)
    yb_ref[...] = jnp.where(even, edges[0], edges[1]).astype(jnp.bfloat16)


def drag_kernel(mark_ref, along_ref, ya_ref, yb_ref, drag_ref, back_ref):
    rows = drag_ref.shape[0]
    width = along_ref.shape[1] // 2
    lanes = rows * TILE
    even = is_even("gy")
    ya, yb = unfold(ya_ref), unfold(yb_ref)
    before, after = jnp.where(even, yb, ya), jnp.where(even, ya, yb)
    smooth = []
    for x in range(FX):
        block = along_ref[x * FY : (x + 1) * FY, :]
        padded = jnp.concatenate([before[x : x + 1], block, after[x : x + 1]], axis=0)
        smooth.append((padded[0:FY] + 2.0 * block + padded[2 : FY + 2]) / 16.0)
    smooth = jnp.concatenate(smooth, axis=0)
    halves = []
    for half in range(2):
        base = half * width
        density = smooth[:, base + lanes : base + lanes + TILE]
        scale = 1.0 / (1.0 + density * density)
        halves.append(smooth[:, base : base + lanes] * jnp.concatenate([scale] * rows, axis=1))
    for r in range(rows):
        where = slice(r * TILE, (r + 1) * TILE)
        both = jnp.concatenate([halves[0][:, where], halves[1][:, where]], axis=1)
        drag_ref[r] = both.reshape(FX, FY, FZ).astype(jnp.bfloat16)
    mark = width % LANES
    marks = mark_ref[...].astype(jnp.float32)
    column, height = marks[:, mark : mark + 1], marks[:, mark + 1 : mark + 2]
    hot = one_hot(column == iota((1, COLS), 1).astype(jnp.float32))
    place = (iota((1, lanes), 1) % TILE).astype(jnp.float32)
    low = dot(hot, halves[0].astype(jnp.bfloat16))
    high = dot(hot, halves[1].astype(jnp.bfloat16))
    back_ref[...] = jnp.where(place >= height, low, high).astype(jnp.bfloat16)


def force_kernel(back_ref, slot_ref, code_ref, part_ref, small_ref, drag_ref, *refs):
    state_refs, out_ref, drag_hbm, table_ref, sem = refs[:4], refs[4], refs[5], refs[6], refs[7]
    store = pltpu.make_async_copy(drag_ref, drag_hbm, sem)
    store.start()
    rows, slots = out_ref.shape
    parts = part_ref.shape[1]
    tiles = slot_ref.shape[1]
    migr = (slots - parts) // 4
    match = one_hot(iota((back_ref.shape[0], tiles), 0) == slot_ref[...])
    table_ref[...] = dot(back_ref[...], match, TN).astype(jnp.bfloat16)
    channels = part_ref.shape[0]
    closure_row, live_row, _, _ = small_rows(rows, parts // GROUP, slots)
    damping = small_ref[closure_row:live_row, channels : channels + 1]

    def look(code):
        values = dot(table_ref[...], ones(equal(tiles, code // TILE))).astype(jnp.bfloat16)
        hit = equal(TILE, code % TILE)
        found = []
        for r in range(rows):
            picked = jnp.where(hit, values[r * TILE : (r + 1) * TILE], jnp.bfloat16(0))
            while picked.shape[0] > 16:
                half = picked.shape[0] // 2
                picked = picked[:half] + picked[half:]
            found.append(jnp.sum(picked.astype(jnp.float32), axis=0, keepdims=True))
        return jnp.concatenate(found, axis=0)

    for begin in range(0, parts, CHUNK):
        where = slice(begin, begin + CHUNK)
        live = side_by_side(small_ref, live_row, begin, CHUNK)
        out_ref[:, where] = live * (look(code_ref[:, where]) - damping * part_ref[:rows, where])
    drag = look(code_ref[:, parts:])
    for row in range(4):
        begin = parts + row * migr
        arrived = state_refs[row][:, :].astype(jnp.float32)
        live = jnp.concatenate([arrived[k : k + 1, migr:] for k in range(migr // LANES)], axis=1)
        force = drag[:, row * migr : (row + 1) * migr] - damping * arrived[:rows, :migr]
        out_ref[:, begin : begin + migr] = live * force
    store.wait()


def call(kernel, shapes, *operands, limit=None, late=(), scratch=()):
    vmem, hbm = pl.BlockSpec(memory_space=pltpu.VMEM), pl.BlockSpec(memory_space=pltpu.HBM)
    return pl.pallas_call(
        kernel,
        out_shape=shapes,
        in_specs=[hbm if limit else vmem] * len(operands),
        out_specs=[hbm if limit or i in late else vmem for i in range(len(shapes))],
        scratch_shapes=scratch,
        compiler_params=pltpu.CompilerParams(vmem_limit_bytes=limit or VMEM),
    )(*operands)


def shift(block, axis, step):
    size = lax.axis_size(axis)
    return lax.ppermute(block, axis, [(i, (i + step) % size) for i in range(size)])


def per_device(
    particles,
    migrant_index,
    migrant_count,
    migrated_slot_cell,
    source_tile_size,
    tile_owner,
    tile_offset,
    closure,
    damping,
):
    f32, bf16, i32 = jnp.float32, jnp.bfloat16, jnp.int32
    shape = jax.ShapeDtypeStruct
    channels, parts = particles.shape
    rows = closure.shape[0]
    migr = migrant_index.shape[1]
    slots = migrated_slot_cell.shape[0]
    tiles = source_tile_size.shape[1]
    devices = lax.axis_size("gx") * lax.axis_size("gy")
    capacity = max(2, 2 * tiles // devices)
    count = devices * capacity
    width = (rows + 1) * TILE
    lanes = (width + LANES) // LANES * LANES
    small_count = small_rows(rows, parts // GROUP, slots)[-1]
    operands = (
        particles, migrant_index, migrant_count, source_tile_size, tile_owner.reshape(1, tiles),
        tile_offset.reshape(1, tiles), closure, damping.reshape(1, rows), migrated_slot_cell.reshape(1, slots),
    )
    *leaving, small = call(
        pick_kernel,
        [shape((channels, migr + LANES), bf16)] * 4 + [shape((small_count, GROUP), f32)],
        *operands, limit=LARGE,
        scratch=[(pltpu.SMEM if i == 2 else pltpu.VMEM)(x.shape, x.dtype) for i, x in enumerate(operands)]
        + [pltpu.VMEM((4, channels, migr + LANES), bf16), pltpu.VMEM((small_count, GROUP), f32),
           pltpu.SemaphoreType.DMA((12,)), pltpu.SemaphoreType.DMA((5,))],
    )
    arrived = [
        shift(block, axis, step)
        for block, (axis, step) in zip(leaving, (("gx", 1), ("gx", -1), ("gy", 1), ("gy", -1)))
    ]
    sums, code, slot, marks = call(
        functools.partial(deposit_kernel, capacity, rows),
        [shape((width, tiles), f32), shape((1, slots), i32), shape((1, tiles), i32),
         shape((lanes - width, tiles), bf16)],
        particles, small, scratch=[pltpu.VMEM((2, tiles, LANES), i32)],
    )
    (payload,) = call(
        functools.partial(pack_kernel, rows), [shape((count, lanes), bf16)],
        sums, code, slot, marks, small, *arrived,
    )
    received = lax.all_to_all(
        payload.reshape(devices, capacity, lanes), ("gx", "gy"), split_axis=0, concat_axis=0, tiled=True
    ).reshape(count, lanes)
    grid, edge = shape((COLS, 2 * width), f32), shape((2 * FX, width), bf16)
    gas, xa, xb = call(place_kernel, [grid, edge, edge], received)
    xa, xb = exchange(xa, xb, "gx")
    along, ya, yb = call(along_kernel, [grid, edge, edge], gas, xa, xb)
    ya, yb = exchange(ya, yb, "gy")
    drag, back = call(
        drag_kernel,
        [shape((rows, FX, FY, FZ), bf16), shape((count, rows * TILE), bf16)],
        received[:, lanes - LANES :], along, ya, yb,
    )
    returned = lax.all_to_all(
        back.reshape(devices, capacity, rows * TILE), ("gx", "gy"), split_axis=0, concat_axis=0, tiled=True
    ).reshape(count, rows * TILE)
    force, drag = call(
        force_kernel, [shape((rows, slots), f32), shape(drag.shape, bf16)],
        returned, slot, code, particles, small, drag, *arrived, late=(1,),
        scratch=[pltpu.VMEM((rows * TILE, tiles), bf16), pltpu.SemaphoreType.DMA],
    )
    return drag, force


def solution(mesh):
    both = ("gx", "gy")
    in_specs = (
        P(None, both),
        P(both, None),
        P(both, None),
        P(both),
        P(both, None),
        P(both, None),
        P(both),
        P(),
        P(),
    )
    out_specs = (P(None, "gx", "gy", None), P(None, both))
    return jax.shard_map(
        per_device, mesh=mesh, in_specs=in_specs, out_specs=out_specs, check_vma=False
    )
```

```python
import functools

import jax
import jax.numpy as jnp
from jax import lax
from jax.experimental import pallas as pl
from jax.experimental.pallas import tpu as pltpu
from jax.sharding import PartitionSpec as P

TILE = 64
FX = 8
FY = 8
FZ = 128
COLS = FX * FY
LANES = 128
GROUP = 256
CHUNK = 2048
VMEM = 48 * 1024 * 1024
LARGE = 63 * 1024 * 1024

NT = (((1,), (1,)), ((), ()))
TN = (((0,), (0,)), ((), ()))


def iota(shape, dim):
    return lax.broadcasted_iota(jnp.int32, shape, dim)


def dot(a, b, dims=(((1,), (0,)), ((), ()))):
    return lax.dot_general(a, b, dims, preferred_element_type=jnp.float32)


def one_hot(mask):
    return jnp.where(mask, 1.0, 0.0).astype(jnp.bfloat16)


def equal(rows, row):
    numbers = iota((rows, row.shape[1]), 0).astype(jnp.float32).astype(jnp.bfloat16)
    return numbers == row.astype(jnp.float32).astype(jnp.bfloat16)


def ones(mask):
    return jnp.where(mask, jnp.bfloat16(1), jnp.bfloat16(0))


def fetch(sources, targets, sems):
    copies = [
        pltpu.make_async_copy(source, target, sems.at[i])
        for i, (source, target) in enumerate(zip(sources, targets))
    ]
    for copy in copies:
        copy.start()
    return copies


def leaving_row(index_ref, count_ref, parts):
    migr = index_ref.shape[1]
    lane = iota((1, migr), 1)
    rows = [jnp.where(lane < count_ref[0, r], index_ref[r : r + 1, :], parts) for r in range(4)]
    return jnp.concatenate(rows, axis=1)


def small_rows(rows, leaving, slots):
    leave = 2 * rows
    cells = leave + leaving // GROUP
    return rows, leave, cells, cells + slots // GROUP


def pick_kernel(
    part_hbm, index_hbm, count_hbm, size_hbm, owner_hbm, offset_hbm, closure_hbm, damping_hbm, cell_hbm, *refs
):
    out_hbm, small_hbm, refs = refs[:4], refs[4], refs[5:]
    part_ref, index_ref, count_ref, size_ref, owner_ref, offset_ref = refs[:6]
    closure_ref, damping_ref, cell_ref, out_ref, small_ref, sems, out_sems = refs[6:]
    channels, parts = part_ref.shape
    migr = index_ref.shape[1]
    slots = cell_ref.shape[1]
    groups = parts // GROUP
    rows, width = closure_ref.shape
    closure_row, leave_row, cell_row, _ = small_rows(rows, 4 * migr, slots)
    copies = fetch(
        [index_hbm, count_hbm, part_hbm, size_hbm, owner_hbm, offset_hbm, closure_hbm, damping_hbm, cell_hbm],
        [index_ref, count_ref, part_ref, size_ref, owner_ref, offset_ref, closure_ref, damping_ref, cell_ref],
        sems,
    )
    copies[0].wait()
    copies[1].wait()
    leave = leaving_row(index_ref, count_ref, parts)
    high = leave // GROUP
    low = ones(equal(GROUP, leave % GROUP))
    for copy in copies[3:]:
        copy.wait()
    for row, ref in enumerate((size_ref, owner_ref, offset_ref)):
        small_ref[row : row + 1, :] = ref[...].astype(jnp.float32)
    small_ref[closure_row:leave_row, :width] = closure_ref[...]
    diagonal = iota((rows, rows), 0) == iota((rows, rows), 1)
    damping = jnp.sum(jnp.where(diagonal, damping_ref[...], 0.0), axis=1, keepdims=True)
    small_ref[closure_row:leave_row, width : width + 1] = damping
    for first, line in ((leave_row, leave), (cell_row, cell_ref[...])):
        for k in range(line.shape[1] // GROUP):
            part = line[:, k * GROUP : (k + 1) * GROUP]
            small_ref[first + k : first + k + 1, :] = part.astype(jnp.float32)
    stores = [pltpu.make_async_copy(small_ref, small_hbm, out_sems.at[4])]
    stores[0].start()
    copies[2].wait()
    table = jnp.concatenate(
        [part_ref[:, g * GROUP : (g + 1) * GROUP].astype(jnp.bfloat16) for g in range(groups)], axis=0
    )
    live = jnp.where(leave < parts, 1.0, 0.0)
    for r in range(4):
        where = slice(r * migr, (r + 1) * migr)
        found = dot(table, low[:, where])
        picked = jnp.zeros((channels, migr), jnp.float32)
        for g in range(groups):
            picked = jnp.where(high[:, where] == g, found[g * channels : (g + 1) * channels], picked)
        out_ref[r, :, :migr] = picked.astype(jnp.bfloat16)
        flags = [live[:, k : k + LANES] for k in range(r * migr, (r + 1) * migr, LANES)]
        flags.append(jnp.zeros((channels - len(flags), LANES), jnp.float32))
        out_ref[r, :, migr:] = jnp.concatenate(flags, axis=0).astype(jnp.bfloat16)
        stores.append(pltpu.make_async_copy(out_ref.at[r], out_hbm[r], out_sems.at[r]))
        stores[-1].start()
    for store in stores:
        store.wait()


def mix(closure, state):
    state = state.astype(jnp.float32)
    mixed = closure[:, 0:1] * state[0:1]
    for f in range(1, state.shape[0]):
        mixed = mixed + closure[:, f : f + 1] * state[f : f + 1]
    return mixed, state[0:1]


def side_by_side(ref, first, begin, width):
    first = first + begin // GROUP
    rows = [ref[r : r + 1, :] for r in range(first, first + width // GROUP)]
    return jnp.concatenate(rows, axis=1)


def spread(mixed, first, place):
    hit = equal(TILE, place)
    values = jnp.concatenate([mixed, first], axis=0).astype(jnp.bfloat16)
    return jnp.concatenate(
        [jnp.where(hit, values[r : r + 1], jnp.bfloat16(0)) for r in range(values.shape[0])], axis=0
    )


def deposit_kernel(
    capacity, rows, leaving, part_ref, small_ref, sum_ref, code_ref, slot_ref, mark_ref, live_ref, columns_ref
):
    channels, parts = part_ref.shape
    slots = code_ref.shape[1]
    tiles = slot_ref.shape[1]
    groups = parts // GROUP
    closure_row, leave_row, cell_row, _ = small_rows(rows, leaving, slots)
    closure = small_ref[closure_row:leave_row, :channels]

    leave = side_by_side(small_ref, leave_row, 0, leaving).astype(jnp.int32)
    pieces = leaving // LANES
    columns = [leave[:, k * LANES : (k + 1) * LANES] % GROUP for k in range(pieces)]
    columns.append(jnp.zeros((LANES - pieces, LANES), jnp.int32))
    columns = jnp.concatenate(columns, axis=0).astype(jnp.float32).T
    lane = iota((LANES, GROUP), 1).astype(jnp.float32)
    low = jnp.concatenate([one_hot(lane == columns[:, k : k + 1]) for k in range(pieces)], axis=0)
    live_ref[...] = 1.0 - dot(ones(equal(groups, leave // GROUP)), low)

    sizes, owners, offset = [small_ref[r : r + 1, :] for r in range(3)]
    offset = offset.astype(jnp.int32)
    square = (tiles, tiles)
    below, across = iota(square, 0), iota(square, 1)
    inputs = [sizes, owners, (offset % FZ).astype(jnp.float32), jnp.zeros((5, tiles), jnp.float32)]
    inputs = jnp.concatenate(inputs, axis=0).astype(jnp.bfloat16)
    turned = dot(ones(below == across), inputs, NT)
    start = dot(ones(across < below), inputs, NT)[:, 0:1].astype(jnp.int32)
    height = turned[:, 2:3].astype(jnp.int32)
    code = iota((tiles, 1), 0) * TILE + (height - start) % TILE
    code_step = code - jnp.concatenate([jnp.zeros((1, 1), jnp.int32), code[: tiles - 1]], axis=0)
    earlier = ones((turned[:, 1:2] == owners) & (below < across))
    rank = dot(jnp.ones((8, tiles), jnp.bfloat16), earlier)[0:1]
    slot_ref[...] = (owners * capacity + rank).astype(jnp.int32)
    columns_ref[0] = jnp.broadcast_to(start, (tiles, LANES)).astype(jnp.int16)
    columns_ref[1] = jnp.broadcast_to(code_step, (tiles, LANES)).astype(jnp.int16)
    lines = iota(mark_ref.shape, 0)
    marks = jnp.where(lines == 0, offset // FZ, jnp.where(lines == 1, offset % FZ, 0))
    mark_ref[...] = marks.astype(jnp.float32).astype(jnp.bfloat16)

    def find(begin):
        cell = side_by_side(small_ref, cell_row, begin, CHUNK).astype(jnp.int32)
        starts = jnp.concatenate([columns_ref[0]] * (CHUNK // LANES), axis=1)
        steps = jnp.concatenate([columns_ref[1]] * (CHUNK // LANES), axis=1)
        found = jnp.where(cell.astype(jnp.int16) >= starts, steps, jnp.int16(0))
        while found.shape[0] > 16:
            half = found.shape[0] // 2
            found = found[:half] + found[half:]
        found = jnp.sum(found.astype(jnp.int32), axis=0, keepdims=True) & 0xFFFF
        return found // TILE, (found + cell) % TILE

    for begin in range(parts, slots, CHUNK):
        tile, place = find(begin)
        code_ref[:, begin : begin + CHUNK] = tile * TILE + place
    for begin in range(0, parts, CHUNK):
        tile, place = find(begin)
        code_ref[:, begin : begin + CHUNK] = tile * TILE + place
        live = side_by_side(live_ref, 0, begin, CHUNK)
        state = part_ref[:, begin : begin + CHUNK] * live
        mixed, first = mix(closure, state.astype(jnp.bfloat16))
        added = dot(spread(mixed, first, place), ones(equal(tiles, tile)), NT)
        if begin == 0:
            sum_ref[...] = added
        else:
            sum_ref[...] += added


def pack_kernel(rows, sum_ref, code_ref, slot_ref, mark_ref, small_ref, *refs):
    state_refs, out_ref = refs[:4], refs[4]
    channels, tiles = state_refs[0].shape[0], slot_ref.shape[1]
    closure = small_ref[rows : 2 * rows, :channels]
    migr = state_refs[0].shape[1] - LANES
    code = code_ref[:, code_ref.shape[1] - 4 * migr :]
    state = jnp.concatenate([ref[:, :migr] for ref in state_refs], axis=1)
    mixed, first = mix(closure, state)
    total = sum_ref[...] + dot(spread(mixed, first, code % TILE), ones(equal(tiles, code // TILE)), NT)
    table = jnp.concatenate([total.astype(jnp.bfloat16), mark_ref[...]], axis=0)
    match = one_hot(iota((out_ref.shape[0], tiles), 0) == slot_ref[...])
    out_ref[...] = dot(match, table, NT).astype(jnp.bfloat16)


def is_even(axis):
    return lax.axis_index(axis) % 2 == 0


def exchange(block_a, block_b, axis):
    size = lax.axis_size(axis)
    blocks = {}
    for odd, block in ((1, block_b), (0, block_a)):
        pairs = [(i, (i + 1) % size if i % 2 == odd else (i - 1) % size) for i in range(size)]
        blocks[odd] = lax.ppermute(block, axis, pairs)
    return blocks[0], blocks[1]


def place_kernel(tile_ref, gas_ref, xa_ref, xb_ref):
    even = is_even("gx")
    count, lanes = tile_ref.shape
    width = gas_ref.shape[1] // 2
    marks = tile_ref[:, lanes - LANES :].astype(jnp.float32)
    column = marks[:, width % LANES : width % LANES + 1]
    height = marks[:, width % LANES + 1 : width % LANES + 2]
    lane = iota((1, LANES), 1)
    hot = one_hot(column == lane.astype(jnp.float32))
    place = (iota((1, width), 1) % TILE).astype(jnp.float32)
    values = tile_ref[:, :width].astype(jnp.float32)
    for half, mask in enumerate((place >= height, place < height)):
        total = dot(hot, jnp.where(mask, values, 0.0).astype(jnp.bfloat16), TN)
        where = slice(half * width, (half + 1) * width)
        gas_ref[:, where] = total[:COLS]
        rows = slice(half * FY, (half + 1) * FY)
        low, high = total[:FY], total[COLS - FY : COLS]
        xa_ref[rows, :] = jnp.where(even, high, low).astype(jnp.bfloat16)
        xb_ref[rows, :] = jnp.where(even, low, high).astype(jnp.bfloat16)


def unfold(ref):
    edge = ref[...].astype(jnp.float32)
    half = edge.shape[0] // 2
    return jnp.concatenate([edge[:half], edge[half:]], axis=1)


def along_kernel(gas_ref, xb_ref, xa_ref, out_ref, ya_ref, yb_ref):
    even = is_even("gx")
    xa, xb = unfold(xa_ref), unfold(xb_ref)
    blocks = [gas_ref[x * FY : (x + 1) * FY, :] for x in range(FX)]
    blocks = [jnp.where(even, xb, xa)] + blocks + [jnp.where(even, xa, xb)]
    along = [blocks[x] + 2.0 * blocks[x + 1] + blocks[x + 2] for x in range(FX)]
    for x in range(FX):
        out_ref[x * FY : (x + 1) * FY, :] = along[x]
    width = ya_ref.shape[1]
    edges = []
    for row in (0, FY - 1):
        edge = jnp.concatenate([along[x][row : row + 1] for x in range(FX)], axis=0)
        edges.append(jnp.concatenate([edge[:, :width], edge[:, width:]], axis=0))
    even = is_even("gy")
    ya_ref[...] = jnp.where(even, edges[1], edges[0]).astype(jnp.bfloat16)
    yb_ref[...] = jnp.where(even, edges[0], edges[1]).astype(jnp.bfloat16)


def drag_kernel(mark_ref, along_ref, yb_ref, ya_ref, drag_ref, back_ref):
    rows = drag_ref.shape[0]
    width = along_ref.shape[1] // 2
    lanes = rows * TILE
    even = is_even("gy")
    ya, yb = unfold(ya_ref), unfold(yb_ref)
    before, after = jnp.where(even, yb, ya), jnp.where(even, ya, yb)
    smooth = []
    for x in range(FX):
        block = along_ref[x * FY : (x + 1) * FY, :]
        padded = jnp.concatenate([before[x : x + 1], block, after[x : x + 1]], axis=0)
        smooth.append((padded[0:FY] + 2.0 * block + padded[2 : FY + 2]) / 16.0)
    smooth = jnp.concatenate(smooth, axis=0)
    halves = []
    for half in range(2):
        base = half * width
        density = smooth[:, base + lanes : base + lanes + TILE]
        scale = 1.0 / (1.0 + density * density)
        halves.append(smooth[:, base : base + lanes] * jnp.concatenate([scale] * rows, axis=1))
    for r in range(rows):
        where = slice(r * TILE, (r + 1) * TILE)
        both = jnp.concatenate([halves[0][:, where], halves[1][:, where]], axis=1)
        drag_ref[r] = both.reshape(FX, FY, FZ).astype(jnp.bfloat16)
    mark = width % LANES
    marks = mark_ref[...].astype(jnp.float32)
    column, height = marks[:, mark : mark + 1], marks[:, mark + 1 : mark + 2]
    hot = one_hot(column == iota((1, COLS), 1).astype(jnp.float32))
    place = (iota((1, lanes), 1) % TILE).astype(jnp.float32)
    low = dot(hot, halves[0].astype(jnp.bfloat16))
    high = dot(hot, halves[1].astype(jnp.bfloat16))
    back_ref[...] = jnp.where(place >= height, low, high).astype(jnp.bfloat16)


def force_kernel(back_ref, slot_ref, code_ref, part_ref, small_ref, live_ref, drag_ref, *refs):
    state_refs, (out_hbm, drag_hbm, out_ref, table_ref, sems) = refs[:4], refs[4:]
    stores = [pltpu.make_async_copy(drag_ref, drag_hbm, sems.at[0])]
    stores[0].start()

    def store(where):
        stores.append(pltpu.make_async_copy(out_ref.at[:, where], out_hbm.at[:, where], sems.at[len(stores)]))
        stores[-1].start()

    rows, slots = out_ref.shape
    parts = part_ref.shape[1]
    tiles = slot_ref.shape[1]
    migr = (slots - parts) // 4
    match = one_hot(iota((back_ref.shape[0], tiles), 0) == slot_ref[...])
    table_ref[...] = dot(back_ref[...], match, TN).astype(jnp.bfloat16)
    channels = part_ref.shape[0]
    damping = small_ref[rows : 2 * rows, channels : channels + 1]

    def look(code):
        values = dot(table_ref[...], ones(equal(tiles, code // TILE))).astype(jnp.bfloat16)
        hit = equal(TILE, code % TILE)
        found = []
        for r in range(rows):
            picked = jnp.where(hit, values[r * TILE : (r + 1) * TILE], jnp.bfloat16(0))
            while picked.shape[0] > 16:
                half = picked.shape[0] // 2
                picked = picked[:half] + picked[half:]
            found.append(jnp.sum(picked.astype(jnp.float32), axis=0, keepdims=True))
        return jnp.concatenate(found, axis=0)

    for begin in range(0, parts, CHUNK):
        where = slice(begin, begin + CHUNK)
        live = side_by_side(live_ref, 0, begin, CHUNK)
        out_ref[:, where] = live * (look(code_ref[:, where]) - damping * part_ref[:rows, where])
        store(where)
    drag = look(code_ref[:, parts:])
    for row in range(4):
        begin = parts + row * migr
        arrived = state_refs[row][:, :].astype(jnp.float32)
        live = jnp.concatenate([arrived[k : k + 1, migr:] for k in range(migr // LANES)], axis=1)
        force = drag[:, row * migr : (row + 1) * migr] - damping * arrived[:rows, :migr]
        out_ref[:, begin : begin + migr] = live * force
    store(slice(parts, slots))
    for copy in stores:
        copy.wait()


def call(kernel, shapes, *operands, limit=None, late=(), scratch=()):
    vmem, hbm = pl.BlockSpec(memory_space=pltpu.VMEM), pl.BlockSpec(memory_space=pltpu.HBM)
    return pl.pallas_call(
        kernel,
        out_shape=shapes,
        in_specs=[hbm if limit else vmem] * len(operands),
        out_specs=[hbm if limit or i in late else vmem for i in range(len(shapes))],
        scratch_shapes=scratch,
        compiler_params=pltpu.CompilerParams(vmem_limit_bytes=limit or VMEM),
    )(*operands)


def shift(block, axis, step):
    size = lax.axis_size(axis)
    return lax.ppermute(block, axis, [(i, (i + step) % size) for i in range(size)])


def per_device(
    particles,
    migrant_index,
    migrant_count,
    migrated_slot_cell,
    source_tile_size,
    tile_owner,
    tile_offset,
    closure,
    damping,
):
    f32, bf16, i32 = jnp.float32, jnp.bfloat16, jnp.int32
    shape = jax.ShapeDtypeStruct
    channels, parts = particles.shape
    rows = closure.shape[0]
    migr = migrant_index.shape[1]
    slots = migrated_slot_cell.shape[0]
    tiles = source_tile_size.shape[1]
    devices = lax.axis_size("gx") * lax.axis_size("gy")
    capacity = max(2, 2 * tiles // devices)
    count = devices * capacity
    width = (rows + 1) * TILE
    lanes = (width + LANES) // LANES * LANES
    small_count = small_rows(rows, 4 * migr, slots)[-1]
    operands = (
        particles, migrant_index, migrant_count, source_tile_size, tile_owner.reshape(1, tiles),
        tile_offset.reshape(1, tiles), closure, damping.reshape(1, rows), migrated_slot_cell.reshape(1, slots),
    )
    *leaving, small = call(
        pick_kernel,
        [shape((channels, migr + LANES), bf16)] * 4 + [shape((small_count, GROUP), f32)],
        *operands, limit=LARGE,
        scratch=[(pltpu.SMEM if i == 2 else pltpu.VMEM)(x.shape, x.dtype) for i, x in enumerate(operands)]
        + [pltpu.VMEM((4, channels, migr + LANES), bf16), pltpu.VMEM((small_count, GROUP), f32),
           pltpu.SemaphoreType.DMA((9,)), pltpu.SemaphoreType.DMA((5,))],
    )
    arrived = [
        shift(block, axis, step)
        for block, (axis, step) in zip(leaving, (("gx", 1), ("gx", -1), ("gy", 1), ("gy", -1)))
    ]
    sums, code, slot, marks, live = call(
        functools.partial(deposit_kernel, capacity, rows, 4 * migr),
        [shape((width, tiles), f32), shape((1, slots), i32), shape((1, tiles), i32),
         shape((lanes - width, tiles), bf16), shape((parts // GROUP, GROUP), f32)],
        particles, small, scratch=[pltpu.VMEM((2, tiles, LANES), jnp.int16)],
    )
    (payload,) = call(
        functools.partial(pack_kernel, rows), [shape((count, lanes), bf16)],
        sums, code, slot, marks, small, *arrived,
    )
    received = lax.all_to_all(
        payload.reshape(devices, capacity, lanes), ("gx", "gy"), split_axis=0, concat_axis=0, tiled=True
    ).reshape(count, lanes)
    grid, edge = shape((COLS, 2 * width), f32), shape((2 * FX, width), bf16)
    gas, xa, xb = call(place_kernel, [grid, edge, edge], received)
    xa, xb = exchange(xa, xb, "gx")
    along, ya, yb = call(along_kernel, [grid, edge, edge], gas, xb, xa)
    ya, yb = exchange(ya, yb, "gy")
    drag, back = call(
        drag_kernel,
        [shape((rows, FX, FY, FZ), bf16), shape((count, rows * TILE), bf16)],
        received[:, lanes - LANES :], along, yb, ya,
    )
    returned = lax.all_to_all(
        back.reshape(devices, capacity, rows * TILE), ("gx", "gy"), split_axis=0, concat_axis=0, tiled=True
    ).reshape(count, rows * TILE)
    force, drag = call(
        force_kernel, [shape((rows, slots), f32), shape(drag.shape, bf16)],
        returned, slot, code, particles, small, live, drag, *arrived, late=(0, 1),
        scratch=[pltpu.VMEM((rows, slots), f32), pltpu.VMEM((rows * TILE, tiles), bf16),
                 pltpu.SemaphoreType.DMA((2 + parts // CHUNK,))],
    )
    return drag, force


def solution(mesh):
    both = ("gx", "gy")
    in_specs = (
        P(None, both),
        P(both, None),
        P(both, None),
        P(both),
        P(both, None),
        P(both, None),
        P(both),
        P(),
        P(),
    )
    out_specs = (P(None, "gx", "gy", None), P(None, both))
    return jax.shard_map(
        per_device, mesh=mesh, in_specs=in_specs, out_specs=out_specs, check_vma=False
    )
```

```python
import functools

import jax
import jax.numpy as jnp
from jax import lax
from jax.experimental import pallas as pl
from jax.experimental.pallas import tpu as pltpu
from jax.sharding import PartitionSpec as P

TILE = 64
FX = 8
FY = 8
FZ = 128
COLS = FX * FY
LANES = 128
GROUP = 256
CHUNK = 2048
VMEM = 48 * 1024 * 1024
LARGE = 63 * 1024 * 1024

NT = (((1,), (1,)), ((), ()))
TN = (((0,), (0,)), ((), ()))


def iota(shape, dim):
    return lax.broadcasted_iota(jnp.int32, shape, dim)


def dot(a, b, dims=(((1,), (0,)), ((), ()))):
    return lax.dot_general(a, b, dims, preferred_element_type=jnp.float32)


def one_hot(mask):
    return jnp.where(mask, 1.0, 0.0).astype(jnp.bfloat16)


def equal(rows, row):
    numbers = iota((rows, row.shape[1]), 0).astype(jnp.float32).astype(jnp.bfloat16)
    return numbers == row.astype(jnp.float32).astype(jnp.bfloat16)


def ones(mask):
    return jnp.where(mask, jnp.bfloat16(1), jnp.bfloat16(0))


def fetch(sources, targets, sems):
    copies = [
        pltpu.make_async_copy(source, target, sems.at[i])
        for i, (source, target) in enumerate(zip(sources, targets))
    ]
    for copy in copies:
        copy.start()
    return copies


def is_even(axis):
    return lax.axis_index(axis) % 2 == 0


def exchange(block_a, block_b, axis):
    size = lax.axis_size(axis)
    blocks = {}
    for odd, block in ((1, block_b), (0, block_a)):
        pairs = [(i, (i + 1) % size if i % 2 == odd else (i - 1) % size) for i in range(size)]
        blocks[odd] = lax.ppermute(block, axis, pairs)
    return blocks[0], blocks[1]


def ordered(first, second, axis):
    even = is_even(axis)
    return jnp.where(even, second, first), jnp.where(even, first, second)


def leaving_row(index_ref, count_ref, parts):
    migr = index_ref.shape[1]
    lane = iota((1, migr), 1)
    odd = [jnp.where(is_even(axis), 0, 1) for axis in ("gx", "gy")]
    rows = []
    for row in (odd[0], 1 - odd[0], 2 + odd[1], 3 - odd[1]):
        rows.append(jnp.where(lane < count_ref[0, row], index_ref[pl.ds(row, 1), :], parts))
    return jnp.concatenate(rows, axis=1)


def arrived_blocks(refs):
    blocks = [ref[...].astype(jnp.float32) for ref in refs]
    return ordered(blocks[0], blocks[1], "gx") + ordered(blocks[2], blocks[3], "gy")


def small_rows(rows, leaving, slots):
    leave = 2 * rows
    cells = leave + leaving // GROUP
    return rows, leave, cells, cells + slots // GROUP


def pick_kernel(
    part_hbm, index_hbm, count_hbm, size_hbm, owner_hbm, offset_hbm, closure_hbm, damping_hbm, cell_hbm, *refs
):
    out_hbm, small_hbm, refs = refs[:4], refs[4], refs[5:]
    part_ref, index_ref, count_ref, size_ref, owner_ref, offset_ref = refs[:6]
    closure_ref, damping_ref, cell_ref, out_ref, small_ref, sems, out_sems = refs[6:]
    channels, parts = part_ref.shape
    migr = index_ref.shape[1]
    slots = cell_ref.shape[1]
    groups = parts // GROUP
    rows, width = closure_ref.shape
    closure_row, leave_row, cell_row, _ = small_rows(rows, 4 * migr, slots)
    copies = fetch(
        [index_hbm, count_hbm, part_hbm, size_hbm, owner_hbm, offset_hbm, closure_hbm, damping_hbm, cell_hbm],
        [index_ref, count_ref, part_ref, size_ref, owner_ref, offset_ref, closure_ref, damping_ref, cell_ref],
        sems,
    )
    copies[0].wait()
    copies[1].wait()
    leave = leaving_row(index_ref, count_ref, parts)
    high = leave // GROUP
    low = ones(equal(GROUP, leave % GROUP))
    for copy in copies[3:]:
        copy.wait()
    for row, ref in enumerate((size_ref, owner_ref, offset_ref)):
        small_ref[row : row + 1, :] = ref[...].astype(jnp.float32)
    small_ref[closure_row:leave_row, :width] = closure_ref[...]
    diagonal = iota((rows, rows), 0) == iota((rows, rows), 1)
    damping = jnp.sum(jnp.where(diagonal, damping_ref[...], 0.0), axis=1, keepdims=True)
    small_ref[closure_row:leave_row, width : width + 1] = damping
    for first, line in ((leave_row, leave), (cell_row, cell_ref[...])):
        for k in range(line.shape[1] // GROUP):
            part = line[:, k * GROUP : (k + 1) * GROUP]
            small_ref[first + k : first + k + 1, :] = part.astype(jnp.float32)
    stores = [pltpu.make_async_copy(small_ref, small_hbm, out_sems.at[4])]
    stores[0].start()
    copies[2].wait()
    table = jnp.concatenate(
        [part_ref[:, g * GROUP : (g + 1) * GROUP].astype(jnp.bfloat16) for g in range(groups)], axis=0
    )
    live = jnp.where(leave < parts, 1.0, 0.0)
    for r in range(4):
        where = slice(r * migr, (r + 1) * migr)
        found = dot(table, low[:, where])
        picked = jnp.zeros((channels, migr), jnp.float32)
        for g in range(groups):
            picked = jnp.where(high[:, where] == g, found[g * channels : (g + 1) * channels], picked)
        out_ref[r, :, :migr] = picked.astype(jnp.bfloat16)
        flags = [live[:, k : k + LANES] for k in range(r * migr, (r + 1) * migr, LANES)]
        flags.append(jnp.zeros((channels - len(flags), LANES), jnp.float32))
        out_ref[r, :, migr:] = jnp.concatenate(flags, axis=0).astype(jnp.bfloat16)
        stores.append(pltpu.make_async_copy(out_ref.at[r], out_hbm[r], out_sems.at[r]))
        stores[-1].start()
    for store in stores:
        store.wait()


def mix(closure, state):
    state = state.astype(jnp.float32)
    mixed = closure[:, 0:1] * state[0:1]
    for f in range(1, state.shape[0]):
        mixed = mixed + closure[:, f : f + 1] * state[f : f + 1]
    return mixed, state[0:1]


def side_by_side(ref, first, begin, width):
    first = first + begin // GROUP
    rows = [ref[r : r + 1, :] for r in range(first, first + width // GROUP)]
    return jnp.concatenate(rows, axis=1)


def spread(mixed, first, place):
    hit = equal(TILE, place)
    values = jnp.concatenate([mixed, first], axis=0).astype(jnp.bfloat16)
    return jnp.concatenate(
        [jnp.where(hit, values[r : r + 1], jnp.bfloat16(0)) for r in range(values.shape[0])], axis=0
    )


def deposit_kernel(
    capacity, rows, leaving, part_ref, small_ref, sum_ref, code_ref, slot_ref, mark_ref, live_ref, columns_ref
):
    channels, parts = part_ref.shape
    slots = code_ref.shape[1]
    tiles = slot_ref.shape[1]
    groups = parts // GROUP
    closure_row, leave_row, cell_row, _ = small_rows(rows, leaving, slots)
    closure = small_ref[closure_row:leave_row, :channels]

    leave = side_by_side(small_ref, leave_row, 0, leaving).astype(jnp.int32)
    pieces = leaving // LANES
    columns = [leave[:, k * LANES : (k + 1) * LANES] % GROUP for k in range(pieces)]
    columns.append(jnp.zeros((LANES - pieces, LANES), jnp.int32))
    columns = jnp.concatenate(columns, axis=0).astype(jnp.float32).T
    lane = iota((LANES, GROUP), 1).astype(jnp.float32)
    low = jnp.concatenate([one_hot(lane == columns[:, k : k + 1]) for k in range(pieces)], axis=0)
    live_ref[...] = 1.0 - dot(ones(equal(groups, leave // GROUP)), low)

    sizes, owners, offset = [small_ref[r : r + 1, :] for r in range(3)]
    offset = offset.astype(jnp.int32)
    square = (tiles, tiles)
    below, across = iota(square, 0), iota(square, 1)
    inputs = [sizes, owners, (offset % FZ).astype(jnp.float32), jnp.zeros((5, tiles), jnp.float32)]
    inputs = jnp.concatenate(inputs, axis=0).astype(jnp.bfloat16)
    turned = dot(ones(below == across), inputs, NT)
    start = dot(ones(across < below), inputs, NT)[:, 0:1].astype(jnp.int32)
    height = turned[:, 2:3].astype(jnp.int32)
    code = iota((tiles, 1), 0) * TILE + (height - start) % TILE
    code_step = code - jnp.concatenate([jnp.zeros((1, 1), jnp.int32), code[: tiles - 1]], axis=0)
    earlier = ones((turned[:, 1:2] == owners) & (below < across))
    rank = dot(jnp.ones((8, tiles), jnp.bfloat16), earlier)[0:1]
    slot_ref[...] = (owners * capacity + rank).astype(jnp.int32)
    columns_ref[0] = jnp.broadcast_to(start, (tiles, LANES)).astype(jnp.int16)
    columns_ref[1] = jnp.broadcast_to(code_step, (tiles, LANES)).astype(jnp.int16)
    lines = iota(mark_ref.shape, 0)
    marks = jnp.where(lines == 0, offset // FZ, jnp.where(lines == 1, offset % FZ, 0))
    mark_ref[...] = marks.astype(jnp.float32).astype(jnp.bfloat16)

    def find(begin):
        cell = side_by_side(small_ref, cell_row, begin, CHUNK).astype(jnp.int32)
        starts = jnp.concatenate([columns_ref[0]] * (CHUNK // LANES), axis=1)
        steps = jnp.concatenate([columns_ref[1]] * (CHUNK // LANES), axis=1)
        found = jnp.where(cell.astype(jnp.int16) >= starts, steps, jnp.int16(0))
        while found.shape[0] > 16:
            half = found.shape[0] // 2
            found = found[:half] + found[half:]
        found = jnp.sum(found.astype(jnp.int32), axis=0, keepdims=True) & 0xFFFF
        return found // TILE, (found + cell) % TILE

    for begin in range(parts, slots, CHUNK):
        tile, place = find(begin)
        code_ref[:, begin : begin + CHUNK] = tile * TILE + place
    for begin in range(0, parts, CHUNK):
        tile, place = find(begin)
        code_ref[:, begin : begin + CHUNK] = tile * TILE + place
        live = side_by_side(live_ref, 0, begin, CHUNK)
        state = part_ref[:, begin : begin + CHUNK] * live
        mixed, first = mix(closure, state.astype(jnp.bfloat16))
        added = dot(spread(mixed, first, place), ones(equal(tiles, tile)), NT)
        if begin == 0:
            sum_ref[...] = added
        else:
            sum_ref[...] += added


def pack_kernel(rows, sum_ref, code_ref, slot_ref, mark_ref, small_ref, *refs):
    state_refs, out_ref = refs[:4], refs[4]
    channels, tiles = state_refs[0].shape[0], slot_ref.shape[1]
    closure = small_ref[rows : 2 * rows, :channels]
    migr = state_refs[0].shape[1] - LANES
    code = code_ref[:, code_ref.shape[1] - 4 * migr :]
    state = jnp.concatenate([block[:, :migr] for block in arrived_blocks(state_refs)], axis=1)
    mixed, first = mix(closure, state)
    total = sum_ref[...] + dot(spread(mixed, first, code % TILE), ones(equal(tiles, code // TILE)), NT)
    table = jnp.concatenate([total.astype(jnp.bfloat16), mark_ref[...]], axis=0)
    match = one_hot(iota((out_ref.shape[0], tiles), 0) == slot_ref[...])
    out_ref[...] = dot(match, table, NT).astype(jnp.bfloat16)


def place_kernel(tile_ref, gas_ref, xa_ref, xb_ref):
    even = is_even("gx")
    count, lanes = tile_ref.shape
    width = gas_ref.shape[1] // 2
    marks = tile_ref[:, lanes - LANES :].astype(jnp.float32)
    column = marks[:, width % LANES : width % LANES + 1]
    height = marks[:, width % LANES + 1 : width % LANES + 2]
    lane = iota((1, LANES), 1)
    hot = one_hot(column == lane.astype(jnp.float32))
    place = (iota((1, width), 1) % TILE).astype(jnp.float32)
    values = tile_ref[:, :width].astype(jnp.float32)
    for half, mask in enumerate((place >= height, place < height)):
        total = dot(hot, jnp.where(mask, values, 0.0).astype(jnp.bfloat16), TN)
        where = slice(half * width, (half + 1) * width)
        gas_ref[:, where] = total[:COLS]
        rows = slice(half * FY, (half + 1) * FY)
        low, high = total[:FY], total[COLS - FY : COLS]
        xa_ref[rows, :] = jnp.where(even, high, low).astype(jnp.bfloat16)
        xb_ref[rows, :] = jnp.where(even, low, high).astype(jnp.bfloat16)


def unfold(ref):
    edge = ref[...].astype(jnp.float32)
    half = edge.shape[0] // 2
    return jnp.concatenate([edge[:half], edge[half:]], axis=1)


def along_kernel(gas_ref, xb_ref, xa_ref, out_ref, ya_ref, yb_ref):
    before, after = ordered(unfold(xa_ref), unfold(xb_ref), "gx")
    blocks = [before] + [gas_ref[x * FY : (x + 1) * FY, :] for x in range(FX)] + [after]
    along = [blocks[x] + 2.0 * blocks[x + 1] + blocks[x + 2] for x in range(FX)]
    for x in range(FX):
        out_ref[x * FY : (x + 1) * FY, :] = along[x]
    width = ya_ref.shape[1]
    edges = []
    for row in (0, FY - 1):
        edge = jnp.concatenate([along[x][row : row + 1] for x in range(FX)], axis=0)
        edges.append(jnp.concatenate([edge[:, :width], edge[:, width:]], axis=0))
    even = is_even("gy")
    ya_ref[...] = jnp.where(even, edges[1], edges[0]).astype(jnp.bfloat16)
    yb_ref[...] = jnp.where(even, edges[0], edges[1]).astype(jnp.bfloat16)


def drag_kernel(mark_ref, along_ref, yb_ref, ya_ref, drag_ref, back_ref):
    rows = drag_ref.shape[0]
    width = along_ref.shape[1] // 2
    lanes = rows * TILE
    before, after = ordered(unfold(ya_ref), unfold(yb_ref), "gy")
    smooth = []
    for x in range(FX):
        block = along_ref[x * FY : (x + 1) * FY, :]
        padded = jnp.concatenate([before[x : x + 1], block, after[x : x + 1]], axis=0)
        smooth.append((padded[0:FY] + 2.0 * block + padded[2 : FY + 2]) / 16.0)
    smooth = jnp.concatenate(smooth, axis=0)
    halves = []
    for half in range(2):
        base = half * width
        density = smooth[:, base + lanes : base + lanes + TILE]
        scale = 1.0 / (1.0 + density * density)
        halves.append(smooth[:, base : base + lanes] * jnp.concatenate([scale] * rows, axis=1))
    for r in range(rows):
        where = slice(r * TILE, (r + 1) * TILE)
        both = jnp.concatenate([halves[0][:, where], halves[1][:, where]], axis=1)
        drag_ref[r] = both.reshape(FX, FY, FZ).astype(jnp.bfloat16)
    mark = width % LANES
    marks = mark_ref[...].astype(jnp.float32)
    column, height = marks[:, mark : mark + 1], marks[:, mark + 1 : mark + 2]
    hot = one_hot(column == iota((1, COLS), 1).astype(jnp.float32))
    place = (iota((1, lanes), 1) % TILE).astype(jnp.float32)
    low = dot(hot, halves[0].astype(jnp.bfloat16))
    high = dot(hot, halves[1].astype(jnp.bfloat16))
    back_ref[...] = jnp.where(place >= height, low, high).astype(jnp.bfloat16)


def force_kernel(back_ref, slot_ref, code_ref, part_ref, small_ref, live_ref, drag_ref, *refs):
    state_refs, (out_hbm, drag_hbm, out_ref, table_ref, sems) = refs[:4], refs[4:]
    stores = [pltpu.make_async_copy(drag_ref, drag_hbm, sems.at[0])]
    stores[0].start()

    def store(where):
        stores.append(pltpu.make_async_copy(out_ref.at[:, where], out_hbm.at[:, where], sems.at[len(stores)]))
        stores[-1].start()

    rows, slots = out_ref.shape
    parts = part_ref.shape[1]
    tiles = slot_ref.shape[1]
    migr = (slots - parts) // 4
    match = one_hot(iota((back_ref.shape[0], tiles), 0) == slot_ref[...])
    table_ref[...] = dot(back_ref[...], match, TN).astype(jnp.bfloat16)
    channels = part_ref.shape[0]
    damping = small_ref[rows : 2 * rows, channels : channels + 1]

    def look(code):
        values = dot(table_ref[...], ones(equal(tiles, code // TILE))).astype(jnp.bfloat16)
        hit = equal(TILE, code % TILE)
        found = []
        for r in range(rows):
            picked = jnp.where(hit, values[r * TILE : (r + 1) * TILE], jnp.bfloat16(0))
            while picked.shape[0] > 16:
                half = picked.shape[0] // 2
                picked = picked[:half] + picked[half:]
            found.append(jnp.sum(picked.astype(jnp.float32), axis=0, keepdims=True))
        return jnp.concatenate(found, axis=0)

    for begin in range(0, parts, CHUNK):
        where = slice(begin, begin + CHUNK)
        live = side_by_side(live_ref, 0, begin, CHUNK)
        out_ref[:, where] = live * (look(code_ref[:, where]) - damping * part_ref[:rows, where])
        store(where)
    drag = look(code_ref[:, parts:])
    for row, arrived in enumerate(arrived_blocks(state_refs)):
        begin = parts + row * migr
        live = jnp.concatenate([arrived[k : k + 1, migr:] for k in range(migr // LANES)], axis=1)
        force = drag[:, row * migr : (row + 1) * migr] - damping * arrived[:rows, :migr]
        out_ref[:, begin : begin + migr] = live * force
    store(slice(parts, slots))
    for copy in stores:
        copy.wait()


def call(kernel, shapes, *operands, limit=None, late=(), scratch=()):
    vmem, hbm = pl.BlockSpec(memory_space=pltpu.VMEM), pl.BlockSpec(memory_space=pltpu.HBM)
    return pl.pallas_call(
        kernel,
        out_shape=shapes,
        in_specs=[hbm if limit else vmem] * len(operands),
        out_specs=[hbm if limit or i in late else vmem for i in range(len(shapes))],
        scratch_shapes=scratch,
        compiler_params=pltpu.CompilerParams(vmem_limit_bytes=limit or VMEM),
    )(*operands)


def per_device(
    particles,
    migrant_index,
    migrant_count,
    migrated_slot_cell,
    source_tile_size,
    tile_owner,
    tile_offset,
    closure,
    damping,
):
    f32, bf16, i32 = jnp.float32, jnp.bfloat16, jnp.int32
    shape = jax.ShapeDtypeStruct
    channels, parts = particles.shape
    rows = closure.shape[0]
    migr = migrant_index.shape[1]
    slots = migrated_slot_cell.shape[0]
    tiles = source_tile_size.shape[1]
    devices = lax.axis_size("gx") * lax.axis_size("gy")
    capacity = max(2, 2 * tiles // devices)
    count = devices * capacity
    width = (rows + 1) * TILE
    lanes = (width + LANES) // LANES * LANES
    small_count = small_rows(rows, 4 * migr, slots)[-1]
    operands = (
        particles, migrant_index, migrant_count, source_tile_size, tile_owner.reshape(1, tiles),
        tile_offset.reshape(1, tiles), closure, damping.reshape(1, rows), migrated_slot_cell.reshape(1, slots),
    )
    *leaving, small = call(
        pick_kernel,
        [shape((channels, migr + LANES), bf16)] * 4 + [shape((small_count, GROUP), f32)],
        *operands, limit=LARGE,
        scratch=[(pltpu.SMEM if i == 2 else pltpu.VMEM)(x.shape, x.dtype) for i, x in enumerate(operands)]
        + [pltpu.VMEM((4, channels, migr + LANES), bf16), pltpu.VMEM((small_count, GROUP), f32),
           pltpu.SemaphoreType.DMA((9,)), pltpu.SemaphoreType.DMA((5,))],
    )
    arrived = exchange(*leaving[:2], "gx") + exchange(*leaving[2:], "gy")
    sums, code, slot, marks, live = call(
        functools.partial(deposit_kernel, capacity, rows, 4 * migr),
        [shape((width, tiles), f32), shape((1, slots), i32), shape((1, tiles), i32),
         shape((lanes - width, tiles), bf16), shape((parts // GROUP, GROUP), f32)],
        particles, small, scratch=[pltpu.VMEM((2, tiles, LANES), jnp.int16)],
    )
    (payload,) = call(
        functools.partial(pack_kernel, rows), [shape((count, lanes), bf16)],
        sums, code, slot, marks, small, *arrived,
    )
    received = lax.all_to_all(
        payload.reshape(devices, capacity, lanes), ("gx", "gy"), split_axis=0, concat_axis=0, tiled=True
    ).reshape(count, lanes)
    grid, edge = shape((COLS, 2 * width), f32), shape((2 * FX, width), bf16)
    gas, xa, xb = call(place_kernel, [grid, edge, edge], received)
    xa, xb = exchange(xa, xb, "gx")
    along, ya, yb = call(along_kernel, [grid, edge, edge], gas, xb, xa)
    ya, yb = exchange(ya, yb, "gy")
    drag, back = call(
        drag_kernel,
        [shape((rows, FX, FY, FZ), bf16), shape((count, rows * TILE), bf16)],
        received[:, lanes - LANES :], along, yb, ya,
    )
    returned = lax.all_to_all(
        back.reshape(devices, capacity, rows * TILE), ("gx", "gy"), split_axis=0, concat_axis=0, tiled=True
    ).reshape(count, rows * TILE)
    force, drag = call(
        force_kernel, [shape((rows, slots), f32), shape(drag.shape, bf16)],
        returned, slot, code, particles, small, live, drag, *arrived, late=(0, 1),
        scratch=[pltpu.VMEM((rows, slots), f32), pltpu.VMEM((rows * TILE, tiles), bf16),
                 pltpu.SemaphoreType.DMA((2 + parts // CHUNK,))],
    )
    return drag, force


def solution(mesh):
    both = ("gx", "gy")
    in_specs = (
        P(None, both),
        P(both, None),
        P(both, None),
        P(both),
        P(both, None),
        P(both, None),
        P(both),
        P(),
        P(),
    )
    out_specs = (P(None, "gx", "gy", None), P(None, both))
    return jax.shard_map(
        per_device, mesh=mesh, in_specs=in_specs, out_specs=out_specs, check_vma=False
    )
```

```python
import functools

import jax
import jax.numpy as jnp
from jax import lax
from jax.experimental import pallas as pl
from jax.experimental.pallas import tpu as pltpu
from jax.sharding import PartitionSpec as P

TILE = 64
FX = 8
FY = 8
FZ = 128
COLS = FX * FY
LANES = 128
GROUP = 256
CHUNK = 2048
VMEM = 48 * 1024 * 1024
LARGE = 63 * 1024 * 1024

NT = (((1,), (1,)), ((), ()))
TN = (((0,), (0,)), ((), ()))


def iota(shape, dim):
    return lax.broadcasted_iota(jnp.int32, shape, dim)


def dot(a, b, dims=(((1,), (0,)), ((), ()))):
    return lax.dot_general(a, b, dims, preferred_element_type=jnp.float32)


def one_hot(mask):
    return jnp.where(mask, 1.0, 0.0).astype(jnp.bfloat16)


def equal(rows, row):
    numbers = iota((rows, row.shape[1]), 0).astype(jnp.float32).astype(jnp.bfloat16)
    return numbers == row.astype(jnp.float32).astype(jnp.bfloat16)


def ones(mask):
    return jnp.where(mask, jnp.bfloat16(1), jnp.bfloat16(0))


def fetch(sources, targets, sems):
    copies = [
        pltpu.make_async_copy(source, target, sems.at[i])
        for i, (source, target) in enumerate(zip(sources, targets))
    ]
    for copy in copies:
        copy.start()
    return copies


def is_even(axis):
    return lax.axis_index(axis) % 2 == 0


def exchange(block_a, block_b, axis):
    size = lax.axis_size(axis)
    blocks = {}
    for odd, block in ((1, block_b), (0, block_a)):
        pairs = [(i, (i + 1) % size if i % 2 == odd else (i - 1) % size) for i in range(size)]
        blocks[odd] = lax.ppermute(block, axis, pairs)
    return blocks[0], blocks[1]


def ordered(first, second, axis):
    even = is_even(axis)
    return jnp.where(even, second, first), jnp.where(even, first, second)


def leaving_row(index_ref, count_ref, parts):
    migr = index_ref.shape[1]
    lane = iota((1, migr), 1)
    odd = [jnp.where(is_even(axis), 0, 1) for axis in ("gx", "gy")]
    rows = []
    for row in (odd[0], 1 - odd[0], 2 + odd[1], 3 - odd[1]):
        rows.append(jnp.where(lane < count_ref[0, row], index_ref[pl.ds(row, 1), :], parts))
    return jnp.concatenate(rows, axis=1)


def arrived_blocks(refs):
    blocks = [ref[...].astype(jnp.float32) for ref in refs]
    return ordered(blocks[0], blocks[1], "gx") + ordered(blocks[2], blocks[3], "gy")


def small_rows(rows, leaving, slots):
    leave = 2 * rows
    cells = leave + leaving // GROUP
    return rows, leave, cells, cells + slots // GROUP


def pick_kernel(
    part_hbm, index_hbm, count_hbm, size_hbm, owner_hbm, offset_hbm, closure_hbm, damping_hbm, cell_hbm, *refs
):
    out_hbm, small_hbm, refs = refs[:4], refs[4], refs[5:]
    part_ref, index_ref, count_ref, size_ref, owner_ref, offset_ref = refs[:6]
    closure_ref, damping_ref, cell_ref, out_ref, small_ref, sems, out_sems = refs[6:]
    channels, parts = part_ref.shape
    migr = index_ref.shape[1]
    slots = cell_ref.shape[1]
    groups = parts // GROUP
    rows, width = closure_ref.shape
    closure_row, leave_row, cell_row, _ = small_rows(rows, 4 * migr, slots)
    copies = fetch(
        [index_hbm, count_hbm, part_hbm, size_hbm, owner_hbm, offset_hbm, closure_hbm, damping_hbm, cell_hbm],
        [index_ref, count_ref, part_ref, size_ref, owner_ref, offset_ref, closure_ref, damping_ref, cell_ref],
        sems,
    )
    copies[0].wait()
    copies[1].wait()
    leave = leaving_row(index_ref, count_ref, parts)
    high = leave // GROUP
    low = ones(equal(GROUP, leave % GROUP))
    for copy in copies[3:]:
        copy.wait()
    for row, ref in enumerate((size_ref, owner_ref, offset_ref)):
        small_ref[row : row + 1, :] = ref[...].astype(jnp.float32)
    small_ref[closure_row:leave_row, :width] = closure_ref[...]
    diagonal = iota((rows, rows), 0) == iota((rows, rows), 1)
    damping = jnp.sum(jnp.where(diagonal, damping_ref[...], 0.0), axis=1, keepdims=True)
    small_ref[closure_row:leave_row, width : width + 1] = damping
    for first, line in ((leave_row, leave), (cell_row, cell_ref[...])):
        for k in range(line.shape[1] // GROUP):
            part = line[:, k * GROUP : (k + 1) * GROUP]
            small_ref[first + k : first + k + 1, :] = part.astype(jnp.float32)
    stores = [pltpu.make_async_copy(small_ref, small_hbm, out_sems.at[4])]
    stores[0].start()
    copies[2].wait()
    table = jnp.concatenate(
        [part_ref[:, g * GROUP : (g + 1) * GROUP].astype(jnp.bfloat16) for g in range(groups)], axis=0
    )
    live = jnp.where(leave < parts, 1.0, 0.0)
    for r in range(4):
        where = slice(r * migr, (r + 1) * migr)
        found = dot(table, low[:, where])
        picked = jnp.zeros((channels, migr), jnp.float32)
        for g in range(groups):
            picked = jnp.where(high[:, where] == g, found[g * channels : (g + 1) * channels], picked)
        out_ref[r, :, :migr] = picked.astype(jnp.bfloat16)
        flags = [live[:, k : k + LANES] for k in range(r * migr, (r + 1) * migr, LANES)]
        flags.append(jnp.zeros((channels - len(flags), LANES), jnp.float32))
        out_ref[r, :, migr:] = jnp.concatenate(flags, axis=0).astype(jnp.bfloat16)
        stores.append(pltpu.make_async_copy(out_ref.at[r], out_hbm[r], out_sems.at[r]))
        stores[-1].start()
    for store in stores:
        store.wait()


def mix(closure, state):
    state = state.astype(jnp.float32)
    mixed = closure[:, 0:1] * state[0:1]
    for f in range(1, state.shape[0]):
        mixed = mixed + closure[:, f : f + 1] * state[f : f + 1]
    return mixed, state[0:1]


def side_by_side(ref, first, begin, width):
    lanes = ref.shape[1]
    first = first + begin // lanes
    rows = [ref[r : r + 1, :] for r in range(first, first + width // lanes)]
    return jnp.concatenate(rows, axis=1)


def spread(mixed, first, place):
    hit = equal(TILE, place)
    values = jnp.concatenate([mixed, first], axis=0).astype(jnp.bfloat16)
    return jnp.concatenate(
        [jnp.where(hit, values[r : r + 1], jnp.bfloat16(0)) for r in range(values.shape[0])], axis=0
    )


def deposit_kernel(
    capacity, rows, leaving, part_ref, small_ref, sum_ref, code_ref, slot_ref, mark_ref, live_ref
):
    channels, parts = part_ref.shape
    slots = code_ref.shape[1]
    tiles = slot_ref.shape[1]
    groups = parts // GROUP
    closure_row, leave_row, cell_row, _ = small_rows(rows, leaving, slots)
    closure = small_ref[closure_row:leave_row, :channels]

    leave = side_by_side(small_ref, leave_row, 0, leaving).astype(jnp.int32)
    halves = [leave[:, : leaving // 2], leave[:, leaving // 2 :]]
    high = jnp.concatenate([ones(equal(2 * groups, half // LANES)) for half in halves], axis=0)
    low = jnp.concatenate([ones(equal(LANES, half % LANES)) for half in halves], axis=0)
    hits = dot(high, low, NT)
    live_ref[...] = 1.0 - (hits[: 2 * groups, :LANES] + hits[2 * groups :, LANES:])

    sizes, owners, offset = [small_ref[r : r + 1, :] for r in range(3)]
    offset = offset.astype(jnp.int32)
    square = (tiles, tiles)
    below, across = iota(square, 0), iota(square, 1)
    inputs = [sizes, owners, (offset % FZ).astype(jnp.float32), jnp.zeros((5, tiles), jnp.float32)]
    inputs = jnp.concatenate(inputs, axis=0).astype(jnp.bfloat16)
    turned = dot(ones(below == across), inputs, NT)
    start = dot(ones(across < below), inputs, NT)[:, 0:1].astype(jnp.int32)
    height = turned[:, 2:3].astype(jnp.int32)
    code = iota((tiles, 1), 0) * TILE + (height - start) % TILE
    code_step = code - jnp.concatenate([jnp.zeros((1, 1), jnp.int32), code[: tiles - 1]], axis=0)
    earlier = ones((turned[:, 1:2] == owners) & (below < across))
    rank = dot(jnp.ones((8, tiles), jnp.bfloat16), earlier)[0:1]
    slot_ref[...] = (owners * capacity + rank).astype(jnp.int32)
    starts = jnp.broadcast_to(start.astype(jnp.int16), (tiles, CHUNK))
    steps = jnp.broadcast_to(code_step.astype(jnp.int16), (tiles, CHUNK))
    lines = iota(mark_ref.shape, 0)
    marks = jnp.where(lines == 0, offset // FZ, jnp.where(lines == 1, offset % FZ, 0))
    mark_ref[...] = marks.astype(jnp.float32).astype(jnp.bfloat16)

    def find(begin):
        cell = side_by_side(small_ref, cell_row, begin, CHUNK).astype(jnp.int32)
        found = jnp.where(cell.astype(jnp.int16) >= starts, steps, jnp.int16(0))
        while found.shape[0] > 16:
            half = found.shape[0] // 2
            found = found[:half] + found[half:]
        found = jnp.sum(found.astype(jnp.int32), axis=0, keepdims=True) & 0xFFFF
        return found // TILE, (found + cell) % TILE

    for begin in range(parts, slots, CHUNK):
        tile, place = find(begin)
        code_ref[:, begin : begin + CHUNK] = tile * TILE + place
    for begin in range(0, parts, CHUNK):
        tile, place = find(begin)
        code_ref[:, begin : begin + CHUNK] = tile * TILE + place
        live = side_by_side(live_ref, 0, begin, CHUNK)
        state = part_ref[:, begin : begin + CHUNK] * live
        mixed, first = mix(closure, state.astype(jnp.bfloat16))
        added = dot(spread(mixed, first, place), ones(equal(tiles, tile)), NT)
        total = added if begin == 0 else total + added
    sum_ref[...] = total


def pack_kernel(rows, sum_ref, code_ref, slot_ref, mark_ref, small_ref, *refs):
    state_refs, out_ref = refs[:4], refs[4]
    channels, tiles = state_refs[0].shape[0], slot_ref.shape[1]
    closure = small_ref[rows : 2 * rows, :channels]
    migr = state_refs[0].shape[1] - LANES
    code = code_ref[:, code_ref.shape[1] - 4 * migr :]
    state = jnp.concatenate([block[:, :migr] for block in arrived_blocks(state_refs)], axis=1)
    mixed, first = mix(closure, state)
    total = sum_ref[...] + dot(spread(mixed, first, code % TILE), ones(equal(tiles, code // TILE)), NT)
    table = jnp.concatenate([total.astype(jnp.bfloat16), mark_ref[...]], axis=0)
    match = one_hot(iota((out_ref.shape[0], tiles), 0) == slot_ref[...])
    out_ref[...] = dot(match, table, NT).astype(jnp.bfloat16)


def place_kernel(tile_ref, gas_ref, xa_ref, xb_ref):
    even = is_even("gx")
    count, lanes = tile_ref.shape
    width = gas_ref.shape[1] // 2
    marks = tile_ref[:, lanes - LANES :].astype(jnp.float32)
    column = marks[:, width % LANES : width % LANES + 1]
    height = marks[:, width % LANES + 1 : width % LANES + 2]
    lane = iota((1, LANES), 1)
    hot = one_hot(column == lane.astype(jnp.float32))
    place = (iota((1, width), 1) % TILE).astype(jnp.float32)
    values = tile_ref[:, :width].astype(jnp.float32)
    for half, mask in enumerate((place >= height, place < height)):
        total = dot(hot, jnp.where(mask, values, 0.0).astype(jnp.bfloat16), TN)
        where = slice(half * width, (half + 1) * width)
        gas_ref[:, where] = total[:COLS]
        rows = slice(half * FY, (half + 1) * FY)
        low, high = total[:FY], total[COLS - FY : COLS]
        xa_ref[rows, :] = jnp.where(even, high, low).astype(jnp.bfloat16)
        xb_ref[rows, :] = jnp.where(even, low, high).astype(jnp.bfloat16)


def unfold(ref):
    edge = ref[...].astype(jnp.float32)
    half = edge.shape[0] // 2
    return jnp.concatenate([edge[:half], edge[half:]], axis=1)


def along_kernel(gas_ref, xb_ref, xa_ref, out_ref, ya_ref, yb_ref):
    before, after = ordered(unfold(xa_ref), unfold(xb_ref), "gx")
    blocks = [before] + [gas_ref[x * FY : (x + 1) * FY, :] for x in range(FX)] + [after]
    along = [blocks[x] + 2.0 * blocks[x + 1] + blocks[x + 2] for x in range(FX)]
    for x in range(FX):
        out_ref[x * FY : (x + 1) * FY, :] = along[x]
    width = ya_ref.shape[1]
    edges = []
    for row in (0, FY - 1):
        edge = jnp.concatenate([along[x][row : row + 1] for x in range(FX)], axis=0)
        edges.append(jnp.concatenate([edge[:, :width], edge[:, width:]], axis=0))
    even = is_even("gy")
    ya_ref[...] = jnp.where(even, edges[1], edges[0]).astype(jnp.bfloat16)
    yb_ref[...] = jnp.where(even, edges[0], edges[1]).astype(jnp.bfloat16)


def drag_kernel(mark_ref, along_ref, yb_ref, ya_ref, drag_ref, back_ref):
    rows = drag_ref.shape[0]
    width = along_ref.shape[1] // 2
    lanes = rows * TILE
    before, after = ordered(unfold(ya_ref), unfold(yb_ref), "gy")
    smooth = []
    for x in range(FX):
        block = along_ref[x * FY : (x + 1) * FY, :]
        padded = jnp.concatenate([before[x : x + 1], block, after[x : x + 1]], axis=0)
        smooth.append((padded[0:FY] + 2.0 * block + padded[2 : FY + 2]) / 16.0)
    smooth = jnp.concatenate(smooth, axis=0)
    halves = []
    for half in range(2):
        base = half * width
        density = smooth[:, base + lanes : base + lanes + TILE]
        scale = 1.0 / (1.0 + density * density)
        halves.append(smooth[:, base : base + lanes] * jnp.concatenate([scale] * rows, axis=1))
    for r in range(rows):
        where = slice(r * TILE, (r + 1) * TILE)
        both = jnp.concatenate([halves[0][:, where], halves[1][:, where]], axis=1)
        drag_ref[r] = both.reshape(FX, FY, FZ).astype(jnp.bfloat16)
    mark = width % LANES
    marks = mark_ref[...].astype(jnp.float32)
    column, height = marks[:, mark : mark + 1], marks[:, mark + 1 : mark + 2]
    hot = one_hot(column == iota((1, COLS), 1).astype(jnp.float32))
    place = (iota((1, lanes), 1) % TILE).astype(jnp.float32)
    low = dot(hot, halves[0].astype(jnp.bfloat16))
    high = dot(hot, halves[1].astype(jnp.bfloat16))
    back_ref[...] = jnp.where(place >= height, low, high).astype(jnp.bfloat16)


def force_kernel(back_ref, slot_ref, code_ref, part_ref, small_ref, live_ref, drag_ref, *refs):
    state_refs, (out_hbm, drag_hbm, out_ref, table_ref, sems) = refs[:4], refs[4:]
    stores = [pltpu.make_async_copy(drag_ref, drag_hbm, sems.at[0])]
    stores[0].start()

    def store(where):
        stores.append(pltpu.make_async_copy(out_ref.at[:, where], out_hbm.at[:, where], sems.at[len(stores)]))
        stores[-1].start()

    rows, slots = out_ref.shape
    parts = part_ref.shape[1]
    tiles = slot_ref.shape[1]
    migr = (slots - parts) // 4
    match = one_hot(iota((back_ref.shape[0], tiles), 0) == slot_ref[...])
    table_ref[...] = dot(back_ref[...], match, TN).astype(jnp.bfloat16)
    channels = part_ref.shape[0]
    damping = small_ref[rows : 2 * rows, channels : channels + 1]

    def look(code):
        values = dot(table_ref[...], ones(equal(tiles, code // TILE))).astype(jnp.bfloat16)
        hit = equal(TILE, code % TILE)
        found = []
        for r in range(rows):
            picked = jnp.where(hit, values[r * TILE : (r + 1) * TILE], jnp.bfloat16(0))
            while picked.shape[0] > 16:
                half = picked.shape[0] // 2
                picked = picked[:half] + picked[half:]
            found.append(jnp.sum(picked.astype(jnp.float32), axis=0, keepdims=True))
        return jnp.concatenate(found, axis=0)

    for begin in range(0, parts, CHUNK):
        where = slice(begin, begin + CHUNK)
        live = side_by_side(live_ref, 0, begin, CHUNK)
        out_ref[:, where] = live * (look(code_ref[:, where]) - damping * part_ref[:rows, where])
        store(where)
    drag = look(code_ref[:, parts:])
    for row, arrived in enumerate(arrived_blocks(state_refs)):
        begin = parts + row * migr
        live = jnp.concatenate([arrived[k : k + 1, migr:] for k in range(migr // LANES)], axis=1)
        force = drag[:, row * migr : (row + 1) * migr] - damping * arrived[:rows, :migr]
        out_ref[:, begin : begin + migr] = live * force
    store(slice(parts, slots))
    for copy in stores:
        copy.wait()


def call(kernel, shapes, *operands, limit=None, late=(), scratch=()):
    vmem, hbm = pl.BlockSpec(memory_space=pltpu.VMEM), pl.BlockSpec(memory_space=pltpu.HBM)
    return pl.pallas_call(
        kernel,
        out_shape=shapes,
        in_specs=[hbm if limit else vmem] * len(operands),
        out_specs=[hbm if limit or i in late else vmem for i in range(len(shapes))],
        scratch_shapes=scratch,
        compiler_params=pltpu.CompilerParams(vmem_limit_bytes=limit or VMEM),
    )(*operands)


def per_device(
    particles,
    migrant_index,
    migrant_count,
    migrated_slot_cell,
    source_tile_size,
    tile_owner,
    tile_offset,
    closure,
    damping,
):
    f32, bf16, i32 = jnp.float32, jnp.bfloat16, jnp.int32
    shape = jax.ShapeDtypeStruct
    channels, parts = particles.shape
    rows = closure.shape[0]
    migr = migrant_index.shape[1]
    slots = migrated_slot_cell.shape[0]
    tiles = source_tile_size.shape[1]
    devices = lax.axis_size("gx") * lax.axis_size("gy")
    capacity = max(2, 2 * tiles // devices)
    count = devices * capacity
    width = (rows + 1) * TILE
    lanes = (width + LANES) // LANES * LANES
    small_count = small_rows(rows, 4 * migr, slots)[-1]
    operands = (
        particles, migrant_index, migrant_count, source_tile_size, tile_owner.reshape(1, tiles),
        tile_offset.reshape(1, tiles), closure, damping.reshape(1, rows), migrated_slot_cell.reshape(1, slots),
    )
    *leaving, small = call(
        pick_kernel,
        [shape((channels, migr + LANES), bf16)] * 4 + [shape((small_count, GROUP), f32)],
        *operands, limit=LARGE,
        scratch=[(pltpu.SMEM if i == 2 else pltpu.VMEM)(x.shape, x.dtype) for i, x in enumerate(operands)]
        + [pltpu.VMEM((4, channels, migr + LANES), bf16), pltpu.VMEM((small_count, GROUP), f32),
           pltpu.SemaphoreType.DMA((9,)), pltpu.SemaphoreType.DMA((5,))],
    )
    arrived = exchange(*leaving[:2], "gx") + exchange(*leaving[2:], "gy")
    sums, code, slot, marks, live = call(
        functools.partial(deposit_kernel, capacity, rows, 4 * migr),
        [shape((width, tiles), f32), shape((1, slots), i32), shape((1, tiles), i32),
         shape((lanes - width, tiles), bf16), shape((parts // LANES, LANES), f32)],
        particles, small,
    )
    (payload,) = call(
        functools.partial(pack_kernel, rows), [shape((count, lanes), bf16)],
        sums, code, slot, marks, small, *arrived,
    )
    received = lax.all_to_all(
        payload.reshape(devices, capacity, lanes), ("gx", "gy"), split_axis=0, concat_axis=0, tiled=True
    ).reshape(count, lanes)
    grid, edge = shape((COLS, 2 * width), f32), shape((2 * FX, width), bf16)
    gas, xa, xb = call(place_kernel, [grid, edge, edge], received)
    xa, xb = exchange(xa, xb, "gx")
    along, ya, yb = call(along_kernel, [grid, edge, edge], gas, xb, xa)
    ya, yb = exchange(ya, yb, "gy")
    drag, back = call(
        drag_kernel,
        [shape((rows, FX, FY, FZ), bf16), shape((count, rows * TILE), bf16)],
        received[:, lanes - LANES :], along, yb, ya,
    )
    returned = lax.all_to_all(
        back.reshape(devices, capacity, rows * TILE), ("gx", "gy"), split_axis=0, concat_axis=0, tiled=True
    ).reshape(count, rows * TILE)
    force, drag = call(
        force_kernel, [shape((rows, slots), f32), shape(drag.shape, bf16)],
        returned, slot, code, particles, small, live, drag, *arrived, late=(0, 1),
        scratch=[pltpu.VMEM((rows, slots), f32), pltpu.VMEM((rows * TILE, tiles), bf16),
                 pltpu.SemaphoreType.DMA((2 + parts // CHUNK,))],
    )
    return drag, force


def solution(mesh):
    both = ("gx", "gy")
    in_specs = (
        P(None, both),
        P(both, None),
        P(both, None),
        P(both),
        P(both, None),
        P(both, None),
        P(both),
        P(),
        P(),
    )
    out_specs = (P(None, "gx", "gy", None), P(None, both))
    return jax.shard_map(
        per_device, mesh=mesh, in_specs=in_specs, out_specs=out_specs, check_vma=False
    )
```

```python
import functools

import jax
import jax.numpy as jnp
from jax import lax
from jax.experimental import pallas as pl
from jax.experimental.pallas import tpu as pltpu
from jax.sharding import PartitionSpec as P

TILE = 64
FX = 8
FY = 8
FZ = 128
COLS = FX * FY
LANES = 128
GROUP = 256
CHUNK = 2048
VMEM = 48 * 1024 * 1024
LARGE = 63 * 1024 * 1024

NT = (((1,), (1,)), ((), ()))
TN = (((0,), (0,)), ((), ()))


def iota(shape, dim):
    return lax.broadcasted_iota(jnp.int32, shape, dim)


def dot(a, b, dims=(((1,), (0,)), ((), ()))):
    return lax.dot_general(a, b, dims, preferred_element_type=jnp.float32)


def one_hot(mask):
    return jnp.where(mask, 1.0, 0.0).astype(jnp.bfloat16)


def equal(rows, row):
    numbers = iota((rows, row.shape[1]), 0).astype(jnp.float32).astype(jnp.bfloat16)
    return numbers == row.astype(jnp.float32).astype(jnp.bfloat16)


def ones(mask):
    return jnp.where(mask, jnp.bfloat16(1), jnp.bfloat16(0))


def fetch(sources, targets, sems):
    copies = [
        pltpu.make_async_copy(source, target, sems.at[i])
        for i, (source, target) in enumerate(zip(sources, targets))
    ]
    for copy in copies:
        copy.start()
    return copies


def is_even(axis):
    return lax.axis_index(axis) % 2 == 0


def exchange(block_a, block_b, axis):
    size = lax.axis_size(axis)
    blocks = {}
    for odd, block in ((1, block_b), (0, block_a)):
        pairs = [(i, (i + 1) % size if i % 2 == odd else (i - 1) % size) for i in range(size)]
        blocks[odd] = lax.ppermute(block, axis, pairs)
    return blocks[0], blocks[1]


def ordered(first, second, axis):
    even = is_even(axis)
    return jnp.where(even, second, first), jnp.where(even, first, second)


def leaving_row(index_ref, count_ref, parts):
    migr = index_ref.shape[1]
    lane = iota((1, migr), 1)
    odd = [jnp.where(is_even(axis), 0, 1) for axis in ("gx", "gy")]
    rows = []
    for row in (odd[0], 1 - odd[0], 2 + odd[1], 3 - odd[1]):
        rows.append(jnp.where(lane < count_ref[0, row], index_ref[pl.ds(row, 1), :], parts))
    return jnp.concatenate(rows, axis=1)


def arrived_blocks(refs):
    yb, xb, ya, xa = [ref[...].astype(jnp.float32) for ref in refs]
    return ordered(xa, xb, "gx") + ordered(ya, yb, "gy")


def small_rows(rows, leaving, slots):
    leave = 2 * rows
    cells = leave + leaving // GROUP
    return rows, leave, cells, cells + slots // GROUP


def pick_kernel(
    part_hbm, index_hbm, count_hbm, size_hbm, owner_hbm, offset_hbm, closure_hbm, damping_hbm, cell_hbm, *refs
):
    out_hbm, small_hbm, refs = refs[:4], refs[4], refs[5:]
    part_ref, index_ref, count_ref, size_ref, owner_ref, offset_ref = refs[:6]
    closure_ref, damping_ref, cell_ref, out_ref, small_ref, sems, out_sems = refs[6:]
    channels, parts = part_ref.shape
    migr = index_ref.shape[1]
    slots = cell_ref.shape[1]
    groups = parts // GROUP
    rows, width = closure_ref.shape
    closure_row, leave_row, cell_row, _ = small_rows(rows, 4 * migr, slots)
    copies = fetch(
        [index_hbm, count_hbm, part_hbm, size_hbm, owner_hbm, offset_hbm, closure_hbm, damping_hbm, cell_hbm],
        [index_ref, count_ref, part_ref, size_ref, owner_ref, offset_ref, closure_ref, damping_ref, cell_ref],
        sems,
    )
    copies[0].wait()
    copies[1].wait()
    leave = leaving_row(index_ref, count_ref, parts)
    high = leave // GROUP
    low = ones(equal(GROUP, leave % GROUP))
    for copy in copies[3:]:
        copy.wait()
    for row, ref in enumerate((size_ref, owner_ref, offset_ref)):
        small_ref[row : row + 1, :] = ref[...].astype(jnp.float32)
    small_ref[closure_row:leave_row, :width] = closure_ref[...]
    diagonal = iota((rows, rows), 0) == iota((rows, rows), 1)
    damping = jnp.sum(jnp.where(diagonal, damping_ref[...], 0.0), axis=1, keepdims=True)
    small_ref[closure_row:leave_row, width : width + 1] = damping
    for first, line in ((leave_row, leave), (cell_row, cell_ref[...])):
        for k in range(line.shape[1] // GROUP):
            part = line[:, k * GROUP : (k + 1) * GROUP]
            small_ref[first + k : first + k + 1, :] = part.astype(jnp.float32)
    stores = [pltpu.make_async_copy(small_ref, small_hbm, out_sems.at[4])]
    stores[0].start()
    copies[2].wait()
    table = jnp.concatenate(
        [part_ref[:, g * GROUP : (g + 1) * GROUP].astype(jnp.bfloat16) for g in range(groups)], axis=0
    )
    live = jnp.where(leave < parts, 1.0, 0.0)
    for r in range(4):
        where = slice(r * migr, (r + 1) * migr)
        found = dot(table, low[:, where])
        picked = jnp.zeros((channels, migr), jnp.float32)
        for g in range(groups):
            picked = jnp.where(high[:, where] == g, found[g * channels : (g + 1) * channels], picked)
        out_ref[r, :, :migr] = picked.astype(jnp.bfloat16)
        flags = [live[:, k : k + LANES] for k in range(r * migr, (r + 1) * migr, LANES)]
        flags.append(jnp.zeros((channels - len(flags), LANES), jnp.float32))
        out_ref[r, :, migr:] = jnp.concatenate(flags, axis=0).astype(jnp.bfloat16)
        stores.append(pltpu.make_async_copy(out_ref.at[r], out_hbm[r], out_sems.at[r]))
        stores[-1].start()
    for store in stores:
        store.wait()


def mix(closure, state):
    state = state.astype(jnp.float32)
    mixed = closure[:, 0:1] * state[0:1]
    for f in range(1, state.shape[0]):
        mixed = mixed + closure[:, f : f + 1] * state[f : f + 1]
    return mixed, state[0:1]


def side_by_side(ref, first, begin, width):
    lanes = ref.shape[1]
    first = first + begin // lanes
    rows = [ref[r : r + 1, :] for r in range(first, first + width // lanes)]
    return jnp.concatenate(rows, axis=1)


def spread(mixed, first, place):
    hit = equal(TILE, place)
    values = jnp.concatenate([mixed, first], axis=0).astype(jnp.bfloat16)
    return jnp.concatenate(
        [jnp.where(hit, values[r : r + 1], jnp.bfloat16(0)) for r in range(values.shape[0])], axis=0
    )


def deposit_kernel(
    capacity, rows, leaving, part_ref, small_ref, sum_ref, code_ref, slot_ref, mark_ref, live_ref
):
    channels, parts = part_ref.shape
    slots = code_ref.shape[1]
    tiles = slot_ref.shape[1]
    groups = parts // GROUP
    closure_row, leave_row, cell_row, _ = small_rows(rows, leaving, slots)
    closure = small_ref[closure_row:leave_row, :channels]

    leave = side_by_side(small_ref, leave_row, 0, leaving).astype(jnp.int32)
    halves = [leave[:, : leaving // 2], leave[:, leaving // 2 :]]
    high = jnp.concatenate([ones(equal(2 * groups, half // LANES)) for half in halves], axis=0)
    low = jnp.concatenate([ones(equal(LANES, half % LANES)) for half in halves], axis=0)
    hits = dot(high, low, NT)
    live_ref[...] = 1.0 - (hits[: 2 * groups, :LANES] + hits[2 * groups :, LANES:])

    sizes, owners, offset = [small_ref[r : r + 1, :] for r in range(3)]
    offset = offset.astype(jnp.int32)
    square = (tiles, tiles)
    below, across = iota(square, 0), iota(square, 1)
    inputs = [sizes, owners, (offset % FZ).astype(jnp.float32), jnp.zeros((5, tiles), jnp.float32)]
    inputs = jnp.concatenate(inputs, axis=0).astype(jnp.bfloat16)
    turned = dot(ones(below == across), inputs, NT)
    start = dot(ones(across < below), inputs, NT)[:, 0:1].astype(jnp.int32)
    height = turned[:, 2:3].astype(jnp.int32)
    code = iota((tiles, 1), 0) * TILE + (height - start) % TILE
    code_step = code - jnp.concatenate([jnp.zeros((1, 1), jnp.int32), code[: tiles - 1]], axis=0)
    earlier = ones((turned[:, 1:2] == owners) & (below < across))
    rank = dot(jnp.ones((8, tiles), jnp.bfloat16), earlier)[0:1]
    slot_ref[...] = (owners * capacity + rank).astype(jnp.int32)
    starts = jnp.broadcast_to(start.astype(jnp.int16), (tiles, CHUNK))
    steps = jnp.broadcast_to(code_step.astype(jnp.int16), (tiles, CHUNK))
    lines = iota(mark_ref.shape, 0)
    marks = jnp.where(lines == 0, offset // FZ, jnp.where(lines == 1, offset % FZ, 0))
    mark_ref[...] = marks.astype(jnp.float32).astype(jnp.bfloat16)

    def find(begin):
        cell = side_by_side(small_ref, cell_row, begin, CHUNK).astype(jnp.int32)
        found = jnp.where(cell.astype(jnp.int16) >= starts, steps, jnp.int16(0))
        while found.shape[0] > 16:
            half = found.shape[0] // 2
            found = found[:half] + found[half:]
        found = jnp.sum(found.astype(jnp.int32), axis=0, keepdims=True) & 0xFFFF
        return found // TILE, (found + cell) % TILE

    for begin in range(parts, slots, CHUNK):
        tile, place = find(begin)
        code_ref[:, begin : begin + CHUNK] = tile * TILE + place
    for begin in range(0, parts, CHUNK):
        tile, place = find(begin)
        code_ref[:, begin : begin + CHUNK] = tile * TILE + place
        live = side_by_side(live_ref, 0, begin, CHUNK)
        state = part_ref[:, begin : begin + CHUNK] * live
        mixed, first = mix(closure, state.astype(jnp.bfloat16))
        added = dot(spread(mixed, first, place), ones(equal(tiles, tile)), NT)
        total = added if begin == 0 else total + added
    sum_ref[...] = total


def pack_kernel(rows, sum_ref, code_ref, slot_ref, mark_ref, small_ref, *refs):
    state_refs, out_ref = refs[:4], refs[4]
    channels, tiles = state_refs[0].shape[0], slot_ref.shape[1]
    closure = small_ref[rows : 2 * rows, :channels]
    migr = state_refs[0].shape[1] - LANES
    code = code_ref[:, code_ref.shape[1] - 4 * migr :]
    state = jnp.concatenate([block[:, :migr] for block in arrived_blocks(state_refs)], axis=1)
    mixed, first = mix(closure, state)
    total = sum_ref[...] + dot(spread(mixed, first, code % TILE), ones(equal(tiles, code // TILE)), NT)
    table = jnp.concatenate([total.astype(jnp.bfloat16), mark_ref[...]], axis=0)
    match = one_hot(iota((out_ref.shape[0], tiles), 0) == slot_ref[...])
    out_ref[...] = dot(match, table, NT).astype(jnp.bfloat16)


def place_kernel(tile_ref, gas_ref, xa_ref, xb_ref):
    even = is_even("gx")
    count, lanes = tile_ref.shape
    width = gas_ref.shape[1] // 2
    marks = tile_ref[:, lanes - LANES :].astype(jnp.float32)
    column = marks[:, width % LANES : width % LANES + 1]
    height = marks[:, width % LANES + 1 : width % LANES + 2]
    lane = iota((1, LANES), 1)
    hot = one_hot(column == lane.astype(jnp.float32))
    place = (iota((1, width), 1) % TILE).astype(jnp.float32)
    values = tile_ref[:, :width].astype(jnp.float32)
    for half, mask in enumerate((place >= height, place < height)):
        total = dot(hot, jnp.where(mask, values, 0.0).astype(jnp.bfloat16), TN)
        where = slice(half * width, (half + 1) * width)
        gas_ref[:, where] = total[:COLS]
        rows = slice(half * FY, (half + 1) * FY)
        low, high = total[:FY], total[COLS - FY : COLS]
        xa_ref[rows, :] = jnp.where(even, high, low).astype(jnp.bfloat16)
        xb_ref[rows, :] = jnp.where(even, low, high).astype(jnp.bfloat16)


def unfold(ref):
    edge = ref[...].astype(jnp.float32)
    half = edge.shape[0] // 2
    return jnp.concatenate([edge[:half], edge[half:]], axis=1)


def along_kernel(gas_ref, xb_ref, xa_ref, out_ref, ya_ref, yb_ref):
    before, after = ordered(unfold(xa_ref), unfold(xb_ref), "gx")
    blocks = [before] + [gas_ref[x * FY : (x + 1) * FY, :] for x in range(FX)] + [after]
    along = [blocks[x] + 2.0 * blocks[x + 1] + blocks[x + 2] for x in range(FX)]
    for x in range(FX):
        out_ref[x * FY : (x + 1) * FY, :] = along[x]
    width = ya_ref.shape[1]
    edges = []
    for row in (0, FY - 1):
        edge = jnp.concatenate([along[x][row : row + 1] for x in range(FX)], axis=0)
        edges.append(jnp.concatenate([edge[:, :width], edge[:, width:]], axis=0))
    even = is_even("gy")
    ya_ref[...] = jnp.where(even, edges[1], edges[0]).astype(jnp.bfloat16)
    yb_ref[...] = jnp.where(even, edges[0], edges[1]).astype(jnp.bfloat16)


def drag_kernel(mark_ref, along_ref, yb_ref, ya_ref, drag_ref, back_ref):
    rows = drag_ref.shape[0]
    width = along_ref.shape[1] // 2
    lanes = rows * TILE
    before, after = ordered(unfold(ya_ref), unfold(yb_ref), "gy")
    smooth = []
    for x in range(FX):
        block = along_ref[x * FY : (x + 1) * FY, :]
        padded = jnp.concatenate([before[x : x + 1], block, after[x : x + 1]], axis=0)
        smooth.append((padded[0:FY] + 2.0 * block + padded[2 : FY + 2]) / 16.0)
    smooth = jnp.concatenate(smooth, axis=0)
    halves = []
    for half in range(2):
        base = half * width
        density = smooth[:, base + lanes : base + lanes + TILE]
        scale = 1.0 / (1.0 + density * density)
        halves.append(smooth[:, base : base + lanes] * jnp.concatenate([scale] * rows, axis=1))
    for r in range(rows):
        where = slice(r * TILE, (r + 1) * TILE)
        both = jnp.concatenate([halves[0][:, where], halves[1][:, where]], axis=1)
        drag_ref[r] = both.reshape(FX, FY, FZ).astype(jnp.bfloat16)
    mark = width % LANES
    marks = mark_ref[...].astype(jnp.float32)
    column, height = marks[:, mark : mark + 1], marks[:, mark + 1 : mark + 2]
    hot = one_hot(column == iota((1, COLS), 1).astype(jnp.float32))
    place = (iota((1, lanes), 1) % TILE).astype(jnp.float32)
    low = dot(hot, halves[0].astype(jnp.bfloat16))
    high = dot(hot, halves[1].astype(jnp.bfloat16))
    back_ref[...] = jnp.where(place >= height, low, high).astype(jnp.bfloat16)


def force_kernel(back_ref, slot_ref, code_ref, part_ref, small_ref, live_ref, drag_ref, *refs):
    state_refs, (out_hbm, drag_hbm, out_ref, table_ref, sems) = refs[:4], refs[4:]
    stores = [pltpu.make_async_copy(drag_ref, drag_hbm, sems.at[0])]
    stores[0].start()

    def store(where):
        stores.append(pltpu.make_async_copy(out_ref.at[:, where], out_hbm.at[:, where], sems.at[len(stores)]))
        stores[-1].start()

    rows, slots = out_ref.shape
    parts = part_ref.shape[1]
    tiles = slot_ref.shape[1]
    migr = (slots - parts) // 4
    match = one_hot(iota((back_ref.shape[0], tiles), 0) == slot_ref[...])
    table_ref[...] = dot(back_ref[...], match, TN).astype(jnp.bfloat16)
    channels = part_ref.shape[0]
    damping = small_ref[rows : 2 * rows, channels : channels + 1]

    def look(code):
        values = dot(table_ref[...], ones(equal(tiles, code // TILE))).astype(jnp.bfloat16)
        hit = equal(TILE, code % TILE)
        found = []
        for r in range(rows):
            picked = jnp.where(hit, values[r * TILE : (r + 1) * TILE], jnp.bfloat16(0))
            while picked.shape[0] > 16:
                half = picked.shape[0] // 2
                picked = picked[:half] + picked[half:]
            found.append(jnp.sum(picked.astype(jnp.float32), axis=0, keepdims=True))
        return jnp.concatenate(found, axis=0)

    for begin in range(0, parts, CHUNK):
        where = slice(begin, begin + CHUNK)
        live = side_by_side(live_ref, 0, begin, CHUNK)
        out_ref[:, where] = live * (look(code_ref[:, where]) - damping * part_ref[:rows, where])
        store(where)
    drag = look(code_ref[:, parts:])
    for row, arrived in enumerate(arrived_blocks(state_refs)):
        begin = parts + row * migr
        live = jnp.concatenate([arrived[k : k + 1, migr:] for k in range(migr // LANES)], axis=1)
        force = drag[:, row * migr : (row + 1) * migr] - damping * arrived[:rows, :migr]
        out_ref[:, begin : begin + migr] = live * force
    store(slice(parts, slots))
    for copy in stores:
        copy.wait()


def call(kernel, shapes, *operands, limit=None, late=(), scratch=()):
    vmem, hbm = pl.BlockSpec(memory_space=pltpu.VMEM), pl.BlockSpec(memory_space=pltpu.HBM)
    return pl.pallas_call(
        kernel,
        out_shape=shapes,
        in_specs=[hbm if limit else vmem] * len(operands),
        out_specs=[hbm if limit or i in late else vmem for i in range(len(shapes))],
        scratch_shapes=scratch,
        compiler_params=pltpu.CompilerParams(vmem_limit_bytes=limit or VMEM),
    )(*operands)


def per_device(
    particles,
    migrant_index,
    migrant_count,
    migrated_slot_cell,
    source_tile_size,
    tile_owner,
    tile_offset,
    closure,
    damping,
):
    f32, bf16, i32 = jnp.float32, jnp.bfloat16, jnp.int32
    shape = jax.ShapeDtypeStruct
    channels, parts = particles.shape
    rows = closure.shape[0]
    migr = migrant_index.shape[1]
    slots = migrated_slot_cell.shape[0]
    tiles = source_tile_size.shape[1]
    devices = lax.axis_size("gx") * lax.axis_size("gy")
    capacity = max(2, 2 * tiles // devices)
    count = devices * capacity
    width = (rows + 1) * TILE
    lanes = (width + LANES) // LANES * LANES
    small_count = small_rows(rows, 4 * migr, slots)[-1]
    operands = (
        particles, migrant_index, migrant_count, source_tile_size, tile_owner.reshape(1, tiles),
        tile_offset.reshape(1, tiles), closure, damping.reshape(1, rows), migrated_slot_cell.reshape(1, slots),
    )
    *leaving, small = call(
        pick_kernel,
        [shape((channels, migr + LANES), bf16)] * 4 + [shape((small_count, GROUP), f32)],
        *operands, limit=LARGE,
        scratch=[(pltpu.SMEM if i == 2 else pltpu.VMEM)(x.shape, x.dtype) for i, x in enumerate(operands)]
        + [pltpu.VMEM((4, channels, migr + LANES), bf16), pltpu.VMEM((small_count, GROUP), f32),
           pltpu.SemaphoreType.DMA((9,)), pltpu.SemaphoreType.DMA((5,))],
    )
    (xa, xb), (ya, yb) = exchange(*leaving[:2], "gx"), exchange(*leaving[2:], "gy")
    arrived = yb, xb, ya, xa
    sums, code, slot, marks, live = call(
        functools.partial(deposit_kernel, capacity, rows, 4 * migr),
        [shape((width, tiles), f32), shape((1, slots), i32), shape((1, tiles), i32),
         shape((lanes - width, tiles), bf16), shape((parts // LANES, LANES), f32)],
        particles, small,
    )
    (payload,) = call(
        functools.partial(pack_kernel, rows), [shape((count, lanes), bf16)],
        sums, code, slot, marks, small, *arrived,
    )
    received = lax.all_to_all(
        payload.reshape(devices, capacity, lanes), ("gx", "gy"), split_axis=0, concat_axis=0, tiled=True
    ).reshape(count, lanes)
    grid, edge = shape((COLS, 2 * width), f32), shape((2 * FX, width), bf16)
    gas, xa, xb = call(place_kernel, [grid, edge, edge], received)
    xa, xb = exchange(xa, xb, "gx")
    along, ya, yb = call(along_kernel, [grid, edge, edge], gas, xb, xa)
    ya, yb = exchange(ya, yb, "gy")
    drag, back = call(
        drag_kernel,
        [shape((rows, FX, FY, FZ), bf16), shape((count, rows * TILE), bf16)],
        received[:, lanes - LANES :], along, yb, ya,
    )
    returned = lax.all_to_all(
        back.reshape(devices, capacity, rows * TILE), ("gx", "gy"), split_axis=0, concat_axis=0, tiled=True
    ).reshape(count, rows * TILE)
    force, drag = call(
        force_kernel, [shape((rows, slots), f32), shape(drag.shape, bf16)],
        returned, slot, code, particles, small, live, drag, *arrived, late=(0, 1),
        scratch=[pltpu.VMEM((rows, slots), f32), pltpu.VMEM((rows * TILE, tiles), bf16),
                 pltpu.SemaphoreType.DMA((2 + parts // CHUNK,))],
    )
    return drag, force


def solution(mesh):
    both = ("gx", "gy")
    in_specs = (
        P(None, both),
        P(both, None),
        P(both, None),
        P(both),
        P(both, None),
        P(both, None),
        P(both),
        P(),
        P(),
    )
    out_specs = (P(None, "gx", "gy", None), P(None, both))
    return jax.shard_map(
        per_device, mesh=mesh, in_specs=in_specs, out_specs=out_specs, check_vma=False
    )
```

```python
import functools

import jax
import jax.numpy as jnp
from jax import lax
from jax.experimental import pallas as pl
from jax.experimental.pallas import tpu as pltpu
from jax.sharding import PartitionSpec as P

TILE = 64
FX = 8
FY = 8
FZ = 128
COLS = FX * FY
LANES = 128
GROUP = 256
CHUNK = 2048
VMEM = 48 * 1024 * 1024
LARGE = 63 * 1024 * 1024

NT = (((1,), (1,)), ((), ()))
TN = (((0,), (0,)), ((), ()))


def iota(shape, dim):
    return lax.broadcasted_iota(jnp.int32, shape, dim)


def dot(a, b, dims=(((1,), (0,)), ((), ()))):
    return lax.dot_general(a, b, dims, preferred_element_type=jnp.float32)


def one_hot(mask):
    return jnp.where(mask, 1.0, 0.0).astype(jnp.bfloat16)


def equal(rows, row):
    numbers = iota((rows, row.shape[1]), 0).astype(jnp.float32).astype(jnp.bfloat16)
    return numbers == row.astype(jnp.float32).astype(jnp.bfloat16)


def ones(mask):
    return jnp.where(mask, jnp.bfloat16(1), jnp.bfloat16(0))


def fetch(sources, targets, sems):
    copies = [
        pltpu.make_async_copy(source, target, sems.at[i])
        for i, (source, target) in enumerate(zip(sources, targets))
    ]
    for copy in copies:
        copy.start()
    return copies


def is_even(axis):
    return lax.axis_index(axis) % 2 == 0


def exchange(block_a, block_b, axis):
    size = lax.axis_size(axis)
    blocks = {}
    for odd, block in ((1, block_b), (0, block_a)):
        pairs = [(i, (i + 1) % size if i % 2 == odd else (i - 1) % size) for i in range(size)]
        blocks[odd] = lax.ppermute(block, axis, pairs)
    return blocks[0], blocks[1]


def ordered(first, second, axis):
    even = is_even(axis)
    return jnp.where(even, second, first), jnp.where(even, first, second)


def leaving_row(index_ref, count_ref, parts):
    migr = index_ref.shape[1]
    lane = iota((1, migr), 1)
    odd = [jnp.where(is_even(axis), 0, 1) for axis in ("gx", "gy")]
    rows = []
    for row in (odd[0], 1 - odd[0], 2 + odd[1], 3 - odd[1]):
        rows.append(jnp.where(lane < count_ref[0, row], index_ref[pl.ds(row, 1), :], parts))
    return jnp.concatenate(rows, axis=1)


def arrived_blocks(refs):
    yb, xb, ya, xa = [ref[...].astype(jnp.float32) for ref in refs]
    return ordered(xa, xb, "gx") + ordered(ya, yb, "gy")


def small_rows(rows, leaving, slots):
    leave = 2 * rows
    cells = leave + leaving // GROUP
    return rows, leave, cells, cells + slots // GROUP


def pick_kernel(
    part_hbm, index_hbm, count_hbm, size_hbm, owner_hbm, offset_hbm, closure_hbm, damping_hbm, cell_hbm, *refs
):
    out_hbm, small_hbm, refs = refs[:4], refs[4], refs[5:]
    part_ref, index_ref, count_ref, size_ref, owner_ref, offset_ref = refs[:6]
    closure_ref, damping_ref, cell_ref, out_ref, small_ref, sems, out_sems = refs[6:]
    channels, parts = part_ref.shape
    migr = index_ref.shape[1]
    slots = cell_ref.shape[1]
    groups = parts // GROUP
    rows, width = closure_ref.shape
    closure_row, leave_row, cell_row, _ = small_rows(rows, 4 * migr, slots)
    copies = fetch(
        [index_hbm, count_hbm, part_hbm, size_hbm, owner_hbm, offset_hbm, closure_hbm, damping_hbm, cell_hbm],
        [index_ref, count_ref, part_ref, size_ref, owner_ref, offset_ref, closure_ref, damping_ref, cell_ref],
        sems,
    )
    copies[0].wait()
    copies[1].wait()
    leave = leaving_row(index_ref, count_ref, parts)
    high = leave // GROUP
    low = ones(equal(GROUP, leave % GROUP))
    for copy in copies[3:]:
        copy.wait()
    for row, ref in enumerate((size_ref, owner_ref, offset_ref)):
        small_ref[row : row + 1, :] = ref[...].astype(jnp.float32)
    small_ref[closure_row:leave_row, :width] = closure_ref[...]
    diagonal = iota((rows, rows), 0) == iota((rows, rows), 1)
    damping = jnp.sum(jnp.where(diagonal, damping_ref[...], 0.0), axis=1, keepdims=True)
    small_ref[closure_row:leave_row, width : width + 1] = damping
    for first, line in ((leave_row, leave), (cell_row, cell_ref[...])):
        for k in range(line.shape[1] // GROUP):
            part = line[:, k * GROUP : (k + 1) * GROUP]
            small_ref[first + k : first + k + 1, :] = part.astype(jnp.float32)
    stores = [pltpu.make_async_copy(small_ref, small_hbm, out_sems.at[4])]
    stores[0].start()
    copies[2].wait()
    table = jnp.concatenate(
        [part_ref[:, g * GROUP : (g + 1) * GROUP].astype(jnp.bfloat16) for g in range(groups)], axis=0
    )
    live = jnp.where(leave < parts, 1.0, 0.0)
    for r in range(4):
        where = slice(r * migr, (r + 1) * migr)
        found = dot(table, low[:, where])
        picked = jnp.zeros((channels, migr), jnp.float32)
        for g in range(groups):
            picked = jnp.where(high[:, where] == g, found[g * channels : (g + 1) * channels], picked)
        out_ref[r, :, :migr] = picked.astype(jnp.bfloat16)
        flags = [live[:, k : k + LANES] for k in range(r * migr, (r + 1) * migr, LANES)]
        flags.append(jnp.zeros((channels - len(flags), LANES), jnp.float32))
        out_ref[r, :, migr:] = jnp.concatenate(flags, axis=0).astype(jnp.bfloat16)
        stores.append(pltpu.make_async_copy(out_ref.at[r], out_hbm[r], out_sems.at[r]))
        stores[-1].start()
    for store in stores:
        store.wait()


def mix(closure, state):
    state = state.astype(jnp.float32)
    mixed = closure[:, 0:1] * state[0:1]
    for f in range(1, state.shape[0]):
        mixed = mixed + closure[:, f : f + 1] * state[f : f + 1]
    return mixed, state[0:1]


def side_by_side(ref, first, begin, width):
    lanes = ref.shape[1]
    first = first + begin // lanes
    rows = [ref[r : r + 1, :] for r in range(first, first + width // lanes)]
    return jnp.concatenate(rows, axis=1)


def spread(mixed, first, place):
    hit = equal(TILE, place)
    values = jnp.concatenate([mixed, first], axis=0).astype(jnp.bfloat16)
    return jnp.concatenate(
        [jnp.where(hit, values[r : r + 1], jnp.bfloat16(0)) for r in range(values.shape[0])], axis=0
    )


def deposit_kernel(
    capacity, rows, leaving, part_ref, small_ref, sum_ref, code_ref, slot_ref, mark_ref, live_ref
):
    channels, parts = part_ref.shape
    slots = code_ref.shape[1]
    tiles = slot_ref.shape[1]
    groups = parts // GROUP
    closure_row, leave_row, cell_row, _ = small_rows(rows, leaving, slots)
    closure = small_ref[closure_row:leave_row, :channels]

    leave = side_by_side(small_ref, leave_row, 0, leaving).astype(jnp.int32)
    halves = [leave[:, : leaving // 2], leave[:, leaving // 2 :]]
    high = jnp.concatenate([ones(equal(2 * groups, half // LANES)) for half in halves], axis=0)
    low = jnp.concatenate([ones(equal(LANES, half % LANES)) for half in halves], axis=0)
    hits = dot(high, low, NT)
    live_ref[...] = 1.0 - (hits[: 2 * groups, :LANES] + hits[2 * groups :, LANES:])

    sizes, owners, offset = [small_ref[r : r + 1, :] for r in range(3)]
    offset = offset.astype(jnp.int32)
    square = (tiles, tiles)
    below, across = iota(square, 0), iota(square, 1)
    inputs = [sizes, owners, (offset % FZ).astype(jnp.float32), jnp.zeros((5, tiles), jnp.float32)]
    inputs = jnp.concatenate(inputs, axis=0).astype(jnp.bfloat16)
    turned = dot(ones(below == across), inputs, NT)
    start = dot(ones(across < below), inputs, NT)[:, 0:1].astype(jnp.int32)
    height = turned[:, 2:3].astype(jnp.int32)
    code = iota((tiles, 1), 0) * TILE + (height - start) % TILE
    code_step = code - jnp.concatenate([jnp.zeros((1, 1), jnp.int32), code[: tiles - 1]], axis=0)
    earlier = ones((turned[:, 1:2] == owners) & (below < across))
    rank = dot(jnp.ones((8, tiles), jnp.bfloat16), earlier)[0:1]
    slot_ref[...] = (owners * capacity + rank).astype(jnp.int32)
    starts = jnp.broadcast_to(start.astype(jnp.int16), (tiles, CHUNK))
    steps = jnp.broadcast_to(code_step.astype(jnp.int16), (tiles, CHUNK))
    lines = iota(mark_ref.shape, 0)
    marks = jnp.where(lines == 0, offset // FZ, jnp.where(lines == 1, offset % FZ, 0))
    mark_ref[...] = marks.astype(jnp.float32).astype(jnp.bfloat16)

    def find(begin):
        cell = side_by_side(small_ref, cell_row, begin, CHUNK).astype(jnp.int32)
        found = jnp.where(cell.astype(jnp.int16) >= starts, steps, jnp.int16(0))
        while found.shape[0] > 16:
            half = found.shape[0] // 2
            found = found[:half] + found[half:]
        found = jnp.sum(found.astype(jnp.int32), axis=0, keepdims=True) & 0xFFFF
        return found // TILE, (found + cell) % TILE

    for begin in range(parts, slots, CHUNK):
        tile, place = find(begin)
        code_ref[:, begin : begin + CHUNK] = tile * TILE + place
    for begin in range(0, parts, CHUNK):
        tile, place = find(begin)
        code_ref[:, begin : begin + CHUNK] = tile * TILE + place
        live = side_by_side(live_ref, 0, begin, CHUNK)
        state = part_ref[:, begin : begin + CHUNK] * live
        mixed, first = mix(closure, state.astype(jnp.bfloat16))
        added = dot(spread(mixed, first, place), ones(equal(tiles, tile)), NT)
        total = added if begin == 0 else total + added
    sum_ref[...] = total


def pack_kernel(rows, sum_ref, code_ref, slot_ref, mark_ref, small_ref, *refs):
    state_refs, out_ref = refs[:4], refs[4]
    channels, tiles = state_refs[0].shape[0], slot_ref.shape[1]
    closure = small_ref[rows : 2 * rows, :channels]
    migr = state_refs[0].shape[1] - LANES
    code = code_ref[:, code_ref.shape[1] - 4 * migr :]
    state = jnp.concatenate([block[:, :migr] for block in arrived_blocks(state_refs)], axis=1)
    mixed, first = mix(closure, state)
    total = sum_ref[...] + dot(spread(mixed, first, code % TILE), ones(equal(tiles, code // TILE)), NT)
    table = jnp.concatenate([total.astype(jnp.bfloat16), mark_ref[...]], axis=0)
    match = one_hot(iota((out_ref.shape[0], tiles), 0) == slot_ref[...])
    out_ref[...] = dot(match, table, NT).astype(jnp.bfloat16)


def place_kernel(tile_ref, gas_ref, xa_ref, xb_ref, ya_ref, yb_ref):
    x_even, y_even = is_even("gx"), is_even("gy")
    count, lanes = tile_ref.shape
    width = gas_ref.shape[1] // 2
    marks = tile_ref[:, lanes - LANES :].astype(jnp.float32)
    column = marks[:, width % LANES : width % LANES + 1]
    height = marks[:, width % LANES + 1 : width % LANES + 2]
    lane = iota((1, LANES), 1)
    edge = jnp.where(lane < COLS + FX, (lane - COLS) * FY, (lane - COLS - FX) * FY + FY - 1)
    target = jnp.where(lane < COLS, lane, jnp.where(lane < COLS + 2 * FX, edge, -1))
    hot = one_hot(column == target.astype(jnp.float32))
    place = (iota((1, width), 1) % TILE).astype(jnp.float32)
    values = tile_ref[:, :width].astype(jnp.float32)
    for half, mask in enumerate((place >= height, place < height)):
        total = dot(hot, jnp.where(mask, values, 0.0).astype(jnp.bfloat16), TN)
        where = slice(half * width, (half + 1) * width)
        gas_ref[:, where] = total[:COLS]
        rows = slice(half * FY, (half + 1) * FY)
        low, high = total[:FY], total[COLS - FY : COLS]
        xa_ref[rows, :] = jnp.where(x_even, high, low).astype(jnp.bfloat16)
        xb_ref[rows, :] = jnp.where(x_even, low, high).astype(jnp.bfloat16)
        low, high = total[COLS : COLS + FX], total[COLS + FX : COLS + 2 * FX]
        ya_ref[rows, :] = jnp.where(y_even, high, low).astype(jnp.bfloat16)
        yb_ref[rows, :] = jnp.where(y_even, low, high).astype(jnp.bfloat16)


def unfold(ref):
    edge = ref[...].astype(jnp.float32)
    half = edge.shape[0] // 2
    return jnp.concatenate([edge[:half], edge[half:]], axis=1)


def corner_kernel(yb_ref, ya_ref, ca_ref, cb_ref):
    even = is_even("gx")
    sides = ordered(ya_ref[...].astype(jnp.float32), yb_ref[...].astype(jnp.float32), "gy")
    rest = jnp.zeros((ca_ref.shape[0] - 4, ca_ref.shape[1]), jnp.float32)
    low = jnp.concatenate([side[r : r + 1] for side in sides for r in (0, FX)] + [rest], axis=0)
    high = jnp.concatenate([side[r : r + 1] for side in sides for r in (FX - 1, 2 * FX - 1)] + [rest], axis=0)
    ca_ref[...] = jnp.where(even, high, low).astype(jnp.bfloat16)
    cb_ref[...] = jnp.where(even, low, high).astype(jnp.bfloat16)


def drag_kernel(
    mark_ref, gas_ref, yb_ref, ya_ref, xb_ref, xa_ref, cb_ref, ca_ref, drag_ref, back_ref
):
    rows = drag_ref.shape[0]
    width = gas_ref.shape[1] // 2
    lanes = rows * TILE

    def along(padded):
        return padded[0:FX] + 2.0 * padded[1 : FX + 1] + padded[2 : FX + 2]

    corners = ordered(ca_ref[...].astype(jnp.float32), cb_ref[...].astype(jnp.float32), "gx")
    edges = []
    for side, block in enumerate(ordered(unfold(ya_ref), unfold(yb_ref), "gy")):
        first, last = [
            jnp.concatenate([c[2 * side : 2 * side + 1], c[2 * side + 1 : 2 * side + 2]], axis=1) for c in corners
        ]
        edges.append(along(jnp.concatenate([first, block, last], axis=0)))
    before, after = edges
    first, last = ordered(unfold(xa_ref), unfold(xb_ref), "gx")
    blocks = [first] + [gas_ref[x * FY : (x + 1) * FY, :] for x in range(FX)] + [last]
    smooth = []
    for x in range(FX):
        block = blocks[x] + 2.0 * blocks[x + 1] + blocks[x + 2]
        padded = jnp.concatenate([before[x : x + 1], block, after[x : x + 1]], axis=0)
        smooth.append((padded[0:FY] + 2.0 * block + padded[2 : FY + 2]) / 16.0)
    smooth = jnp.concatenate(smooth, axis=0)
    halves = []
    for half in range(2):
        base = half * width
        density = smooth[:, base + lanes : base + lanes + TILE]
        scale = 1.0 / (1.0 + density * density)
        halves.append(smooth[:, base : base + lanes] * jnp.concatenate([scale] * rows, axis=1))
    for r in range(rows):
        where = slice(r * TILE, (r + 1) * TILE)
        both = jnp.concatenate([halves[0][:, where], halves[1][:, where]], axis=1)
        drag_ref[r] = both.reshape(FX, FY, FZ).astype(jnp.bfloat16)
    mark = width % LANES
    marks = mark_ref[...].astype(jnp.float32)
    column, height = marks[:, mark : mark + 1], marks[:, mark + 1 : mark + 2]
    hot = one_hot(column == iota((1, COLS), 1).astype(jnp.float32))
    place = (iota((1, lanes), 1) % TILE).astype(jnp.float32)
    low = dot(hot, halves[0].astype(jnp.bfloat16))
    high = dot(hot, halves[1].astype(jnp.bfloat16))
    back_ref[...] = jnp.where(place >= height, low, high).astype(jnp.bfloat16)


def force_kernel(back_ref, slot_ref, code_ref, part_ref, small_ref, live_ref, drag_ref, *refs):
    state_refs, (out_hbm, drag_hbm, out_ref, table_ref, sems) = refs[:4], refs[4:]
    stores = [pltpu.make_async_copy(drag_ref, drag_hbm, sems.at[0])]
    stores[0].start()

    def store(where):
        stores.append(pltpu.make_async_copy(out_ref.at[:, where], out_hbm.at[:, where], sems.at[len(stores)]))
        stores[-1].start()

    rows, slots = out_ref.shape
    parts = part_ref.shape[1]
    tiles = slot_ref.shape[1]
    migr = (slots - parts) // 4
    match = one_hot(iota((back_ref.shape[0], tiles), 0) == slot_ref[...])
    table_ref[...] = dot(back_ref[...], match, TN).astype(jnp.bfloat16)
    channels = part_ref.shape[0]
    damping = small_ref[rows : 2 * rows, channels : channels + 1]

    def look(code):
        values = dot(table_ref[...], ones(equal(tiles, code // TILE))).astype(jnp.bfloat16)
        hit = equal(TILE, code % TILE)
        found = []
        for r in range(rows):
            picked = jnp.where(hit, values[r * TILE : (r + 1) * TILE], jnp.bfloat16(0))
            while picked.shape[0] > 16:
                half = picked.shape[0] // 2
                picked = picked[:half] + picked[half:]
            found.append(jnp.sum(picked.astype(jnp.float32), axis=0, keepdims=True))
        return jnp.concatenate(found, axis=0)

    for begin in range(0, parts, CHUNK):
        where = slice(begin, begin + CHUNK)
        live = side_by_side(live_ref, 0, begin, CHUNK)
        out_ref[:, where] = live * (look(code_ref[:, where]) - damping * part_ref[:rows, where])
        store(where)
    drag = look(code_ref[:, parts:])
    for row, arrived in enumerate(arrived_blocks(state_refs)):
        begin = parts + row * migr
        live = jnp.concatenate([arrived[k : k + 1, migr:] for k in range(migr // LANES)], axis=1)
        force = drag[:, row * migr : (row + 1) * migr] - damping * arrived[:rows, :migr]
        out_ref[:, begin : begin + migr] = live * force
    store(slice(parts, slots))
    for copy in stores:
        copy.wait()


def call(kernel, shapes, *operands, limit=None, late=(), scratch=()):
    vmem, hbm = pl.BlockSpec(memory_space=pltpu.VMEM), pl.BlockSpec(memory_space=pltpu.HBM)
    return pl.pallas_call(
        kernel,
        out_shape=shapes,
        in_specs=[hbm if limit else vmem] * len(operands),
        out_specs=[hbm if limit or i in late else vmem for i in range(len(shapes))],
        scratch_shapes=scratch,
        compiler_params=pltpu.CompilerParams(vmem_limit_bytes=limit or VMEM),
    )(*operands)


def per_device(
    particles,
    migrant_index,
    migrant_count,
    migrated_slot_cell,
    source_tile_size,
    tile_owner,
    tile_offset,
    closure,
    damping,
):
    f32, bf16, i32 = jnp.float32, jnp.bfloat16, jnp.int32
    shape = jax.ShapeDtypeStruct
    channels, parts = particles.shape
    rows = closure.shape[0]
    migr = migrant_index.shape[1]
    slots = migrated_slot_cell.shape[0]
    tiles = source_tile_size.shape[1]
    devices = lax.axis_size("gx") * lax.axis_size("gy")
    capacity = max(2, 2 * tiles // devices)
    count = devices * capacity
    width = (rows + 1) * TILE
    lanes = (width + LANES) // LANES * LANES
    small_count = small_rows(rows, 4 * migr, slots)[-1]
    operands = (
        particles, migrant_index, migrant_count, source_tile_size, tile_owner.reshape(1, tiles),
        tile_offset.reshape(1, tiles), closure, damping.reshape(1, rows), migrated_slot_cell.reshape(1, slots),
    )
    *leaving, small = call(
        pick_kernel,
        [shape((channels, migr + LANES), bf16)] * 4 + [shape((small_count, GROUP), f32)],
        *operands, limit=LARGE,
        scratch=[(pltpu.SMEM if i == 2 else pltpu.VMEM)(x.shape, x.dtype) for i, x in enumerate(operands)]
        + [pltpu.VMEM((4, channels, migr + LANES), bf16), pltpu.VMEM((small_count, GROUP), f32),
           pltpu.SemaphoreType.DMA((9,)), pltpu.SemaphoreType.DMA((5,))],
    )
    (xa, xb), (ya, yb) = exchange(*leaving[:2], "gx"), exchange(*leaving[2:], "gy")
    arrived = yb, xb, ya, xa
    sums, code, slot, marks, live = call(
        functools.partial(deposit_kernel, capacity, rows, 4 * migr),
        [shape((width, tiles), f32), shape((1, slots), i32), shape((1, tiles), i32),
         shape((lanes - width, tiles), bf16), shape((parts // LANES, LANES), f32)],
        particles, small,
    )
    (payload,) = call(
        functools.partial(pack_kernel, rows), [shape((count, lanes), bf16)],
        sums, code, slot, marks, small, *arrived,
    )
    received = lax.all_to_all(
        payload.reshape(devices, capacity, lanes), ("gx", "gy"), split_axis=0, concat_axis=0, tiled=True
    ).reshape(count, lanes)
    grid, edge = shape((COLS, 2 * width), f32), shape((2 * FX, width), bf16)
    gas, xa, xb, ya, yb = call(place_kernel, [grid] + [edge] * 4, received)
    ya, yb = exchange(ya, yb, "gy")
    xa, xb = exchange(xa, xb, "gx")
    ca, cb = exchange(*call(corner_kernel, [edge, edge], yb, ya), "gx")
    drag, back = call(
        drag_kernel,
        [shape((rows, FX, FY, FZ), bf16), shape((count, rows * TILE), bf16)],
        received[:, lanes - LANES :], gas, yb, ya, xb, xa, cb, ca,
    )
    returned = lax.all_to_all(
        back.reshape(devices, capacity, rows * TILE), ("gx", "gy"), split_axis=0, concat_axis=0, tiled=True
    ).reshape(count, rows * TILE)
    force, drag = call(
        force_kernel, [shape((rows, slots), f32), shape(drag.shape, bf16)],
        returned, slot, code, particles, small, live, drag, *arrived, late=(0, 1),
        scratch=[pltpu.VMEM((rows, slots), f32), pltpu.VMEM((rows * TILE, tiles), bf16),
                 pltpu.SemaphoreType.DMA((2 + parts // CHUNK,))],
    )
    return drag, force


def solution(mesh):
    both = ("gx", "gy")
    in_specs = (
        P(None, both),
        P(both, None),
        P(both, None),
        P(both),
        P(both, None),
        P(both, None),
        P(both),
        P(),
        P(),
    )
    out_specs = (P(None, "gx", "gy", None), P(None, both))
    return jax.shard_map(
        per_device, mesh=mesh, in_specs=in_specs, out_specs=out_specs, check_vma=False
    )
```

```python
import functools

import jax
import jax.numpy as jnp
from jax import lax
from jax.experimental import pallas as pl
from jax.experimental.pallas import tpu as pltpu
from jax.sharding import PartitionSpec as P

TILE = 64
FX = 8
FY = 8
FZ = 128
COLS = FX * FY
LANES = 128
GROUP = 256
CHUNK = 2048
VMEM = 48 * 1024 * 1024
LARGE = 63 * 1024 * 1024

NT = (((1,), (1,)), ((), ()))
TN = (((0,), (0,)), ((), ()))


def iota(shape, dim):
    return lax.broadcasted_iota(jnp.int32, shape, dim)


def dot(a, b, dims=(((1,), (0,)), ((), ()))):
    return lax.dot_general(a, b, dims, preferred_element_type=jnp.float32)


def one_hot(mask):
    return jnp.where(mask, 1.0, 0.0).astype(jnp.bfloat16)


def equal(rows, row):
    numbers = iota((rows, row.shape[1]), 0).astype(jnp.float32).astype(jnp.bfloat16)
    return numbers == row.astype(jnp.float32).astype(jnp.bfloat16)


def ones(mask):
    return jnp.where(mask, jnp.bfloat16(1), jnp.bfloat16(0))


def fetch(sources, targets, sems):
    copies = [
        pltpu.make_async_copy(source, target, sems.at[i])
        for i, (source, target) in enumerate(zip(sources, targets))
    ]
    for copy in copies:
        copy.start()
    return copies


def is_even(axis):
    return lax.axis_index(axis) % 2 == 0


def exchange(block_a, block_b, axis):
    size = lax.axis_size(axis)
    blocks = {}
    for odd, block in ((1, block_b), (0, block_a)):
        pairs = [(i, (i + 1) % size if i % 2 == odd else (i - 1) % size) for i in range(size)]
        blocks[odd] = lax.ppermute(block, axis, pairs)
    return blocks[0], blocks[1]


def ordered(first, second, axis):
    even = is_even(axis)
    return jnp.where(even, second, first), jnp.where(even, first, second)


def leaving_row(index_ref, count_ref, parts):
    migr = index_ref.shape[1]
    lane = iota((1, migr), 1)
    odd = [jnp.where(is_even(axis), 0, 1) for axis in ("gx", "gy")]
    rows = []
    for row in (odd[0], 1 - odd[0], 2 + odd[1], 3 - odd[1]):
        rows.append(jnp.where(lane < count_ref[0, row], index_ref[pl.ds(row, 1), :], parts))
    return jnp.concatenate(rows, axis=1)


def arrived_blocks(refs):
    yb, xb, ya, xa = [ref[...].astype(jnp.float32) for ref in refs]
    return ordered(xa, xb, "gx") + ordered(ya, yb, "gy")


def small_rows(rows, leaving, slots):
    leave = 2 * rows
    cells = leave + leaving // GROUP
    return rows, leave, cells, cells + slots // GROUP


def pick_kernel(
    part_hbm, index_hbm, count_hbm, size_hbm, owner_hbm, offset_hbm, closure_hbm, damping_hbm, cell_hbm, *refs
):
    out_hbm, small_hbm, refs = refs[:4], refs[4], refs[5:]
    part_ref, index_ref, count_ref, size_ref, owner_ref, offset_ref = refs[:6]
    closure_ref, damping_ref, cell_ref, out_ref, small_ref, sems, out_sems = refs[6:]
    channels, parts = part_ref.shape
    migr = index_ref.shape[1]
    slots = cell_ref.shape[1]
    groups = parts // GROUP
    rows, width = closure_ref.shape
    closure_row, leave_row, cell_row, _ = small_rows(rows, 4 * migr, slots)
    copies = fetch(
        [index_hbm, count_hbm, part_hbm, size_hbm, owner_hbm, offset_hbm, closure_hbm, damping_hbm, cell_hbm],
        [index_ref, count_ref, part_ref, size_ref, owner_ref, offset_ref, closure_ref, damping_ref, cell_ref],
        sems,
    )
    copies[0].wait()
    copies[1].wait()
    leave = leaving_row(index_ref, count_ref, parts)
    high = leave // GROUP
    low = ones(equal(GROUP, leave % GROUP))
    for copy in copies[3:]:
        copy.wait()
    for row, ref in enumerate((size_ref, owner_ref, offset_ref)):
        small_ref[row : row + 1, :] = ref[...].astype(jnp.float32)
    small_ref[closure_row:leave_row, :width] = closure_ref[...]
    diagonal = iota((rows, rows), 0) == iota((rows, rows), 1)
    damping = jnp.sum(jnp.where(diagonal, damping_ref[...], 0.0), axis=1, keepdims=True)
    small_ref[closure_row:leave_row, width : width + 1] = damping
    for first, line in ((leave_row, leave), (cell_row, cell_ref[...])):
        for k in range(line.shape[1] // GROUP):
            part = line[:, k * GROUP : (k + 1) * GROUP]
            small_ref[first + k : first + k + 1, :] = part.astype(jnp.float32)
    stores = [pltpu.make_async_copy(small_ref, small_hbm, out_sems.at[4])]
    stores[0].start()
    copies[2].wait()
    table = jnp.concatenate(
        [part_ref[:, g * GROUP : (g + 1) * GROUP].astype(jnp.bfloat16) for g in range(groups)], axis=0
    )
    live = jnp.where(leave < parts, 1.0, 0.0)
    for r in range(4):
        where = slice(r * migr, (r + 1) * migr)
        found = dot(table, low[:, where])
        picked = jnp.zeros((channels, migr), jnp.float32)
        for g in range(groups):
            picked = jnp.where(high[:, where] == g, found[g * channels : (g + 1) * channels], picked)
        out_ref[r, :, :migr] = picked.astype(jnp.bfloat16)
        flags = [live[:, k : k + LANES] for k in range(r * migr, (r + 1) * migr, LANES)]
        flags.append(jnp.zeros((channels - len(flags), LANES), jnp.float32))
        out_ref[r, :, migr:] = jnp.concatenate(flags, axis=0).astype(jnp.bfloat16)
        stores.append(pltpu.make_async_copy(out_ref.at[r], out_hbm[r], out_sems.at[r]))
        stores[-1].start()
    for store in stores:
        store.wait()


def mix(closure, state):
    state = state.astype(jnp.float32)
    mixed = closure[:, 0:1] * state[0:1]
    for f in range(1, state.shape[0]):
        mixed = mixed + closure[:, f : f + 1] * state[f : f + 1]
    return mixed, state[0:1]


def side_by_side(ref, first, begin, width):
    lanes = ref.shape[1]
    first = first + begin // lanes
    rows = [ref[r : r + 1, :] for r in range(first, first + width // lanes)]
    return jnp.concatenate(rows, axis=1)


def spread(mixed, first, place):
    hit = equal(TILE, place)
    values = jnp.concatenate([mixed, first], axis=0).astype(jnp.bfloat16)
    return jnp.concatenate(
        [jnp.where(hit, values[r : r + 1], jnp.bfloat16(0)) for r in range(values.shape[0])], axis=0
    )


def deposit_kernel(
    capacity, rows, leaving, part_ref, small_ref, sum_ref, code_ref, slot_ref, mark_ref, live_ref
):
    channels, parts = part_ref.shape
    slots = code_ref.shape[1]
    tiles = slot_ref.shape[1]
    groups = parts // GROUP
    closure_row, leave_row, cell_row, _ = small_rows(rows, leaving, slots)
    closure = small_ref[closure_row:leave_row, :channels]

    leave = side_by_side(small_ref, leave_row, 0, leaving).astype(jnp.int32)
    halves = [leave[:, : leaving // 2], leave[:, leaving // 2 :]]
    high = jnp.concatenate([ones(equal(2 * groups, half // LANES)) for half in halves], axis=0)
    low = jnp.concatenate([ones(equal(LANES, half % LANES)) for half in halves], axis=0)
    hits = dot(high, low, NT)
    live_ref[...] = 1.0 - (hits[: 2 * groups, :LANES] + hits[2 * groups :, LANES:])

    sizes, owners, offset = [small_ref[r : r + 1, :] for r in range(3)]
    offset = offset.astype(jnp.int32)
    square = (tiles, tiles)
    below, across = iota(square, 0), iota(square, 1)
    inputs = [sizes, owners, (offset % FZ).astype(jnp.float32), jnp.zeros((5, tiles), jnp.float32)]
    inputs = jnp.concatenate(inputs, axis=0).astype(jnp.bfloat16)
    turned = dot(ones(below == across), inputs, NT)
    start = dot(ones(across < below), inputs, NT)[:, 0:1].astype(jnp.int32)
    height = turned[:, 2:3].astype(jnp.int32)
    code = iota((tiles, 1), 0) * TILE + (height - start) % TILE
    code_step = code - jnp.concatenate([jnp.zeros((1, 1), jnp.int32), code[: tiles - 1]], axis=0)
    earlier = ones((turned[:, 1:2] == owners) & (below < across))
    rank = dot(jnp.ones((8, tiles), jnp.bfloat16), earlier)[0:1]
    slot_ref[...] = (owners * capacity + rank).astype(jnp.int32)
    starts = jnp.broadcast_to(start.astype(jnp.int16), (tiles, CHUNK))
    steps = jnp.broadcast_to(code_step.astype(jnp.int16), (tiles, CHUNK))
    lines = iota(mark_ref.shape, 0)
    marks = jnp.where(lines == 0, offset // FZ, jnp.where(lines == 1, offset % FZ, 0))
    mark_ref[...] = marks.astype(jnp.float32).astype(jnp.bfloat16)

    def find(begin):
        cell = side_by_side(small_ref, cell_row, begin, CHUNK).astype(jnp.int32)
        found = jnp.where(cell.astype(jnp.int16) >= starts, steps, jnp.int16(0))
        while found.shape[0] > 16:
            half = found.shape[0] // 2
            found = found[:half] + found[half:]
        found = jnp.sum(found.astype(jnp.int32), axis=0, keepdims=True) & 0xFFFF
        return found // TILE, (found + cell) % TILE

    for begin in range(parts, slots, CHUNK):
        tile, place = find(begin)
        code_ref[:, begin : begin + CHUNK] = tile * TILE + place
    for begin in range(0, parts, CHUNK):
        tile, place = find(begin)
        code_ref[:, begin : begin + CHUNK] = tile * TILE + place
        live = side_by_side(live_ref, 0, begin, CHUNK)
        state = part_ref[:, begin : begin + CHUNK] * live
        mixed, first = mix(closure, state.astype(jnp.bfloat16))
        added = dot(spread(mixed, first, place), ones(equal(tiles, tile)), NT)
        total = added if begin == 0 else total + added
    sum_ref[...] = total


def pack_kernel(rows, sum_ref, code_ref, slot_ref, mark_ref, small_ref, *refs):
    state_refs, out_ref = refs[:4], refs[4]
    channels, tiles = state_refs[0].shape[0], slot_ref.shape[1]
    closure = small_ref[rows : 2 * rows, :channels]
    migr = state_refs[0].shape[1] - LANES
    code = code_ref[:, code_ref.shape[1] - 4 * migr :]
    state = jnp.concatenate([block[:, :migr] for block in arrived_blocks(state_refs)], axis=1)
    mixed, first = mix(closure, state)
    total = sum_ref[...] + dot(spread(mixed, first, code % TILE), ones(equal(tiles, code // TILE)), NT)
    table = jnp.concatenate([total.astype(jnp.bfloat16), mark_ref[...]], axis=0)
    match = one_hot(iota((out_ref.shape[0], tiles), 0) == slot_ref[...])
    out_ref[...] = dot(match, table, NT).astype(jnp.bfloat16)


def tile_marks(tile_ref, width):
    marks = tile_ref[:, width // LANES * LANES :]
    return marks[:, width % LANES : width % LANES + 1], marks[:, width % LANES + 1 : width % LANES + 2]


def place_kernel(tile_ref, gas_ref, xa_ref, xb_ref):
    even = is_even("gx")
    count, lanes = tile_ref.shape
    width = gas_ref.shape[1] // 2
    column, height = tile_marks(tile_ref, width)
    hot = ones(column == iota((1, LANES), 1).astype(jnp.float32).astype(jnp.bfloat16))
    place = (iota((1, width), 1) % TILE).astype(jnp.float32).astype(jnp.bfloat16)
    values = tile_ref[:, :width]
    for half, mask in enumerate((place >= height, place < height)):
        total = dot(hot, jnp.where(mask, values, jnp.bfloat16(0)), TN)
        where = slice(half * width, (half + 1) * width)
        gas_ref[:, where] = total[:COLS]
        rows = slice(half * FY, (half + 1) * FY)
        low, high = total[:FY], total[COLS - FY : COLS]
        xa_ref[rows, :] = jnp.where(even, high, low).astype(jnp.bfloat16)
        xb_ref[rows, :] = jnp.where(even, low, high).astype(jnp.bfloat16)


def unfold(ref):
    edge = ref[...].astype(jnp.float32)
    half = edge.shape[0] // 2
    return jnp.concatenate([edge[:half], edge[half:]], axis=1)


def along_kernel(gas_ref, xb_ref, xa_ref, out_ref, ya_ref, yb_ref):
    before, after = ordered(unfold(xa_ref), unfold(xb_ref), "gx")
    blocks = [before] + [gas_ref[x * FY : (x + 1) * FY, :] for x in range(FX)] + [after]
    along = [blocks[x] + 2.0 * blocks[x + 1] + blocks[x + 2] for x in range(FX)]
    for x in range(FX):
        out_ref[x * FY : (x + 1) * FY, :] = along[x]
    width = ya_ref.shape[1]
    edges = []
    for row in (0, FY - 1):
        edge = jnp.concatenate([along[x][row : row + 1] for x in range(FX)], axis=0)
        edges.append(jnp.concatenate([edge[:, :width], edge[:, width:]], axis=0))
    even = is_even("gy")
    ya_ref[...] = jnp.where(even, edges[1], edges[0]).astype(jnp.bfloat16)
    yb_ref[...] = jnp.where(even, edges[0], edges[1]).astype(jnp.bfloat16)


def drag_kernel(tile_ref, along_ref, yb_ref, ya_ref, drag_ref, back_ref):
    rows = drag_ref.shape[0]
    width = along_ref.shape[1] // 2
    lanes = rows * TILE
    before, after = ordered(unfold(ya_ref), unfold(yb_ref), "gy")
    smooth = []
    for x in range(FX):
        block = along_ref[x * FY : (x + 1) * FY, :]
        padded = jnp.concatenate([before[x : x + 1], block, after[x : x + 1]], axis=0)
        smooth.append((padded[0:FY] + 2.0 * block + padded[2 : FY + 2]) / 16.0)
    smooth = jnp.concatenate(smooth, axis=0)
    halves = []
    for half in range(2):
        base = half * width
        density = smooth[:, base + lanes : base + lanes + TILE]
        scale = 1.0 / (1.0 + density * density)
        halves.append(smooth[:, base : base + lanes] * jnp.concatenate([scale] * rows, axis=1))
    for r in range(rows):
        where = slice(r * TILE, (r + 1) * TILE)
        both = jnp.concatenate([halves[0][:, where], halves[1][:, where]], axis=1)
        drag_ref[r] = both.reshape(FX, FY, FZ).astype(jnp.bfloat16)
    column, height = tile_marks(tile_ref, width)
    hot = ones(column == iota((1, COLS), 1).astype(jnp.float32).astype(jnp.bfloat16))
    place = (iota((1, lanes), 1) % TILE).astype(jnp.float32).astype(jnp.bfloat16)
    low = dot(hot, halves[0].astype(jnp.bfloat16))
    high = dot(hot, halves[1].astype(jnp.bfloat16))
    back_ref[...] = jnp.where(place >= height, low.astype(jnp.bfloat16), high.astype(jnp.bfloat16))


def force_kernel(back_ref, slot_ref, code_ref, part_ref, small_ref, live_ref, drag_ref, *refs):
    state_refs, (out_hbm, drag_hbm, out_ref, table_ref, sems) = refs[:4], refs[4:]
    stores = [pltpu.make_async_copy(drag_ref, drag_hbm, sems.at[0])]
    stores[0].start()

    def store(where):
        stores.append(pltpu.make_async_copy(out_ref.at[:, where], out_hbm.at[:, where], sems.at[len(stores)]))
        stores[-1].start()

    rows, slots = out_ref.shape
    parts = part_ref.shape[1]
    tiles = slot_ref.shape[1]
    migr = (slots - parts) // 4
    match = one_hot(iota((back_ref.shape[0], tiles), 0) == slot_ref[...])
    table_ref[...] = dot(back_ref[...], match, TN).astype(jnp.bfloat16)
    channels = part_ref.shape[0]
    damping = small_ref[rows : 2 * rows, channels : channels + 1]

    def look(code):
        values = dot(table_ref[...], ones(equal(tiles, code // TILE))).astype(jnp.bfloat16)
        hit = equal(TILE, code % TILE)
        found = []
        for r in range(rows):
            picked = jnp.where(hit, values[r * TILE : (r + 1) * TILE], jnp.bfloat16(0))
            while picked.shape[0] > 16:
                half = picked.shape[0] // 2
                picked = picked[:half] + picked[half:]
            found.append(jnp.sum(picked.astype(jnp.float32), axis=0, keepdims=True))
        return jnp.concatenate(found, axis=0)

    for begin in range(0, parts, CHUNK):
        where = slice(begin, begin + CHUNK)
        live = side_by_side(live_ref, 0, begin, CHUNK)
        out_ref[:, where] = live * (look(code_ref[:, where]) - damping * part_ref[:rows, where])
        store(where)
    drag = look(code_ref[:, parts:])
    for row, arrived in enumerate(arrived_blocks(state_refs)):
        begin = parts + row * migr
        live = jnp.concatenate([arrived[k : k + 1, migr:] for k in range(migr // LANES)], axis=1)
        force = drag[:, row * migr : (row + 1) * migr] - damping * arrived[:rows, :migr]
        out_ref[:, begin : begin + migr] = live * force
    store(slice(parts, slots))
    for copy in stores:
        copy.wait()


def call(kernel, shapes, *operands, limit=None, late=(), scratch=()):
    vmem, hbm = pl.BlockSpec(memory_space=pltpu.VMEM), pl.BlockSpec(memory_space=pltpu.HBM)
    return pl.pallas_call(
        kernel,
        out_shape=shapes,
        in_specs=[hbm if limit else vmem] * len(operands),
        out_specs=[hbm if limit or i in late else vmem for i in range(len(shapes))],
        scratch_shapes=scratch,
        compiler_params=pltpu.CompilerParams(vmem_limit_bytes=limit or VMEM),
    )(*operands)


def per_device(
    particles,
    migrant_index,
    migrant_count,
    migrated_slot_cell,
    source_tile_size,
    tile_owner,
    tile_offset,
    closure,
    damping,
):
    f32, bf16, i32 = jnp.float32, jnp.bfloat16, jnp.int32
    shape = jax.ShapeDtypeStruct
    channels, parts = particles.shape
    rows = closure.shape[0]
    migr = migrant_index.shape[1]
    slots = migrated_slot_cell.shape[0]
    tiles = source_tile_size.shape[1]
    devices = lax.axis_size("gx") * lax.axis_size("gy")
    capacity = max(2, 2 * tiles // devices)
    count = devices * capacity
    width = (rows + 1) * TILE
    lanes = (width + LANES) // LANES * LANES
    small_count = small_rows(rows, 4 * migr, slots)[-1]
    operands = (
        particles, migrant_index, migrant_count, source_tile_size, tile_owner.reshape(1, tiles),
        tile_offset.reshape(1, tiles), closure, damping.reshape(1, rows), migrated_slot_cell.reshape(1, slots),
    )
    *leaving, small = call(
        pick_kernel,
        [shape((channels, migr + LANES), bf16)] * 4 + [shape((small_count, GROUP), f32)],
        *operands, limit=LARGE,
        scratch=[(pltpu.SMEM if i == 2 else pltpu.VMEM)(x.shape, x.dtype) for i, x in enumerate(operands)]
        + [pltpu.VMEM((4, channels, migr + LANES), bf16), pltpu.VMEM((small_count, GROUP), f32),
           pltpu.SemaphoreType.DMA((9,)), pltpu.SemaphoreType.DMA((5,))],
    )
    (xa, xb), (ya, yb) = exchange(*leaving[:2], "gx"), exchange(*leaving[2:], "gy")
    arrived = yb, xb, ya, xa
    sums, code, slot, marks, live = call(
        functools.partial(deposit_kernel, capacity, rows, 4 * migr),
        [shape((width, tiles), f32), shape((1, slots), i32), shape((1, tiles), i32),
         shape((lanes - width, tiles), bf16), shape((parts // LANES, LANES), f32)],
        particles, small,
    )
    (payload,) = call(
        functools.partial(pack_kernel, rows), [shape((count, lanes), bf16)],
        sums, code, slot, marks, small, *arrived,
    )
    received = lax.all_to_all(
        payload.reshape(devices, capacity, lanes), ("gx", "gy"), split_axis=0, concat_axis=0, tiled=True
    ).reshape(count, lanes)
    grid, edge = shape((COLS, 2 * width), f32), shape((2 * FX, width), bf16)
    gas, xa, xb = call(place_kernel, [grid, edge, edge], received)
    xa, xb = exchange(xa, xb, "gx")
    along, ya, yb = call(along_kernel, [grid, edge, edge], gas, xb, xa)
    ya, yb = exchange(ya, yb, "gy")
    drag, back = call(
        drag_kernel,
        [shape((rows, FX, FY, FZ), bf16), shape((count, rows * TILE), bf16)],
        received, along, yb, ya,
    )
    returned = lax.all_to_all(
        back.reshape(devices, capacity, rows * TILE), ("gx", "gy"), split_axis=0, concat_axis=0, tiled=True
    ).reshape(count, rows * TILE)
    force, drag = call(
        force_kernel, [shape((rows, slots), f32), shape(drag.shape, bf16)],
        returned, slot, code, particles, small, live, drag, *arrived, late=(0, 1),
        scratch=[pltpu.VMEM((rows, slots), f32), pltpu.VMEM((rows * TILE, tiles), bf16),
                 pltpu.SemaphoreType.DMA((2 + parts // CHUNK,))],
    )
    return drag, force


def solution(mesh):
    both = ("gx", "gy")
    in_specs = (
        P(None, both),
        P(both, None),
        P(both, None),
        P(both),
        P(both, None),
        P(both, None),
        P(both),
        P(),
        P(),
    )
    out_specs = (P(None, "gx", "gy", None), P(None, both))
    return jax.shard_map(
        per_device, mesh=mesh, in_specs=in_specs, out_specs=out_specs, check_vma=False
    )
```

```python
import functools

import jax
import jax.numpy as jnp
from jax import lax
from jax.experimental import pallas as pl
from jax.experimental.pallas import tpu as pltpu
from jax.sharding import PartitionSpec as P

TILE = 64
FX = 8
FY = 8
FZ = 128
COLS = FX * FY
LANES = 128
GROUP = 256
CHUNK = 2048
VMEM = 48 * 1024 * 1024
LARGE = 63 * 1024 * 1024

NT = (((1,), (1,)), ((), ()))
TN = (((0,), (0,)), ((), ()))


def iota(shape, dim):
    return lax.broadcasted_iota(jnp.int32, shape, dim)


def dot(a, b, dims=(((1,), (0,)), ((), ()))):
    return lax.dot_general(a, b, dims, preferred_element_type=jnp.float32)


def one_hot(mask):
    return jnp.where(mask, 1.0, 0.0).astype(jnp.bfloat16)


def equal(rows, row):
    numbers = iota((rows, row.shape[1]), 0).astype(jnp.float32).astype(jnp.bfloat16)
    return numbers == row.astype(jnp.float32).astype(jnp.bfloat16)


def ones(mask):
    return jnp.where(mask, jnp.bfloat16(1), jnp.bfloat16(0))


def fetch(sources, targets, sems):
    copies = [
        pltpu.make_async_copy(source, target, sems.at[i])
        for i, (source, target) in enumerate(zip(sources, targets))
    ]
    for copy in copies:
        copy.start()
    return copies


def is_even(axis):
    return lax.axis_index(axis) % 2 == 0


def exchange(block_a, block_b, axis):
    size = lax.axis_size(axis)
    blocks = {}
    for odd, block in ((1, block_b), (0, block_a)):
        pairs = [(i, (i + 1) % size if i % 2 == odd else (i - 1) % size) for i in range(size)]
        blocks[odd] = lax.ppermute(block, axis, pairs)
    return blocks[0], blocks[1]


def ordered(first, second, axis):
    even = is_even(axis)
    return jnp.where(even, second, first), jnp.where(even, first, second)


def leaving_row(index_ref, count_ref, parts):
    migr = index_ref.shape[1]
    lane = iota((1, migr), 1)
    odd = [jnp.where(is_even(axis), 0, 1) for axis in ("gx", "gy")]
    rows = []
    for row in (odd[0], 1 - odd[0], 2 + odd[1], 3 - odd[1]):
        rows.append(jnp.where(lane < count_ref[0, row], index_ref[pl.ds(row, 1), :], parts))
    return jnp.concatenate(rows, axis=1)


def arrived_blocks(refs):
    yb, xb, ya, xa = [ref[...].astype(jnp.float32) for ref in refs]
    return ordered(xa, xb, "gx") + ordered(ya, yb, "gy")


def small_rows(rows, leaving, slots):
    leave = 2 * rows
    cells = leave + leaving // GROUP
    return rows, leave, cells, cells + slots // GROUP


def pick_kernel(
    part_hbm, index_hbm, count_hbm, size_hbm, owner_hbm, offset_hbm, closure_hbm, damping_hbm, cell_hbm, *refs
):
    out_hbm, small_hbm, refs = refs[:4], refs[4], refs[5:]
    part_ref, index_ref, count_ref, size_ref, owner_ref, offset_ref = refs[:6]
    closure_ref, damping_ref, cell_ref, out_ref, small_ref, sems, out_sems = refs[6:]
    channels, parts = part_ref.shape
    migr = index_ref.shape[1]
    slots = cell_ref.shape[1]
    groups = parts // GROUP
    rows, width = closure_ref.shape
    closure_row, leave_row, cell_row, _ = small_rows(rows, 4 * migr, slots)
    copies = fetch(
        [index_hbm, count_hbm, part_hbm, size_hbm, owner_hbm, offset_hbm, closure_hbm, damping_hbm, cell_hbm],
        [index_ref, count_ref, part_ref, size_ref, owner_ref, offset_ref, closure_ref, damping_ref, cell_ref],
        sems,
    )
    copies[0].wait()
    copies[1].wait()
    leave = leaving_row(index_ref, count_ref, parts)
    high = leave // GROUP
    low = ones(equal(GROUP, leave % GROUP))
    for copy in copies[3:]:
        copy.wait()
    for row, ref in enumerate((size_ref, owner_ref, offset_ref)):
        small_ref[row : row + 1, :] = ref[...].astype(jnp.float32)
    small_ref[closure_row:leave_row, :width] = closure_ref[...]
    diagonal = iota((rows, rows), 0) == iota((rows, rows), 1)
    damping = jnp.sum(jnp.where(diagonal, damping_ref[...], 0.0), axis=1, keepdims=True)
    small_ref[closure_row:leave_row, width : width + 1] = damping
    for first, line in ((leave_row, leave), (cell_row, cell_ref[...])):
        for k in range(line.shape[1] // GROUP):
            part = line[:, k * GROUP : (k + 1) * GROUP]
            small_ref[first + k : first + k + 1, :] = part.astype(jnp.float32)
    stores = [pltpu.make_async_copy(small_ref, small_hbm, out_sems.at[4])]
    stores[0].start()
    copies[2].wait()
    table = jnp.concatenate(
        [part_ref[:, g * GROUP : (g + 1) * GROUP].astype(jnp.bfloat16) for g in range(groups)], axis=0
    )
    live = jnp.where(leave < parts, 1.0, 0.0)
    for r in range(4):
        where = slice(r * migr, (r + 1) * migr)
        found = dot(table, low[:, where])
        picked = jnp.zeros((channels, migr), jnp.float32)
        for g in range(groups):
            picked = jnp.where(high[:, where] == g, found[g * channels : (g + 1) * channels], picked)
        out_ref[r, :, :migr] = picked.astype(jnp.bfloat16)
        flags = [live[:, k : k + LANES] for k in range(r * migr, (r + 1) * migr, LANES)]
        flags.append(jnp.zeros((channels - len(flags), LANES), jnp.float32))
        out_ref[r, :, migr:] = jnp.concatenate(flags, axis=0).astype(jnp.bfloat16)
        stores.append(pltpu.make_async_copy(out_ref.at[r], out_hbm[r], out_sems.at[r]))
        stores[-1].start()
    for store in stores:
        store.wait()


def mix(closure, state):
    state = state.astype(jnp.float32)
    mixed = closure[:, 0:1] * state[0:1]
    for f in range(1, state.shape[0]):
        mixed = mixed + closure[:, f : f + 1] * state[f : f + 1]
    return mixed, state[0:1]


def side_by_side(ref, first, begin, width):
    lanes = ref.shape[1]
    first = first + begin // lanes
    rows = [ref[r : r + 1, :] for r in range(first, first + width // lanes)]
    return jnp.concatenate(rows, axis=1)


def spread(mixed, first, place):
    hit = equal(TILE, place)
    values = jnp.concatenate([mixed, first], axis=0).astype(jnp.bfloat16)
    return jnp.concatenate(
        [jnp.where(hit, values[r : r + 1], jnp.bfloat16(0)) for r in range(values.shape[0])], axis=0
    )


def deposit_kernel(capacity, rows, part_ref, small_ref, *refs):
    state_refs, (out_ref, code_ref, slot_ref, live_ref) = refs[:4], refs[4:]
    migr = state_refs[0].shape[1] - LANES
    leaving = 4 * migr
    channels, parts = part_ref.shape
    slots = code_ref.shape[1]
    tiles = slot_ref.shape[1]
    groups = parts // GROUP
    closure_row, leave_row, cell_row, _ = small_rows(rows, leaving, slots)
    closure = small_ref[closure_row:leave_row, :channels]

    leave = side_by_side(small_ref, leave_row, 0, leaving).astype(jnp.int32)
    halves = [leave[:, : leaving // 2], leave[:, leaving // 2 :]]
    high = jnp.concatenate([ones(equal(2 * groups, half // LANES)) for half in halves], axis=0)
    low = jnp.concatenate([ones(equal(LANES, half % LANES)) for half in halves], axis=0)
    hits = dot(high, low, NT)
    live_ref[...] = 1.0 - (hits[: 2 * groups, :LANES] + hits[2 * groups :, LANES:])

    sizes, owners, offset = [small_ref[r : r + 1, :] for r in range(3)]
    offset = offset.astype(jnp.int32)
    square = (tiles, tiles)
    below, across = iota(square, 0), iota(square, 1)
    inputs = [sizes, owners, (offset % FZ).astype(jnp.float32), jnp.zeros((5, tiles), jnp.float32)]
    inputs = jnp.concatenate(inputs, axis=0).astype(jnp.bfloat16)
    turned = dot(ones(below == across), inputs, NT)
    start = dot(ones(across < below), inputs, NT)[:, 0:1].astype(jnp.int32)
    height = turned[:, 2:3].astype(jnp.int32)
    code = iota((tiles, 1), 0) * TILE + (height - start) % TILE
    code_step = code - jnp.concatenate([jnp.zeros((1, 1), jnp.int32), code[: tiles - 1]], axis=0)
    earlier = ones((turned[:, 1:2] == owners) & (below < across))
    rank = dot(jnp.ones((8, tiles), jnp.bfloat16), earlier)[0:1]
    slot_ref[...] = (owners * capacity + rank).astype(jnp.int32)
    starts = jnp.broadcast_to(start.astype(jnp.int16), (tiles, CHUNK))
    steps = jnp.broadcast_to(code_step.astype(jnp.int16), (tiles, CHUNK))

    def find(begin):
        cell = side_by_side(small_ref, cell_row, begin, CHUNK).astype(jnp.int32)
        found = jnp.where(cell.astype(jnp.int16) >= starts, steps, jnp.int16(0))
        while found.shape[0] > 16:
            half = found.shape[0] // 2
            found = found[:half] + found[half:]
        found = jnp.sum(found.astype(jnp.int32), axis=0, keepdims=True) & 0xFFFF
        return found // TILE, (found + cell) % TILE

    arrived = jnp.concatenate([block[:, :migr] for block in arrived_blocks(state_refs)], axis=1)
    total = 0.0
    for begin in range(0, slots, CHUNK):
        tile, place = find(begin)
        code_ref[:, begin : begin + CHUNK] = tile * TILE + place
        if begin < parts:
            live = side_by_side(live_ref, 0, begin, CHUNK)
            state = part_ref[:, begin : begin + CHUNK] * live
        else:
            state = arrived[:, begin - parts : begin - parts + CHUNK]
        mixed, first = mix(closure, state.astype(jnp.bfloat16))
        total = total + dot(spread(mixed, first, place), ones(equal(tiles, tile)), NT)

    lines = iota((out_ref.shape[1] - total.shape[0], tiles), 0)
    marks = jnp.where(lines == 0, offset // FZ, jnp.where(lines == 1, offset % FZ, 0))
    marks = marks.astype(jnp.float32).astype(jnp.bfloat16)
    table = jnp.concatenate([total.astype(jnp.bfloat16), marks], axis=0)
    match = one_hot(iota((out_ref.shape[0], tiles), 0) == slot_ref[...])
    out_ref[...] = dot(match, table, NT).astype(jnp.bfloat16)


def place_kernel(tile_ref, gas_ref, xa_ref, xb_ref):
    even = is_even("gx")
    count, lanes = tile_ref.shape
    width = gas_ref.shape[1] // 2
    marks = tile_ref[:, lanes - LANES :].astype(jnp.float32)
    column = marks[:, width % LANES : width % LANES + 1]
    height = marks[:, width % LANES + 1 : width % LANES + 2]
    lane = iota((1, LANES), 1)
    hot = one_hot(column == lane.astype(jnp.float32))
    place = (iota((1, width), 1) % TILE).astype(jnp.float32)
    values = tile_ref[:, :width].astype(jnp.float32)
    for half, mask in enumerate((place >= height, place < height)):
        total = dot(hot, jnp.where(mask, values, 0.0).astype(jnp.bfloat16), TN)
        where = slice(half * width, (half + 1) * width)
        gas_ref[:, where] = total[:COLS]
        rows = slice(half * FY, (half + 1) * FY)
        low, high = total[:FY], total[COLS - FY : COLS]
        xa_ref[rows, :] = jnp.where(even, high, low).astype(jnp.bfloat16)
        xb_ref[rows, :] = jnp.where(even, low, high).astype(jnp.bfloat16)


def unfold(ref):
    edge = ref[...].astype(jnp.float32)
    half = edge.shape[0] // 2
    return jnp.concatenate([edge[:half], edge[half:]], axis=1)


def along_kernel(gas_ref, xb_ref, xa_ref, out_ref, ya_ref, yb_ref):
    before, after = ordered(unfold(xa_ref), unfold(xb_ref), "gx")
    blocks = [before] + [gas_ref[x * FY : (x + 1) * FY, :] for x in range(FX)] + [after]
    along = [blocks[x] + 2.0 * blocks[x + 1] + blocks[x + 2] for x in range(FX)]
    for x in range(FX):
        out_ref[x * FY : (x + 1) * FY, :] = along[x]
    width = ya_ref.shape[1]
    edges = []
    for row in (0, FY - 1):
        edge = jnp.concatenate([along[x][row : row + 1] for x in range(FX)], axis=0)
        edges.append(jnp.concatenate([edge[:, :width], edge[:, width:]], axis=0))
    even = is_even("gy")
    ya_ref[...] = jnp.where(even, edges[1], edges[0]).astype(jnp.bfloat16)
    yb_ref[...] = jnp.where(even, edges[0], edges[1]).astype(jnp.bfloat16)


def drag_kernel(mark_ref, along_ref, yb_ref, ya_ref, drag_ref, back_ref):
    rows = drag_ref.shape[0]
    width = along_ref.shape[1] // 2
    lanes = rows * TILE
    before, after = ordered(unfold(ya_ref), unfold(yb_ref), "gy")
    smooth = []
    for x in range(FX):
        block = along_ref[x * FY : (x + 1) * FY, :]
        padded = jnp.concatenate([before[x : x + 1], block, after[x : x + 1]], axis=0)
        smooth.append((padded[0:FY] + 2.0 * block + padded[2 : FY + 2]) / 16.0)
    smooth = jnp.concatenate(smooth, axis=0)
    halves = []
    for half in range(2):
        base = half * width
        density = smooth[:, base + lanes : base + lanes + TILE]
        scale = 1.0 / (1.0 + density * density)
        halves.append(smooth[:, base : base + lanes] * jnp.concatenate([scale] * rows, axis=1))
    for r in range(rows):
        where = slice(r * TILE, (r + 1) * TILE)
        both = jnp.concatenate([halves[0][:, where], halves[1][:, where]], axis=1)
        drag_ref[r] = both.reshape(FX, FY, FZ).astype(jnp.bfloat16)
    mark = width % LANES
    marks = mark_ref[...].astype(jnp.float32)
    column, height = marks[:, mark : mark + 1], marks[:, mark + 1 : mark + 2]
    hot = one_hot(column == iota((1, COLS), 1).astype(jnp.float32))
    place = (iota((1, lanes), 1) % TILE).astype(jnp.float32)
    low = dot(hot, halves[0].astype(jnp.bfloat16))
    high = dot(hot, halves[1].astype(jnp.bfloat16))
    back_ref[...] = jnp.where(place >= height, low, high).astype(jnp.bfloat16)


def force_kernel(back_ref, slot_ref, code_ref, part_ref, small_ref, live_ref, drag_ref, *refs):
    state_refs, (out_hbm, drag_hbm, out_ref, table_ref, sems) = refs[:4], refs[4:]
    stores = [pltpu.make_async_copy(drag_ref, drag_hbm, sems.at[0])]
    stores[0].start()

    def store(where):
        stores.append(pltpu.make_async_copy(out_ref.at[:, where], out_hbm.at[:, where], sems.at[len(stores)]))
        stores[-1].start()

    rows, slots = out_ref.shape
    parts = part_ref.shape[1]
    tiles = slot_ref.shape[1]
    migr = (slots - parts) // 4
    match = one_hot(iota((back_ref.shape[0], tiles), 0) == slot_ref[...])
    table_ref[...] = dot(back_ref[...], match, TN).astype(jnp.bfloat16)
    channels = part_ref.shape[0]
    damping = small_ref[rows : 2 * rows, channels : channels + 1]

    def look(code):
        values = dot(table_ref[...], ones(equal(tiles, code // TILE))).astype(jnp.bfloat16)
        hit = equal(TILE, code % TILE)
        found = []
        for r in range(rows):
            picked = jnp.where(hit, values[r * TILE : (r + 1) * TILE], jnp.bfloat16(0))
            while picked.shape[0] > 16:
                half = picked.shape[0] // 2
                picked = picked[:half] + picked[half:]
            found.append(jnp.sum(picked.astype(jnp.float32), axis=0, keepdims=True))
        return jnp.concatenate(found, axis=0)

    for begin in range(0, parts, CHUNK):
        where = slice(begin, begin + CHUNK)
        live = side_by_side(live_ref, 0, begin, CHUNK)
        out_ref[:, where] = live * (look(code_ref[:, where]) - damping * part_ref[:rows, where])
        store(where)
    drag = look(code_ref[:, parts:])
    for row, arrived in enumerate(arrived_blocks(state_refs)):
        begin = parts + row * migr
        live = jnp.concatenate([arrived[k : k + 1, migr:] for k in range(migr // LANES)], axis=1)
        force = drag[:, row * migr : (row + 1) * migr] - damping * arrived[:rows, :migr]
        out_ref[:, begin : begin + migr] = live * force
    store(slice(parts, slots))
    for copy in stores:
        copy.wait()


def call(kernel, shapes, *operands, limit=None, late=(), scratch=()):
    vmem, hbm = pl.BlockSpec(memory_space=pltpu.VMEM), pl.BlockSpec(memory_space=pltpu.HBM)
    return pl.pallas_call(
        kernel,
        out_shape=shapes,
        in_specs=[hbm if limit else vmem] * len(operands),
        out_specs=[hbm if limit or i in late else vmem for i in range(len(shapes))],
        scratch_shapes=scratch,
        compiler_params=pltpu.CompilerParams(vmem_limit_bytes=limit or VMEM),
    )(*operands)


def per_device(
    particles,
    migrant_index,
    migrant_count,
    migrated_slot_cell,
    source_tile_size,
    tile_owner,
    tile_offset,
    closure,
    damping,
):
    f32, bf16, i32 = jnp.float32, jnp.bfloat16, jnp.int32
    shape = jax.ShapeDtypeStruct
    channels, parts = particles.shape
    rows = closure.shape[0]
    migr = migrant_index.shape[1]
    slots = migrated_slot_cell.shape[0]
    tiles = source_tile_size.shape[1]
    devices = lax.axis_size("gx") * lax.axis_size("gy")
    capacity = max(2, 2 * tiles // devices)
    count = devices * capacity
    width = (rows + 1) * TILE
    lanes = (width + LANES) // LANES * LANES
    small_count = small_rows(rows, 4 * migr, slots)[-1]
    operands = (
        particles, migrant_index, migrant_count, source_tile_size, tile_owner.reshape(1, tiles),
        tile_offset.reshape(1, tiles), closure, damping.reshape(1, rows), migrated_slot_cell.reshape(1, slots),
    )
    *leaving, small = call(
        pick_kernel,
        [shape((channels, migr + LANES), bf16)] * 4 + [shape((small_count, GROUP), f32)],
        *operands, limit=LARGE,
        scratch=[(pltpu.SMEM if i == 2 else pltpu.VMEM)(x.shape, x.dtype) for i, x in enumerate(operands)]
        + [pltpu.VMEM((4, channels, migr + LANES), bf16), pltpu.VMEM((small_count, GROUP), f32),
           pltpu.SemaphoreType.DMA((9,)), pltpu.SemaphoreType.DMA((5,))],
    )
    (xa, xb), (ya, yb) = exchange(*leaving[:2], "gx"), exchange(*leaving[2:], "gy")
    arrived = yb, xb, ya, xa
    payload, code, slot, live = call(
        functools.partial(deposit_kernel, capacity, rows),
        [shape((count, lanes), bf16), shape((1, slots), i32), shape((1, tiles), i32),
         shape((parts // LANES, LANES), f32)],
        particles, small, *arrived,
    )
    received = lax.all_to_all(
        payload.reshape(devices, capacity, lanes), ("gx", "gy"), split_axis=0, concat_axis=0, tiled=True
    ).reshape(count, lanes)
    grid, edge = shape((COLS, 2 * width), f32), shape((2 * FX, width), bf16)
    gas, xa, xb = call(place_kernel, [grid, edge, edge], received)
    xa, xb = exchange(xa, xb, "gx")
    along, ya, yb = call(along_kernel, [grid, edge, edge], gas, xb, xa)
    ya, yb = exchange(ya, yb, "gy")
    drag, back = call(
        drag_kernel,
        [shape((rows, FX, FY, FZ), bf16), shape((count, rows * TILE), bf16)],
        received[:, lanes - LANES :], along, yb, ya,
    )
    returned = lax.all_to_all(
        back.reshape(devices, capacity, rows * TILE), ("gx", "gy"), split_axis=0, concat_axis=0, tiled=True
    ).reshape(count, rows * TILE)
    force, drag = call(
        force_kernel, [shape((rows, slots), f32), shape(drag.shape, bf16)],
        returned, slot, code, particles, small, live, drag, *arrived, late=(0, 1),
        scratch=[pltpu.VMEM((rows, slots), f32), pltpu.VMEM((rows * TILE, tiles), bf16),
                 pltpu.SemaphoreType.DMA((2 + parts // CHUNK,))],
    )
    return drag, force


def solution(mesh):
    both = ("gx", "gy")
    in_specs = (
        P(None, both),
        P(both, None),
        P(both, None),
        P(both),
        P(both, None),
        P(both, None),
        P(both),
        P(),
        P(),
    )
    out_specs = (P(None, "gx", "gy", None), P(None, both))
    return jax.shard_map(
        per_device, mesh=mesh, in_specs=in_specs, out_specs=out_specs, check_vma=False
    )
```

```python
import functools

import jax
import jax.numpy as jnp
from jax import lax
from jax.experimental import pallas as pl
from jax.experimental.pallas import tpu as pltpu
from jax.sharding import PartitionSpec as P

TILE = 64
FX = 8
FY = 8
FZ = 128
COLS = FX * FY
LANES = 128
GROUP = 256
CHUNK = 2048
VMEM = 48 * 1024 * 1024
LARGE = 63 * 1024 * 1024

NT = (((1,), (1,)), ((), ()))
TN = (((0,), (0,)), ((), ()))


def iota(shape, dim):
    return lax.broadcasted_iota(jnp.int32, shape, dim)


def dot(a, b, dims=(((1,), (0,)), ((), ()))):
    return lax.dot_general(a, b, dims, preferred_element_type=jnp.float32)


def one_hot(mask):
    return jnp.where(mask, 1.0, 0.0).astype(jnp.bfloat16)


def equal(rows, row):
    numbers = iota((rows, row.shape[1]), 0).astype(jnp.float32).astype(jnp.bfloat16)
    return numbers == row.astype(jnp.float32).astype(jnp.bfloat16)


def ones(mask):
    return jnp.where(mask, jnp.bfloat16(1), jnp.bfloat16(0))


def fetch(sources, targets, sems):
    copies = [
        pltpu.make_async_copy(source, target, sems.at[i])
        for i, (source, target) in enumerate(zip(sources, targets))
    ]
    for copy in copies:
        copy.start()
    return copies


def is_even(axis):
    return lax.axis_index(axis) % 2 == 0


def exchange(block_a, block_b, axis):
    size = lax.axis_size(axis)
    blocks = {}
    for odd, block in ((1, block_b), (0, block_a)):
        pairs = [(i, (i + 1) % size if i % 2 == odd else (i - 1) % size) for i in range(size)]
        blocks[odd] = lax.ppermute(block, axis, pairs)
    return blocks[0], blocks[1]


def ordered(first, second, axis):
    even = is_even(axis)
    return jnp.where(even, second, first), jnp.where(even, first, second)


def leaving_row(index_ref, count_ref, parts):
    migr = index_ref.shape[1]
    lane = iota((1, migr), 1)
    odd = [jnp.where(is_even(axis), 0, 1) for axis in ("gx", "gy")]
    rows = []
    for row in (odd[0], 1 - odd[0], 2 + odd[1], 3 - odd[1]):
        rows.append(jnp.where(lane < count_ref[0, row], index_ref[pl.ds(row, 1), :], parts))
    return jnp.concatenate(rows, axis=1)


def arrived_blocks(refs):
    yb, ya, xb, xa = [ref[...].astype(jnp.float32) for ref in refs]
    return ordered(xa, xb, "gx") + ordered(ya, yb, "gy")


def small_rows(rows, leaving, slots):
    leave = 2 * rows
    cells = leave + leaving // GROUP
    return rows, leave, cells, cells + slots // GROUP


def pick_kernel(
    part_hbm, index_hbm, count_hbm, size_hbm, owner_hbm, offset_hbm, closure_hbm, damping_hbm, cell_hbm, *refs
):
    out_hbm, small_hbm, refs = refs[:4], refs[4], refs[5:]
    part_ref, index_ref, count_ref, size_ref, owner_ref, offset_ref = refs[:6]
    closure_ref, damping_ref, cell_ref, out_ref, small_ref, sems, out_sems = refs[6:]
    channels, parts = part_ref.shape
    migr = index_ref.shape[1]
    slots = cell_ref.shape[1]
    groups = parts // GROUP
    rows, width = closure_ref.shape
    closure_row, leave_row, cell_row, _ = small_rows(rows, 4 * migr, slots)
    copies = fetch(
        [index_hbm, count_hbm, part_hbm, size_hbm, owner_hbm, offset_hbm, closure_hbm, damping_hbm, cell_hbm],
        [index_ref, count_ref, part_ref, size_ref, owner_ref, offset_ref, closure_ref, damping_ref, cell_ref],
        sems,
    )
    copies[0].wait()
    copies[1].wait()
    leave = leaving_row(index_ref, count_ref, parts)
    high = leave // GROUP
    low = ones(equal(GROUP, leave % GROUP))
    for copy in copies[3:]:
        copy.wait()
    for row, ref in enumerate((size_ref, owner_ref, offset_ref)):
        small_ref[row : row + 1, :] = ref[...].astype(jnp.float32)
    small_ref[closure_row:leave_row, :width] = closure_ref[...]
    diagonal = iota((rows, rows), 0) == iota((rows, rows), 1)
    damping = jnp.sum(jnp.where(diagonal, damping_ref[...], 0.0), axis=1, keepdims=True)
    small_ref[closure_row:leave_row, width : width + 1] = damping
    for first, line in ((leave_row, leave), (cell_row, cell_ref[...])):
        for k in range(line.shape[1] // GROUP):
            part = line[:, k * GROUP : (k + 1) * GROUP]
            small_ref[first + k : first + k + 1, :] = part.astype(jnp.float32)
    stores = [pltpu.make_async_copy(small_ref, small_hbm, out_sems.at[4])]
    stores[0].start()
    copies[2].wait()
    table = jnp.concatenate(
        [part_ref[:, g * GROUP : (g + 1) * GROUP].astype(jnp.bfloat16) for g in range(groups)], axis=0
    )
    live = jnp.where(leave < parts, 1.0, 0.0)
    for r in range(4):
        where = slice(r * migr, (r + 1) * migr)
        found = dot(table, low[:, where])
        picked = jnp.zeros((channels, migr), jnp.float32)
        for g in range(groups):
            picked = jnp.where(high[:, where] == g, found[g * channels : (g + 1) * channels], picked)
        out_ref[r, :, :migr] = picked.astype(jnp.bfloat16)
        flags = [live[:, k : k + LANES] for k in range(r * migr, (r + 1) * migr, LANES)]
        flags.append(jnp.zeros((channels - len(flags), LANES), jnp.float32))
        out_ref[r, :, migr:] = jnp.concatenate(flags, axis=0).astype(jnp.bfloat16)
        stores.append(pltpu.make_async_copy(out_ref.at[r], out_hbm[r], out_sems.at[r]))
        stores[-1].start()
    for store in stores:
        store.wait()


def mix(closure, state):
    state = state.astype(jnp.float32)
    mixed = closure[:, 0:1] * state[0:1]
    for f in range(1, state.shape[0]):
        mixed = mixed + closure[:, f : f + 1] * state[f : f + 1]
    return mixed, state[0:1]


def side_by_side(ref, first, begin, width):
    lanes = ref.shape[1]
    first = first + begin // lanes
    rows = [ref[r : r + 1, :] for r in range(first, first + width // lanes)]
    return jnp.concatenate(rows, axis=1)


def spread(mixed, first, place):
    hit = equal(TILE, place)
    values = jnp.concatenate([mixed, first], axis=0).astype(jnp.bfloat16)
    return jnp.concatenate(
        [jnp.where(hit, values[r : r + 1], jnp.bfloat16(0)) for r in range(values.shape[0])], axis=0
    )


def deposit_kernel(
    capacity, rows, leaving, part_ref, small_ref, sum_ref, code_ref, slot_ref, mark_ref, live_ref
):
    channels, parts = part_ref.shape
    slots = code_ref.shape[1]
    tiles = slot_ref.shape[1]
    groups = parts // GROUP
    closure_row, leave_row, cell_row, _ = small_rows(rows, leaving, slots)
    closure = small_ref[closure_row:leave_row, :channels]

    leave = side_by_side(small_ref, leave_row, 0, leaving).astype(jnp.int32)
    halves = [leave[:, : leaving // 2], leave[:, leaving // 2 :]]
    high = jnp.concatenate([ones(equal(2 * groups, half // LANES)) for half in halves], axis=0)
    low = jnp.concatenate([ones(equal(LANES, half % LANES)) for half in halves], axis=0)
    hits = dot(high, low, NT)
    live_ref[...] = 1.0 - (hits[: 2 * groups, :LANES] + hits[2 * groups :, LANES:])

    sizes, owners, offset = [small_ref[r : r + 1, :] for r in range(3)]
    offset = offset.astype(jnp.int32)
    square = (tiles, tiles)
    below, across = iota(square, 0), iota(square, 1)
    inputs = [sizes, owners, (offset % FZ).astype(jnp.float32), jnp.zeros((5, tiles), jnp.float32)]
    inputs = jnp.concatenate(inputs, axis=0).astype(jnp.bfloat16)
    turned = dot(ones(below == across), inputs, NT)
    start = dot(ones(across < below), inputs, NT)[:, 0:1].astype(jnp.int32)
    height = turned[:, 2:3].astype(jnp.int32)
    code = iota((tiles, 1), 0) * TILE + (height - start) % TILE
    code_step = code - jnp.concatenate([jnp.zeros((1, 1), jnp.int32), code[: tiles - 1]], axis=0)
    earlier = ones((turned[:, 1:2] == owners) & (below < across))
    rank = dot(jnp.ones((8, tiles), jnp.bfloat16), earlier)[0:1]
    slot_ref[...] = (owners * capacity + rank).astype(jnp.int32)
    starts = jnp.broadcast_to(start.astype(jnp.int16), (tiles, CHUNK))
    steps = jnp.broadcast_to(code_step.astype(jnp.int16), (tiles, CHUNK))
    lines = iota(mark_ref.shape, 0)
    marks = jnp.where(lines == 0, offset // FZ, jnp.where(lines == 1, offset % FZ, 0))
    mark_ref[...] = marks.astype(jnp.float32).astype(jnp.bfloat16)

    def find(begin):
        cell = side_by_side(small_ref, cell_row, begin, CHUNK).astype(jnp.int32)
        found = jnp.where(cell.astype(jnp.int16) >= starts, steps, jnp.int16(0))
        while found.shape[0] > 16:
            half = found.shape[0] // 2
            found = found[:half] + found[half:]
        found = jnp.sum(found.astype(jnp.int32), axis=0, keepdims=True) & 0xFFFF
        return found // TILE, (found + cell) % TILE

    for begin in range(parts, slots, CHUNK):
        tile, place = find(begin)
        code_ref[:, begin : begin + CHUNK] = tile * TILE + place
    for begin in range(0, parts, CHUNK):
        tile, place = find(begin)
        code_ref[:, begin : begin + CHUNK] = tile * TILE + place
        live = side_by_side(live_ref, 0, begin, CHUNK)
        state = part_ref[:, begin : begin + CHUNK] * live
        mixed, first = mix(closure, state.astype(jnp.bfloat16))
        added = dot(spread(mixed, first, place), ones(equal(tiles, tile)), NT)
        total = added if begin == 0 else total + added
    sum_ref[...] = total


def pack_kernel(rows, sum_ref, code_ref, slot_ref, mark_ref, small_ref, *refs):
    state_refs, out_ref = refs[:4], refs[4]
    channels, tiles = state_refs[0].shape[0], slot_ref.shape[1]
    closure = small_ref[rows : 2 * rows, :channels]
    migr = state_refs[0].shape[1] - LANES
    code = code_ref[:, code_ref.shape[1] - 4 * migr :]
    state = jnp.concatenate([block[:, :migr] for block in arrived_blocks(state_refs)], axis=1)
    mixed, first = mix(closure, state)
    total = sum_ref[...] + dot(spread(mixed, first, code % TILE), ones(equal(tiles, code // TILE)), NT)
    table = jnp.concatenate([total.astype(jnp.bfloat16), mark_ref[...]], axis=0)
    match = one_hot(iota((out_ref.shape[0], tiles), 0) == slot_ref[...])
    out_ref[...] = dot(match, table, NT).astype(jnp.bfloat16)


def place_kernel(tile_ref, gas_ref, xa_ref, xb_ref):
    even = is_even("gx")
    count, lanes = tile_ref.shape
    width = gas_ref.shape[1] // 2
    marks = tile_ref[:, lanes - LANES :].astype(jnp.float32)
    column = marks[:, width % LANES : width % LANES + 1]
    height = marks[:, width % LANES + 1 : width % LANES + 2]
    lane = iota((1, LANES), 1)
    hot = one_hot(column == lane.astype(jnp.float32))
    place = (iota((1, width), 1) % TILE).astype(jnp.float32)
    values = tile_ref[:, :width].astype(jnp.float32)
    for half, mask in enumerate((place >= height, place < height)):
        total = dot(hot, jnp.where(mask, values, 0.0).astype(jnp.bfloat16), TN)
        where = slice(half * width, (half + 1) * width)
        gas_ref[:, where] = total[:COLS]
        rows = slice(half * FY, (half + 1) * FY)
        low, high = total[:FY], total[COLS - FY : COLS]
        xa_ref[rows, :] = jnp.where(even, high, low).astype(jnp.bfloat16)
        xb_ref[rows, :] = jnp.where(even, low, high).astype(jnp.bfloat16)


def unfold(ref):
    edge = ref[...].astype(jnp.float32)
    half = edge.shape[0] // 2
    return jnp.concatenate([edge[:half], edge[half:]], axis=1)


def along_kernel(gas_ref, xb_ref, xa_ref, out_ref, ya_ref, yb_ref):
    before, after = ordered(unfold(xa_ref), unfold(xb_ref), "gx")
    blocks = [before] + [gas_ref[x * FY : (x + 1) * FY, :] for x in range(FX)] + [after]
    along = [blocks[x] + 2.0 * blocks[x + 1] + blocks[x + 2] for x in range(FX)]
    for x in range(FX):
        out_ref[x * FY : (x + 1) * FY, :] = along[x]
    width = ya_ref.shape[1]
    edges = []
    for row in (0, FY - 1):
        edge = jnp.concatenate([along[x][row : row + 1] for x in range(FX)], axis=0)
        edges.append(jnp.concatenate([edge[:, :width], edge[:, width:]], axis=0))
    even = is_even("gy")
    ya_ref[...] = jnp.where(even, edges[1], edges[0]).astype(jnp.bfloat16)
    yb_ref[...] = jnp.where(even, edges[0], edges[1]).astype(jnp.bfloat16)


def drag_kernel(mark_ref, along_ref, yb_ref, ya_ref, drag_ref, back_ref):
    rows = drag_ref.shape[0]
    width = along_ref.shape[1] // 2
    lanes = rows * TILE
    before, after = ordered(unfold(ya_ref), unfold(yb_ref), "gy")
    smooth = []
    for x in range(FX):
        block = along_ref[x * FY : (x + 1) * FY, :]
        padded = jnp.concatenate([before[x : x + 1], block, after[x : x + 1]], axis=0)
        smooth.append((padded[0:FY] + 2.0 * block + padded[2 : FY + 2]) / 16.0)
    smooth = jnp.concatenate(smooth, axis=0)
    halves = []
    for half in range(2):
        base = half * width
        density = smooth[:, base + lanes : base + lanes + TILE]
        scale = 1.0 / (1.0 + density * density)
        halves.append(smooth[:, base : base + lanes] * jnp.concatenate([scale] * rows, axis=1))
    for r in range(rows):
        where = slice(r * TILE, (r + 1) * TILE)
        both = jnp.concatenate([halves[0][:, where], halves[1][:, where]], axis=1)
        drag_ref[r] = both.reshape(FX, FY, FZ).astype(jnp.bfloat16)
    mark = width % LANES
    marks = mark_ref[...].astype(jnp.float32)
    column, height = marks[:, mark : mark + 1], marks[:, mark + 1 : mark + 2]
    hot = one_hot(column == iota((1, COLS), 1).astype(jnp.float32))
    place = (iota((1, lanes), 1) % TILE).astype(jnp.float32)
    low = dot(hot, halves[0].astype(jnp.bfloat16))
    high = dot(hot, halves[1].astype(jnp.bfloat16))
    back_ref[...] = jnp.where(place >= height, low, high).astype(jnp.bfloat16)


def force_kernel(back_ref, slot_ref, code_ref, part_ref, small_ref, live_ref, drag_ref, *refs):
    state_refs, (out_hbm, drag_hbm, out_ref, table_ref, sems) = refs[:4], refs[4:]
    stores = [pltpu.make_async_copy(drag_ref, drag_hbm, sems.at[0])]
    stores[0].start()

    def store(where):
        stores.append(pltpu.make_async_copy(out_ref.at[:, where], out_hbm.at[:, where], sems.at[len(stores)]))
        stores[-1].start()

    rows, slots = out_ref.shape
    parts = part_ref.shape[1]
    tiles = slot_ref.shape[1]
    migr = (slots - parts) // 4
    match = one_hot(iota((back_ref.shape[0], tiles), 0) == slot_ref[...])
    table_ref[...] = dot(back_ref[...], match, TN).astype(jnp.bfloat16)
    channels = part_ref.shape[0]
    damping = small_ref[rows : 2 * rows, channels : channels + 1]

    def look(code):
        values = dot(table_ref[...], ones(equal(tiles, code // TILE))).astype(jnp.bfloat16)
        hit = equal(TILE, code % TILE)
        found = []
        for r in range(rows):
            picked = jnp.where(hit, values[r * TILE : (r + 1) * TILE], jnp.bfloat16(0))
            while picked.shape[0] > 16:
                half = picked.shape[0] // 2
                picked = picked[:half] + picked[half:]
            found.append(jnp.sum(picked.astype(jnp.float32), axis=0, keepdims=True))
        return jnp.concatenate(found, axis=0)

    for begin in range(0, parts, CHUNK):
        where = slice(begin, begin + CHUNK)
        live = side_by_side(live_ref, 0, begin, CHUNK)
        out_ref[:, where] = live * (look(code_ref[:, where]) - damping * part_ref[:rows, where])
        store(where)
    drag = look(code_ref[:, parts:])
    for row, arrived in enumerate(arrived_blocks(state_refs)):
        begin = parts + row * migr
        live = jnp.concatenate([arrived[k : k + 1, migr:] for k in range(migr // LANES)], axis=1)
        force = drag[:, row * migr : (row + 1) * migr] - damping * arrived[:rows, :migr]
        out_ref[:, begin : begin + migr] = live * force
    store(slice(parts, slots))
    for copy in stores:
        copy.wait()


def call(kernel, shapes, *operands, limit=None, late=(), scratch=()):
    vmem, hbm = pl.BlockSpec(memory_space=pltpu.VMEM), pl.BlockSpec(memory_space=pltpu.HBM)
    return pl.pallas_call(
        kernel,
        out_shape=shapes,
        in_specs=[hbm if limit else vmem] * len(operands),
        out_specs=[hbm if limit or i in late else vmem for i in range(len(shapes))],
        scratch_shapes=scratch,
        compiler_params=pltpu.CompilerParams(vmem_limit_bytes=limit or VMEM),
    )(*operands)


def per_device(
    particles,
    migrant_index,
    migrant_count,
    migrated_slot_cell,
    source_tile_size,
    tile_owner,
    tile_offset,
    closure,
    damping,
):
    f32, bf16, i32 = jnp.float32, jnp.bfloat16, jnp.int32
    shape = jax.ShapeDtypeStruct
    channels, parts = particles.shape
    rows = closure.shape[0]
    migr = migrant_index.shape[1]
    slots = migrated_slot_cell.shape[0]
    tiles = source_tile_size.shape[1]
    devices = lax.axis_size("gx") * lax.axis_size("gy")
    capacity = max(2, 2 * tiles // devices)
    count = devices * capacity
    width = (rows + 1) * TILE
    lanes = (width + LANES) // LANES * LANES
    small_count = small_rows(rows, 4 * migr, slots)[-1]
    operands = (
        particles, migrant_index, migrant_count, source_tile_size, tile_owner.reshape(1, tiles),
        tile_offset.reshape(1, tiles), closure, damping.reshape(1, rows), migrated_slot_cell.reshape(1, slots),
    )
    *leaving, small = call(
        pick_kernel,
        [shape((channels, migr + LANES), bf16)] * 4 + [shape((small_count, GROUP), f32)],
        *operands, limit=LARGE,
        scratch=[(pltpu.SMEM if i == 2 else pltpu.VMEM)(x.shape, x.dtype) for i, x in enumerate(operands)]
        + [pltpu.VMEM((4, channels, migr + LANES), bf16), pltpu.VMEM((small_count, GROUP), f32),
           pltpu.SemaphoreType.DMA((9,)), pltpu.SemaphoreType.DMA((5,))],
    )
    (xa, xb), (ya, yb) = exchange(*leaving[:2], "gx"), exchange(*leaving[2:], "gy")
    arrived = yb, ya, xb, xa
    sums, code, slot, marks, live = call(
        functools.partial(deposit_kernel, capacity, rows, 4 * migr),
        [shape((width, tiles), f32), shape((1, slots), i32), shape((1, tiles), i32),
         shape((lanes - width, tiles), bf16), shape((parts // LANES, LANES), f32)],
        particles, small,
    )
    (payload,) = call(
        functools.partial(pack_kernel, rows), [shape((count, lanes), bf16)],
        sums, code, slot, marks, small, *arrived,
    )
    received = lax.all_to_all(
        payload.reshape(devices, capacity, lanes), ("gx", "gy"), split_axis=0, concat_axis=0, tiled=True
    ).reshape(count, lanes)
    grid, edge = shape((COLS, 2 * width), f32), shape((2 * FX, width), bf16)
    gas, xa, xb = call(place_kernel, [grid, edge, edge], received)
    xa, xb = exchange(xa, xb, "gx")
    along, ya, yb = call(along_kernel, [grid, edge, edge], gas, xb, xa)
    ya, yb = exchange(ya, yb, "gy")
    drag, back = call(
        drag_kernel,
        [shape((rows, FX, FY, FZ), bf16), shape((count, rows * TILE), bf16)],
        received[:, lanes - LANES :], along, yb, ya,
    )
    returned = lax.all_to_all(
        back.reshape(devices, capacity, rows * TILE), ("gx", "gy"), split_axis=0, concat_axis=0, tiled=True
    ).reshape(count, rows * TILE)
    force, drag = call(
        force_kernel, [shape((rows, slots), f32), shape(drag.shape, bf16)],
        returned, slot, code, particles, small, live, drag, *arrived, late=(0, 1),
        scratch=[pltpu.VMEM((rows, slots), f32), pltpu.VMEM((rows * TILE, tiles), bf16),
                 pltpu.SemaphoreType.DMA((2 + parts // CHUNK,))],
    )
    return drag, force


def solution(mesh):
    both = ("gx", "gy")
    in_specs = (
        P(None, both),
        P(both, None),
        P(both, None),
        P(both),
        P(both, None),
        P(both, None),
        P(both),
        P(),
        P(),
    )
    out_specs = (P(None, "gx", "gy", None), P(None, both))
    return jax.shard_map(
        per_device, mesh=mesh, in_specs=in_specs, out_specs=out_specs, check_vma=False
    )
```

```python
import functools

import jax
import jax.numpy as jnp
from jax import lax
from jax.experimental import pallas as pl
from jax.experimental.pallas import tpu as pltpu
from jax.sharding import PartitionSpec as P

TILE = 64
FX = 8
FY = 8
FZ = 128
COLS = FX * FY
LANES = 128
GROUP = 256
CHUNK = 2048
VMEM = 48 * 1024 * 1024
LARGE = 63 * 1024 * 1024

NT = (((1,), (1,)), ((), ()))
TN = (((0,), (0,)), ((), ()))


def iota(shape, dim):
    return lax.broadcasted_iota(jnp.int32, shape, dim)


def dot(a, b, dims=(((1,), (0,)), ((), ()))):
    return lax.dot_general(a, b, dims, preferred_element_type=jnp.float32)


def one_hot(mask):
    return jnp.where(mask, 1.0, 0.0).astype(jnp.bfloat16)


def equal(rows, row):
    numbers = iota((rows, row.shape[1]), 0).astype(jnp.float32).astype(jnp.bfloat16)
    return numbers == row.astype(jnp.float32).astype(jnp.bfloat16)


def ones(mask):
    return jnp.where(mask, jnp.bfloat16(1), jnp.bfloat16(0))


def fetch(sources, targets, sems):
    copies = [
        pltpu.make_async_copy(source, target, sems.at[i])
        for i, (source, target) in enumerate(zip(sources, targets))
    ]
    for copy in copies:
        copy.start()
    return copies


def is_even(axis):
    return lax.axis_index(axis) % 2 == 0


def exchange(block_a, block_b, axis):
    size = lax.axis_size(axis)
    blocks = {}
    for odd, block in ((1, block_b), (0, block_a)):
        pairs = [(i, (i + 1) % size if i % 2 == odd else (i - 1) % size) for i in range(size)]
        blocks[odd] = lax.ppermute(block, axis, pairs)
    return blocks[0], blocks[1]


def ordered(first, second, axis):
    even = is_even(axis)
    return jnp.where(even, second, first), jnp.where(even, first, second)


def leaving_row(index_ref, count_ref, parts):
    migr = index_ref.shape[1]
    lane = iota((1, migr), 1)
    odd = [jnp.where(is_even(axis), 0, 1) for axis in ("gx", "gy")]
    rows = []
    for row in (odd[0], 1 - odd[0], 2 + odd[1], 3 - odd[1]):
        rows.append(jnp.where(lane < count_ref[0, row], index_ref[pl.ds(row, 1), :], parts))
    return jnp.concatenate(rows, axis=1)


def arrived_blocks(refs):
    yb, xb, ya, xa = [ref[...].astype(jnp.float32) for ref in refs]
    return ordered(xa, xb, "gx") + ordered(ya, yb, "gy")


def small_rows(rows, leaving, slots):
    leave = 2 * rows
    cells = leave + leaving // GROUP
    return rows, leave, cells, cells + slots // GROUP


def pick_kernel(
    part_hbm, index_hbm, count_hbm, size_hbm, owner_hbm, offset_hbm, closure_hbm, damping_hbm, cell_hbm, *refs
):
    out_hbm, small_hbm, refs = refs[:4], refs[4], refs[5:]
    part_ref, index_ref, count_ref, size_ref, owner_ref, offset_ref = refs[:6]
    closure_ref, damping_ref, cell_ref, out_ref, small_ref, sems, out_sems = refs[6:]
    channels, parts = part_ref.shape
    migr = index_ref.shape[1]
    slots = cell_ref.shape[1]
    groups = parts // GROUP
    rows, width = closure_ref.shape
    closure_row, leave_row, cell_row, _ = small_rows(rows, 4 * migr, slots)
    copies = fetch(
        [index_hbm, count_hbm, part_hbm, size_hbm, owner_hbm, offset_hbm, closure_hbm, damping_hbm, cell_hbm],
        [index_ref, count_ref, part_ref, size_ref, owner_ref, offset_ref, closure_ref, damping_ref, cell_ref],
        sems,
    )
    copies[0].wait()
    copies[1].wait()
    leave = leaving_row(index_ref, count_ref, parts)
    high = leave // GROUP
    low = ones(equal(GROUP, leave % GROUP))
    for copy in copies[3:]:
        copy.wait()
    for row, ref in enumerate((size_ref, owner_ref, offset_ref)):
        small_ref[row : row + 1, :] = ref[...].astype(jnp.float32)
    small_ref[closure_row:leave_row, :width] = closure_ref[...]
    diagonal = iota((rows, rows), 0) == iota((rows, rows), 1)
    damping = jnp.sum(jnp.where(diagonal, damping_ref[...], 0.0), axis=1, keepdims=True)
    small_ref[closure_row:leave_row, width : width + 1] = damping
    for first, line in ((leave_row, leave), (cell_row, cell_ref[...])):
        for k in range(line.shape[1] // GROUP):
            part = line[:, k * GROUP : (k + 1) * GROUP]
            small_ref[first + k : first + k + 1, :] = part.astype(jnp.float32)
    stores = [pltpu.make_async_copy(small_ref, small_hbm, out_sems.at[4])]
    stores[0].start()
    copies[2].wait()
    table = jnp.concatenate(
        [part_ref[:, g * GROUP : (g + 1) * GROUP].astype(jnp.bfloat16) for g in range(groups)], axis=0
    )
    live = jnp.where(leave < parts, 1.0, 0.0)
    for r in range(4):
        where = slice(r * migr, (r + 1) * migr)
        found = dot(table, low[:, where])
        picked = jnp.zeros((channels, migr), jnp.float32)
        for g in range(groups):
            picked = jnp.where(high[:, where] == g, found[g * channels : (g + 1) * channels], picked)
        out_ref[r, :, :migr] = picked.astype(jnp.bfloat16)
        flags = [live[:, k : k + LANES] for k in range(r * migr, (r + 1) * migr, LANES)]
        flags.append(jnp.zeros((channels - len(flags), LANES), jnp.float32))
        out_ref[r, :, migr:] = jnp.concatenate(flags, axis=0).astype(jnp.bfloat16)
        stores.append(pltpu.make_async_copy(out_ref.at[r], out_hbm[r], out_sems.at[r]))
        stores[-1].start()
    for store in stores:
        store.wait()


def mix(closure, state):
    state = state.astype(jnp.float32)
    mixed = closure[:, 0:1] * state[0:1]
    for f in range(1, state.shape[0]):
        mixed = mixed + closure[:, f : f + 1] * state[f : f + 1]
    return mixed, state[0:1]


def side_by_side(ref, first, begin, width):
    lanes = ref.shape[1]
    first = first + begin // lanes
    rows = [ref[r : r + 1, :] for r in range(first, first + width // lanes)]
    return jnp.concatenate(rows, axis=1)


def spread(mixed, first, place):
    hit = equal(TILE, place)
    values = jnp.concatenate([mixed, first], axis=0).astype(jnp.bfloat16)
    return jnp.concatenate(
        [jnp.where(hit, values[r : r + 1], jnp.bfloat16(0)) for r in range(values.shape[0])], axis=0
    )


def deposit_kernel(
    capacity, rows, leaving, part_ref, small_ref, sum_ref, code_ref, slot_ref, mark_ref, live_ref
):
    channels, parts = part_ref.shape
    slots = code_ref.shape[1]
    tiles = slot_ref.shape[1]
    groups = parts // GROUP
    closure_row, leave_row, cell_row, _ = small_rows(rows, leaving, slots)
    closure = small_ref[closure_row:leave_row, :channels]

    leave = side_by_side(small_ref, leave_row, 0, leaving).astype(jnp.int32)
    halves = [leave[:, : leaving // 2], leave[:, leaving // 2 :]]
    high = jnp.concatenate([ones(equal(2 * groups, half // LANES)) for half in halves], axis=0)
    low = jnp.concatenate([ones(equal(LANES, half % LANES)) for half in halves], axis=0)
    hits = dot(high, low, NT)
    live_ref[...] = 1.0 - (hits[: 2 * groups, :LANES] + hits[2 * groups :, LANES:])

    sizes, owners, offset = [small_ref[r : r + 1, :] for r in range(3)]
    offset = offset.astype(jnp.int32)
    square = (tiles, tiles)
    below, across = iota(square, 0), iota(square, 1)
    inputs = [sizes, owners, (offset % FZ).astype(jnp.float32), jnp.zeros((5, tiles), jnp.float32)]
    inputs = jnp.concatenate(inputs, axis=0).astype(jnp.bfloat16)
    turned = dot(ones(below == across), inputs, NT)
    start = dot(ones(across < below), inputs, NT)[:, 0:1].astype(jnp.int32)
    height = turned[:, 2:3].astype(jnp.int32)
    code = iota((tiles, 1), 0) * TILE + (height - start) % TILE
    code_step = code - jnp.concatenate([jnp.zeros((1, 1), jnp.int32), code[: tiles - 1]], axis=0)
    earlier = ones((turned[:, 1:2] == owners) & (below < across))
    rank = dot(jnp.ones((8, tiles), jnp.bfloat16), earlier)[0:1]
    slot_ref[...] = (owners * capacity + rank).astype(jnp.int32)
    starts = jnp.broadcast_to(start.astype(jnp.int16), (tiles, CHUNK))
    steps = jnp.broadcast_to(code_step.astype(jnp.int16), (tiles, CHUNK))
    lines = iota(mark_ref.shape, 0)
    marks = jnp.where(lines == 0, offset // FZ, jnp.where(lines == 1, offset % FZ, 0))
    mark_ref[...] = marks.astype(jnp.float32).astype(jnp.bfloat16)

    def find(begin):
        cell = side_by_side(small_ref, cell_row, begin, CHUNK).astype(jnp.int32)
        found = jnp.where(cell.astype(jnp.int16) >= starts, steps, jnp.int16(0))
        while found.shape[0] > 16:
            half = found.shape[0] // 2
            found = found[:half] + found[half:]
        found = jnp.sum(found.astype(jnp.int32), axis=0, keepdims=True) & 0xFFFF
        return found // TILE, (found + cell) % TILE

    for begin in range(parts, slots, CHUNK):
        tile, place = find(begin)
        code_ref[:, begin : begin + CHUNK] = tile * TILE + place
    for begin in range(0, parts, CHUNK):
        tile, place = find(begin)
        code_ref[:, begin : begin + CHUNK] = tile * TILE + place
        live = side_by_side(live_ref, 0, begin, CHUNK)
        state = part_ref[:, begin : begin + CHUNK] * live
        mixed, first = mix(closure, state.astype(jnp.bfloat16))
        added = dot(spread(mixed, first, place), ones(equal(tiles, tile)), NT)
        total = added if begin == 0 else total + added
    sum_ref[...] = total


def pack_kernel(rows, sum_ref, code_ref, slot_ref, mark_ref, small_ref, *refs):
    state_refs, out_ref = refs[:4], refs[4]
    channels, tiles = state_refs[0].shape[0], slot_ref.shape[1]
    closure = small_ref[rows : 2 * rows, :channels]
    migr = state_refs[0].shape[1] - LANES
    code = code_ref[:, code_ref.shape[1] - 4 * migr :]
    state = jnp.concatenate([block[:, :migr] for block in arrived_blocks(state_refs)], axis=1)
    mixed, first = mix(closure, state)
    total = sum_ref[...] + dot(spread(mixed, first, code % TILE), ones(equal(tiles, code // TILE)), NT)
    table = jnp.concatenate([total.astype(jnp.bfloat16), mark_ref[...]], axis=0)
    match = one_hot(iota((out_ref.shape[0], tiles), 0) == slot_ref[...])
    out_ref[...] = dot(match, table, NT).astype(jnp.bfloat16)


def place_kernel(tile_ref, gas_ref, ya_ref, yb_ref):
    even = is_even("gy")
    count, lanes = tile_ref.shape
    width = gas_ref.shape[1] // 2
    marks = tile_ref[:, lanes - LANES :].astype(jnp.float32)
    column = marks[:, width % LANES : width % LANES + 1]
    height = marks[:, width % LANES + 1 : width % LANES + 2]
    lane = iota((1, LANES), 1)
    edge = jnp.where(lane < COLS + FX, (lane - COLS) * FY, (lane - COLS - FX) * FY + FY - 1)
    target = jnp.where(lane < COLS, lane, jnp.where(lane < COLS + 2 * FX, edge, -1))
    hot = one_hot(column == target.astype(jnp.float32))
    place = (iota((1, width), 1) % TILE).astype(jnp.float32)
    values = tile_ref[:, :width].astype(jnp.float32)
    for half, mask in enumerate((place >= height, place < height)):
        total = dot(hot, jnp.where(mask, values, 0.0).astype(jnp.bfloat16), TN)
        where = slice(half * width, (half + 1) * width)
        gas_ref[:, where] = total[:COLS]
        rows = slice(half * FX, (half + 1) * FX)
        low, high = total[COLS : COLS + FX], total[COLS + FX : COLS + 2 * FX]
        ya_ref[rows, :] = jnp.where(even, high, low).astype(jnp.bfloat16)
        yb_ref[rows, :] = jnp.where(even, low, high).astype(jnp.bfloat16)


def unfold(ref):
    edge = ref[...].astype(jnp.float32)
    half = edge.shape[0] // 2
    return jnp.concatenate([edge[:half], edge[half:]], axis=1)


def along_kernel(gas_ref, yb_ref, ya_ref, out_ref, xa_ref, xb_ref):
    before, after = ordered(unfold(ya_ref), unfold(yb_ref), "gy")
    along = []
    for x in range(FX):
        block = gas_ref[x * FY : (x + 1) * FY, :]
        padded = jnp.concatenate([before[x : x + 1], block, after[x : x + 1]], axis=0)
        along.append(padded[0:FY] + 2.0 * block + padded[2 : FY + 2])
        out_ref[x * FY : (x + 1) * FY, :] = along[x]
    width = xa_ref.shape[1]
    low, high = [jnp.concatenate([along[x][:, :width], along[x][:, width:]], axis=0) for x in (0, FX - 1)]
    even = is_even("gx")
    xa_ref[...] = jnp.where(even, high, low).astype(jnp.bfloat16)
    xb_ref[...] = jnp.where(even, low, high).astype(jnp.bfloat16)


def drag_kernel(mark_ref, along_ref, xb_ref, xa_ref, drag_ref, back_ref):
    rows = drag_ref.shape[0]
    width = along_ref.shape[1] // 2
    lanes = rows * TILE
    first, last = ordered(unfold(xa_ref), unfold(xb_ref), "gx")
    blocks = [first] + [along_ref[x * FY : (x + 1) * FY, :] for x in range(FX)] + [last]
    smooth = [(blocks[x] + 2.0 * blocks[x + 1] + blocks[x + 2]) / 16.0 for x in range(FX)]
    smooth = jnp.concatenate(smooth, axis=0)
    halves = []
    for half in range(2):
        base = half * width
        density = smooth[:, base + lanes : base + lanes + TILE]
        scale = 1.0 / (1.0 + density * density)
        halves.append(smooth[:, base : base + lanes] * jnp.concatenate([scale] * rows, axis=1))
    for r in range(rows):
        where = slice(r * TILE, (r + 1) * TILE)
        both = jnp.concatenate([halves[0][:, where], halves[1][:, where]], axis=1)
        drag_ref[r] = both.reshape(FX, FY, FZ).astype(jnp.bfloat16)
    mark = width % LANES
    marks = mark_ref[...].astype(jnp.float32)
    column, height = marks[:, mark : mark + 1], marks[:, mark + 1 : mark + 2]
    hot = one_hot(column == iota((1, COLS), 1).astype(jnp.float32))
    place = (iota((1, lanes), 1) % TILE).astype(jnp.float32)
    low = dot(hot, halves[0].astype(jnp.bfloat16))
    high = dot(hot, halves[1].astype(jnp.bfloat16))
    back_ref[...] = jnp.where(place >= height, low, high).astype(jnp.bfloat16)


def force_kernel(back_ref, slot_ref, code_ref, part_ref, small_ref, live_ref, drag_ref, *refs):
    state_refs, (out_hbm, drag_hbm, out_ref, table_ref, sems) = refs[:4], refs[4:]
    stores = [pltpu.make_async_copy(drag_ref, drag_hbm, sems.at[0])]
    stores[0].start()

    def store(where):
        stores.append(pltpu.make_async_copy(out_ref.at[:, where], out_hbm.at[:, where], sems.at[len(stores)]))
        stores[-1].start()

    rows, slots = out_ref.shape
    parts = part_ref.shape[1]
    tiles = slot_ref.shape[1]
    migr = (slots - parts) // 4
    match = one_hot(iota((back_ref.shape[0], tiles), 0) == slot_ref[...])
    table_ref[...] = dot(back_ref[...], match, TN).astype(jnp.bfloat16)
    channels = part_ref.shape[0]
    damping = small_ref[rows : 2 * rows, channels : channels + 1]

    def look(code):
        values = dot(table_ref[...], ones(equal(tiles, code // TILE))).astype(jnp.bfloat16)
        hit = equal(TILE, code % TILE)
        found = []
        for r in range(rows):
            picked = jnp.where(hit, values[r * TILE : (r + 1) * TILE], jnp.bfloat16(0))
            while picked.shape[0] > 16:
                half = picked.shape[0] // 2
                picked = picked[:half] + picked[half:]
            found.append(jnp.sum(picked.astype(jnp.float32), axis=0, keepdims=True))
        return jnp.concatenate(found, axis=0)

    for begin in range(0, parts, CHUNK):
        where = slice(begin, begin + CHUNK)
        live = side_by_side(live_ref, 0, begin, CHUNK)
        out_ref[:, where] = live * (look(code_ref[:, where]) - damping * part_ref[:rows, where])
        store(where)
    drag = look(code_ref[:, parts:])
    for row, arrived in enumerate(arrived_blocks(state_refs)):
        begin = parts + row * migr
        live = jnp.concatenate([arrived[k : k + 1, migr:] for k in range(migr // LANES)], axis=1)
        force = drag[:, row * migr : (row + 1) * migr] - damping * arrived[:rows, :migr]
        out_ref[:, begin : begin + migr] = live * force
    store(slice(parts, slots))
    for copy in stores:
        copy.wait()


def call(kernel, shapes, *operands, limit=None, late=(), scratch=()):
    vmem, hbm = pl.BlockSpec(memory_space=pltpu.VMEM), pl.BlockSpec(memory_space=pltpu.HBM)
    return pl.pallas_call(
        kernel,
        out_shape=shapes,
        in_specs=[hbm if limit else vmem] * len(operands),
        out_specs=[hbm if limit or i in late else vmem for i in range(len(shapes))],
        scratch_shapes=scratch,
        compiler_params=pltpu.CompilerParams(vmem_limit_bytes=limit or VMEM),
    )(*operands)


def per_device(
    particles,
    migrant_index,
    migrant_count,
    migrated_slot_cell,
    source_tile_size,
    tile_owner,
    tile_offset,
    closure,
    damping,
):
    f32, bf16, i32 = jnp.float32, jnp.bfloat16, jnp.int32
    shape = jax.ShapeDtypeStruct
    channels, parts = particles.shape
    rows = closure.shape[0]
    migr = migrant_index.shape[1]
    slots = migrated_slot_cell.shape[0]
    tiles = source_tile_size.shape[1]
    devices = lax.axis_size("gx") * lax.axis_size("gy")
    capacity = max(2, 2 * tiles // devices)
    count = devices * capacity
    width = (rows + 1) * TILE
    lanes = (width + LANES) // LANES * LANES
    small_count = small_rows(rows, 4 * migr, slots)[-1]
    operands = (
        particles, migrant_index, migrant_count, source_tile_size, tile_owner.reshape(1, tiles),
        tile_offset.reshape(1, tiles), closure, damping.reshape(1, rows), migrated_slot_cell.reshape(1, slots),
    )
    *leaving, small = call(
        pick_kernel,
        [shape((channels, migr + LANES), bf16)] * 4 + [shape((small_count, GROUP), f32)],
        *operands, limit=LARGE,
        scratch=[(pltpu.SMEM if i == 2 else pltpu.VMEM)(x.shape, x.dtype) for i, x in enumerate(operands)]
        + [pltpu.VMEM((4, channels, migr + LANES), bf16), pltpu.VMEM((small_count, GROUP), f32),
           pltpu.SemaphoreType.DMA((9,)), pltpu.SemaphoreType.DMA((5,))],
    )
    (xa, xb), (ya, yb) = exchange(*leaving[:2], "gx"), exchange(*leaving[2:], "gy")
    arrived = yb, xb, ya, xa
    sums, code, slot, marks, live = call(
        functools.partial(deposit_kernel, capacity, rows, 4 * migr),
        [shape((width, tiles), f32), shape((1, slots), i32), shape((1, tiles), i32),
         shape((lanes - width, tiles), bf16), shape((parts // LANES, LANES), f32)],
        particles, small,
    )
    (payload,) = call(
        functools.partial(pack_kernel, rows), [shape((count, lanes), bf16)],
        sums, code, slot, marks, small, *arrived,
    )
    received = lax.all_to_all(
        payload.reshape(devices, capacity, lanes), ("gx", "gy"), split_axis=0, concat_axis=0, tiled=True
    ).reshape(count, lanes)
    grid, edge = shape((COLS, 2 * width), f32), shape((2 * FX, width), bf16)
    gas, ya, yb = call(place_kernel, [grid, edge, edge], received)
    ya, yb = exchange(ya, yb, "gy")
    along, xa, xb = call(along_kernel, [grid, edge, edge], gas, yb, ya)
    xa, xb = exchange(xa, xb, "gx")
    drag, back = call(
        drag_kernel,
        [shape((rows, FX, FY, FZ), bf16), shape((count, rows * TILE), bf16)],
        received[:, lanes - LANES :], along, xb, xa,
    )
    returned = lax.all_to_all(
        back.reshape(devices, capacity, rows * TILE), ("gx", "gy"), split_axis=0, concat_axis=0, tiled=True
    ).reshape(count, rows * TILE)
    force, drag = call(
        force_kernel, [shape((rows, slots), f32), shape(drag.shape, bf16)],
        returned, slot, code, particles, small, live, drag, *arrived, late=(0, 1),
        scratch=[pltpu.VMEM((rows, slots), f32), pltpu.VMEM((rows * TILE, tiles), bf16),
                 pltpu.SemaphoreType.DMA((2 + parts // CHUNK,))],
    )
    return drag, force


def solution(mesh):
    both = ("gx", "gy")
    in_specs = (
        P(None, both),
        P(both, None),
        P(both, None),
        P(both),
        P(both, None),
        P(both, None),
        P(both),
        P(),
        P(),
    )
    out_specs = (P(None, "gx", "gy", None), P(None, both))
    return jax.shard_map(
        per_device, mesh=mesh, in_specs=in_specs, out_specs=out_specs, check_vma=False
    )
```

```python
import functools

import jax
import jax.numpy as jnp
from jax import lax
from jax.experimental import pallas as pl
from jax.experimental.pallas import tpu as pltpu
from jax.sharding import PartitionSpec as P

FREE = 32.0
TILE = 64
FX = 8
FY = 8
FZ = 128
COLS = FX * FY
LANES = 128
GROUP = 256
CHUNK = 2048
VMEM = 48 * 1024 * 1024
LARGE = 63 * 1024 * 1024

NT = (((1,), (1,)), ((), ()))
TN = (((0,), (0,)), ((), ()))


def iota(shape, dim):
    return lax.broadcasted_iota(jnp.int32, shape, dim)


def dot(a, b, dims=(((1,), (0,)), ((), ()))):
    return lax.dot_general(a, b, dims, preferred_element_type=jnp.float32)


def one_hot(mask):
    return jnp.where(mask, 1.0, 0.0).astype(jnp.bfloat16)


def equal(rows, row):
    numbers = iota((rows, row.shape[1]), 0).astype(jnp.float32).astype(jnp.bfloat16)
    return numbers == row.astype(jnp.float32).astype(jnp.bfloat16)


def ones(mask):
    return jnp.where(mask, jnp.bfloat16(1), jnp.bfloat16(0))


def fetch(sources, targets, sems):
    copies = [
        pltpu.make_async_copy(source, target, sems.at[i])
        for i, (source, target) in enumerate(zip(sources, targets))
    ]
    for copy in copies:
        copy.start()
    return copies


def is_even(axis):
    return lax.axis_index(axis) % 2 == 0


def exchange(block_a, block_b, axis):
    size = lax.axis_size(axis)
    blocks = {}
    for odd, block in ((1, block_b), (0, block_a)):
        pairs = [(i, (i + 1) % size if i % 2 == odd else (i - 1) % size) for i in range(size)]
        blocks[odd] = lax.ppermute(block, axis, pairs)
    return blocks[0], blocks[1]


def ordered(first, second, axis):
    even = is_even(axis)
    return jnp.where(even, second, first), jnp.where(even, first, second)


def leaving_row(index_ref, count_ref, parts):
    migr = index_ref.shape[1]
    lane = iota((1, migr), 1)
    odd = [jnp.where(is_even(axis), 0, 1) for axis in ("gx", "gy")]
    rows = []
    for row in (odd[0], 1 - odd[0], 2 + odd[1], 3 - odd[1]):
        rows.append(jnp.where(lane < count_ref[0, row], index_ref[pl.ds(row, 1), :], parts))
    return jnp.concatenate(rows, axis=1)


def arrived_blocks(refs):
    yb, xb, ya, xa = [ref[...].astype(jnp.float32) for ref in refs]
    return ordered(xa, xb, "gx") + ordered(ya, yb, "gy")


def small_rows(rows, leaving, slots):
    leave = 2 * rows
    cells = leave + leaving // GROUP
    return rows, leave, cells, cells + slots // GROUP


def pick_kernel(
    part_hbm, index_hbm, count_hbm, size_hbm, owner_hbm, offset_hbm, closure_hbm, damping_hbm, cell_hbm, *refs
):
    out_hbm, small_hbm, refs = refs[:4], refs[4], refs[5:]
    part_ref, index_ref, count_ref, size_ref, owner_ref, offset_ref = refs[:6]
    closure_ref, damping_ref, cell_ref, out_ref, small_ref, sems, out_sems = refs[6:]
    channels, parts = part_ref.shape
    migr = index_ref.shape[1]
    slots = cell_ref.shape[1]
    groups = parts // GROUP
    rows, width = closure_ref.shape
    closure_row, leave_row, cell_row, _ = small_rows(rows, 4 * migr, slots)
    copies = fetch(
        [index_hbm, count_hbm, part_hbm, size_hbm, owner_hbm, offset_hbm, closure_hbm, damping_hbm, cell_hbm],
        [index_ref, count_ref, part_ref, size_ref, owner_ref, offset_ref, closure_ref, damping_ref, cell_ref],
        sems,
    )
    copies[0].wait()
    copies[1].wait()
    leave = leaving_row(index_ref, count_ref, parts)
    high = leave // GROUP
    low = ones(equal(GROUP, leave % GROUP))
    for copy in copies[3:]:
        copy.wait()
    for row, ref in enumerate((size_ref, owner_ref, offset_ref)):
        small_ref[row : row + 1, :] = ref[...].astype(jnp.float32)
    small_ref[closure_row:leave_row, :width] = closure_ref[...]
    diagonal = iota((rows, rows), 0) == iota((rows, rows), 1)
    damping = jnp.sum(jnp.where(diagonal, damping_ref[...], 0.0), axis=1, keepdims=True)
    small_ref[closure_row:leave_row, width : width + 1] = damping
    for first, line in ((leave_row, leave), (cell_row, cell_ref[...])):
        for k in range(line.shape[1] // GROUP):
            part = line[:, k * GROUP : (k + 1) * GROUP]
            small_ref[first + k : first + k + 1, :] = part.astype(jnp.float32)
    stores = [pltpu.make_async_copy(small_ref, small_hbm, out_sems.at[4])]
    stores[0].start()
    copies[2].wait()
    table = jnp.concatenate(
        [part_ref[:, g * GROUP : (g + 1) * GROUP].astype(jnp.bfloat16) for g in range(groups)], axis=0
    )
    free = jnp.where(iota((channels, migr), 0) == 0, FREE, 0.0)
    for r in range(4):
        where = slice(r * migr, (r + 1) * migr)
        found = dot(table, low[:, where])
        picked = free
        for g in range(groups):
            picked = jnp.where(high[:, where] == g, found[g * channels : (g + 1) * channels], picked)
        out_ref[r] = picked.astype(jnp.bfloat16)
        stores.append(pltpu.make_async_copy(out_ref.at[r], out_hbm[r], out_sems.at[r]))
        stores[-1].start()
    for store in stores:
        store.wait()


def mix(closure, state):
    state = state.astype(jnp.float32)
    mixed = closure[:, 0:1] * state[0:1]
    for f in range(1, state.shape[0]):
        mixed = mixed + closure[:, f : f + 1] * state[f : f + 1]
    return mixed, state[0:1]


def side_by_side(ref, first, begin, width):
    lanes = ref.shape[1]
    first = first + begin // lanes
    rows = [ref[r : r + 1, :] for r in range(first, first + width // lanes)]
    return jnp.concatenate(rows, axis=1)


def spread(mixed, first, place):
    hit = equal(TILE, place)
    values = jnp.concatenate([mixed, first], axis=0).astype(jnp.bfloat16)
    return jnp.concatenate(
        [jnp.where(hit, values[r : r + 1], jnp.bfloat16(0)) for r in range(values.shape[0])], axis=0
    )


def deposit_kernel(
    capacity, rows, leaving, part_ref, small_ref, sum_ref, code_ref, slot_ref, mark_ref, live_ref
):
    channels, parts = part_ref.shape
    slots = code_ref.shape[1]
    tiles = slot_ref.shape[1]
    groups = parts // GROUP
    closure_row, leave_row, cell_row, _ = small_rows(rows, leaving, slots)
    closure = small_ref[closure_row:leave_row, :channels]

    leave = side_by_side(small_ref, leave_row, 0, leaving).astype(jnp.int32)
    halves = [leave[:, : leaving // 2], leave[:, leaving // 2 :]]
    high = jnp.concatenate([ones(equal(2 * groups, half // LANES)) for half in halves], axis=0)
    low = jnp.concatenate([ones(equal(LANES, half % LANES)) for half in halves], axis=0)
    hits = dot(high, low, NT)
    live_ref[...] = 1.0 - (hits[: 2 * groups, :LANES] + hits[2 * groups :, LANES:])

    sizes, owners, offset = [small_ref[r : r + 1, :] for r in range(3)]
    offset = offset.astype(jnp.int32)
    square = (tiles, tiles)
    below, across = iota(square, 0), iota(square, 1)
    inputs = [sizes, owners, (offset % FZ).astype(jnp.float32), jnp.zeros((5, tiles), jnp.float32)]
    inputs = jnp.concatenate(inputs, axis=0).astype(jnp.bfloat16)
    turned = dot(ones(below == across), inputs, NT)
    start = dot(ones(across < below), inputs, NT)[:, 0:1].astype(jnp.int32)
    height = turned[:, 2:3].astype(jnp.int32)
    code = iota((tiles, 1), 0) * TILE + (height - start) % TILE
    code_step = code - jnp.concatenate([jnp.zeros((1, 1), jnp.int32), code[: tiles - 1]], axis=0)
    earlier = ones((turned[:, 1:2] == owners) & (below < across))
    rank = dot(jnp.ones((8, tiles), jnp.bfloat16), earlier)[0:1]
    slot_ref[...] = (owners * capacity + rank).astype(jnp.int32)
    starts = jnp.broadcast_to(start.astype(jnp.int16), (tiles, CHUNK))
    steps = jnp.broadcast_to(code_step.astype(jnp.int16), (tiles, CHUNK))
    lines = iota(mark_ref.shape, 0)
    marks = jnp.where(lines == 0, offset // FZ, jnp.where(lines == 1, offset % FZ, 0))
    mark_ref[...] = marks.astype(jnp.float32).astype(jnp.bfloat16)

    def find(begin):
        cell = side_by_side(small_ref, cell_row, begin, CHUNK).astype(jnp.int32)
        found = jnp.where(cell.astype(jnp.int16) >= starts, steps, jnp.int16(0))
        while found.shape[0] > 16:
            half = found.shape[0] // 2
            found = found[:half] + found[half:]
        found = jnp.sum(found.astype(jnp.int32), axis=0, keepdims=True) & 0xFFFF
        return found // TILE, (found + cell) % TILE

    for begin in range(parts, slots, CHUNK):
        tile, place = find(begin)
        code_ref[:, begin : begin + CHUNK] = tile * TILE + place
    for begin in range(0, parts, CHUNK):
        tile, place = find(begin)
        code_ref[:, begin : begin + CHUNK] = tile * TILE + place
        live = side_by_side(live_ref, 0, begin, CHUNK)
        state = part_ref[:, begin : begin + CHUNK] * live
        mixed, first = mix(closure, state.astype(jnp.bfloat16))
        added = dot(spread(mixed, first, place), ones(equal(tiles, tile)), NT)
        total = added if begin == 0 else total + added
    sum_ref[...] = total


def pack_kernel(rows, sum_ref, code_ref, slot_ref, mark_ref, small_ref, *refs):
    state_refs, out_ref = refs[:4], refs[4]
    channels, tiles = state_refs[0].shape[0], slot_ref.shape[1]
    closure = small_ref[rows : 2 * rows, :channels]
    code = code_ref[:, code_ref.shape[1] - 4 * state_refs[0].shape[1] :]
    state = jnp.concatenate(arrived_blocks(state_refs), axis=1)
    state = jnp.where(state[0:1] < FREE, state, 0.0)
    mixed, first = mix(closure, state)
    total = sum_ref[...] + dot(spread(mixed, first, code % TILE), ones(equal(tiles, code // TILE)), NT)
    table = jnp.concatenate([total.astype(jnp.bfloat16), mark_ref[...]], axis=0)
    match = one_hot(iota((out_ref.shape[0], tiles), 0) == slot_ref[...])
    out_ref[...] = dot(match, table, NT).astype(jnp.bfloat16)


def place_kernel(tile_ref, gas_ref, xa_ref, xb_ref):
    even = is_even("gx")
    count, lanes = tile_ref.shape
    width = gas_ref.shape[1] // 2
    marks = tile_ref[:, lanes - LANES :].astype(jnp.float32)
    column = marks[:, width % LANES : width % LANES + 1]
    height = marks[:, width % LANES + 1 : width % LANES + 2]
    lane = iota((1, LANES), 1)
    hot = one_hot(column == lane.astype(jnp.float32))
    place = (iota((1, width), 1) % TILE).astype(jnp.float32)
    values = tile_ref[:, :width].astype(jnp.float32)
    for half, mask in enumerate((place >= height, place < height)):
        total = dot(hot, jnp.where(mask, values, 0.0).astype(jnp.bfloat16), TN)
        where = slice(half * width, (half + 1) * width)
        gas_ref[:, where] = total[:COLS]
        rows = slice(half * FY, (half + 1) * FY)
        low, high = total[:FY], total[COLS - FY : COLS]
        xa_ref[rows, :] = jnp.where(even, high, low).astype(jnp.bfloat16)
        xb_ref[rows, :] = jnp.where(even, low, high).astype(jnp.bfloat16)


def unfold(ref):
    edge = ref[...].astype(jnp.float32)
    half = edge.shape[0] // 2
    return jnp.concatenate([edge[:half], edge[half:]], axis=1)


def along_kernel(gas_ref, xb_ref, xa_ref, out_ref, ya_ref, yb_ref):
    before, after = ordered(unfold(xa_ref), unfold(xb_ref), "gx")
    blocks = [before] + [gas_ref[x * FY : (x + 1) * FY, :] for x in range(FX)] + [after]
    along = [blocks[x] + 2.0 * blocks[x + 1] + blocks[x + 2] for x in range(FX)]
    for x in range(FX):
        out_ref[x * FY : (x + 1) * FY, :] = along[x]
    width = ya_ref.shape[1]
    edges = []
    for row in (0, FY - 1):
        edge = jnp.concatenate([along[x][row : row + 1] for x in range(FX)], axis=0)
        edges.append(jnp.concatenate([edge[:, :width], edge[:, width:]], axis=0))
    even = is_even("gy")
    ya_ref[...] = jnp.where(even, edges[1], edges[0]).astype(jnp.bfloat16)
    yb_ref[...] = jnp.where(even, edges[0], edges[1]).astype(jnp.bfloat16)


def drag_kernel(mark_ref, along_ref, yb_ref, ya_ref, drag_ref, back_ref):
    rows = drag_ref.shape[0]
    width = along_ref.shape[1] // 2
    lanes = rows * TILE
    before, after = ordered(unfold(ya_ref), unfold(yb_ref), "gy")
    smooth = []
    for x in range(FX):
        block = along_ref[x * FY : (x + 1) * FY, :]
        padded = jnp.concatenate([before[x : x + 1], block, after[x : x + 1]], axis=0)
        smooth.append((padded[0:FY] + 2.0 * block + padded[2 : FY + 2]) / 16.0)
    smooth = jnp.concatenate(smooth, axis=0)
    halves = []
    for half in range(2):
        base = half * width
        density = smooth[:, base + lanes : base + lanes + TILE]
        scale = 1.0 / (1.0 + density * density)
        halves.append(smooth[:, base : base + lanes] * jnp.concatenate([scale] * rows, axis=1))
    for r in range(rows):
        where = slice(r * TILE, (r + 1) * TILE)
        both = jnp.concatenate([halves[0][:, where], halves[1][:, where]], axis=1)
        drag_ref[r] = both.reshape(FX, FY, FZ).astype(jnp.bfloat16)
    mark = width % LANES
    marks = mark_ref[...].astype(jnp.float32)
    column, height = marks[:, mark : mark + 1], marks[:, mark + 1 : mark + 2]
    hot = one_hot(column == iota((1, COLS), 1).astype(jnp.float32))
    place = (iota((1, lanes), 1) % TILE).astype(jnp.float32)
    low = dot(hot, halves[0].astype(jnp.bfloat16))
    high = dot(hot, halves[1].astype(jnp.bfloat16))
    back_ref[...] = jnp.where(place >= height, low, high).astype(jnp.bfloat16)


def force_kernel(back_ref, slot_ref, code_ref, part_ref, small_ref, live_ref, drag_ref, *refs):
    state_refs, (out_hbm, drag_hbm, out_ref, table_ref, sems) = refs[:4], refs[4:]
    stores = [pltpu.make_async_copy(drag_ref, drag_hbm, sems.at[0])]
    stores[0].start()

    def store(where):
        stores.append(pltpu.make_async_copy(out_ref.at[:, where], out_hbm.at[:, where], sems.at[len(stores)]))
        stores[-1].start()

    rows, slots = out_ref.shape
    parts = part_ref.shape[1]
    tiles = slot_ref.shape[1]
    migr = (slots - parts) // 4
    match = one_hot(iota((back_ref.shape[0], tiles), 0) == slot_ref[...])
    table_ref[...] = dot(back_ref[...], match, TN).astype(jnp.bfloat16)
    channels = part_ref.shape[0]
    damping = small_ref[rows : 2 * rows, channels : channels + 1]

    def look(code):
        values = dot(table_ref[...], ones(equal(tiles, code // TILE))).astype(jnp.bfloat16)
        hit = equal(TILE, code % TILE)
        found = []
        for r in range(rows):
            picked = jnp.where(hit, values[r * TILE : (r + 1) * TILE], jnp.bfloat16(0))
            while picked.shape[0] > 16:
                half = picked.shape[0] // 2
                picked = picked[:half] + picked[half:]
            found.append(jnp.sum(picked.astype(jnp.float32), axis=0, keepdims=True))
        return jnp.concatenate(found, axis=0)

    for begin in range(0, parts, CHUNK):
        where = slice(begin, begin + CHUNK)
        live = side_by_side(live_ref, 0, begin, CHUNK)
        out_ref[:, where] = live * (look(code_ref[:, where]) - damping * part_ref[:rows, where])
        store(where)
    drag = look(code_ref[:, parts:])
    for row, arrived in enumerate(arrived_blocks(state_refs)):
        begin = parts + row * migr
        live = jnp.where(arrived[0:1] < FREE, 1.0, 0.0)
        force = drag[:, row * migr : (row + 1) * migr] - damping * arrived[:rows]
        out_ref[:, begin : begin + migr] = live * force
    store(slice(parts, slots))
    for copy in stores:
        copy.wait()


def call(kernel, shapes, *operands, limit=None, late=(), scratch=()):
    vmem, hbm = pl.BlockSpec(memory_space=pltpu.VMEM), pl.BlockSpec(memory_space=pltpu.HBM)
    return pl.pallas_call(
        kernel,
        out_shape=shapes,
        in_specs=[hbm if limit else vmem] * len(operands),
        out_specs=[hbm if limit or i in late else vmem for i in range(len(shapes))],
        scratch_shapes=scratch,
        compiler_params=pltpu.CompilerParams(vmem_limit_bytes=limit or VMEM),
    )(*operands)


def per_device(
    particles,
    migrant_index,
    migrant_count,
    migrated_slot_cell,
    source_tile_size,
    tile_owner,
    tile_offset,
    closure,
    damping,
):
    f32, bf16, i32 = jnp.float32, jnp.bfloat16, jnp.int32
    shape = jax.ShapeDtypeStruct
    channels, parts = particles.shape
    rows = closure.shape[0]
    migr = migrant_index.shape[1]
    slots = migrated_slot_cell.shape[0]
    tiles = source_tile_size.shape[1]
    devices = lax.axis_size("gx") * lax.axis_size("gy")
    capacity = max(2, 2 * tiles // devices)
    count = devices * capacity
    width = (rows + 1) * TILE
    lanes = (width + LANES) // LANES * LANES
    small_count = small_rows(rows, 4 * migr, slots)[-1]
    operands = (
        particles, migrant_index, migrant_count, source_tile_size, tile_owner.reshape(1, tiles),
        tile_offset.reshape(1, tiles), closure, damping.reshape(1, rows), migrated_slot_cell.reshape(1, slots),
    )
    *leaving, small = call(
        pick_kernel,
        [shape((channels, migr), bf16)] * 4 + [shape((small_count, GROUP), f32)],
        *operands, limit=LARGE,
        scratch=[(pltpu.SMEM if i == 2 else pltpu.VMEM)(x.shape, x.dtype) for i, x in enumerate(operands)]
        + [pltpu.VMEM((4, channels, migr), bf16), pltpu.VMEM((small_count, GROUP), f32),
           pltpu.SemaphoreType.DMA((9,)), pltpu.SemaphoreType.DMA((5,))],
    )
    (xa, xb), (ya, yb) = exchange(*leaving[:2], "gx"), exchange(*leaving[2:], "gy")
    arrived = yb, xb, ya, xa
    sums, code, slot, marks, live = call(
        functools.partial(deposit_kernel, capacity, rows, 4 * migr),
        [shape((width, tiles), f32), shape((1, slots), i32), shape((1, tiles), i32),
         shape((lanes - width, tiles), bf16), shape((parts // LANES, LANES), f32)],
        particles, small,
    )
    (payload,) = call(
        functools.partial(pack_kernel, rows), [shape((count, lanes), bf16)],
        sums, code, slot, marks, small, *arrived,
    )
    received = lax.all_to_all(
        payload.reshape(devices, capacity, lanes), ("gx", "gy"), split_axis=0, concat_axis=0, tiled=True
    ).reshape(count, lanes)
    grid, edge = shape((COLS, 2 * width), f32), shape((2 * FX, width), bf16)
    gas, xa, xb = call(place_kernel, [grid, edge, edge], received)
    xa, xb = exchange(xa, xb, "gx")
    along, ya, yb = call(along_kernel, [grid, edge, edge], gas, xb, xa)
    ya, yb = exchange(ya, yb, "gy")
    drag, back = call(
        drag_kernel,
        [shape((rows, FX, FY, FZ), bf16), shape((count, rows * TILE), bf16)],
        received[:, lanes - LANES :], along, yb, ya,
    )
    returned = lax.all_to_all(
        back.reshape(devices, capacity, rows * TILE), ("gx", "gy"), split_axis=0, concat_axis=0, tiled=True
    ).reshape(count, rows * TILE)
    force, drag = call(
        force_kernel, [shape((rows, slots), f32), shape(drag.shape, bf16)],
        returned, slot, code, particles, small, live, drag, *arrived, late=(0, 1),
        scratch=[pltpu.VMEM((rows, slots), f32), pltpu.VMEM((rows * TILE, tiles), bf16),
                 pltpu.SemaphoreType.DMA((2 + parts // CHUNK,))],
    )
    return drag, force


def solution(mesh):
    both = ("gx", "gy")
    in_specs = (
        P(None, both),
        P(both, None),
        P(both, None),
        P(both),
        P(both, None),
        P(both, None),
        P(both),
        P(),
        P(),
    )
    out_specs = (P(None, "gx", "gy", None), P(None, both))
    return jax.shard_map(
        per_device, mesh=mesh, in_specs=in_specs, out_specs=out_specs, check_vma=False
    )
```

```python
import functools

import jax
import jax.numpy as jnp
from jax import lax
from jax.experimental import pallas as pl
from jax.experimental.pallas import tpu as pltpu
from jax.sharding import PartitionSpec as P

FREE = 32.0
TILE = 64
FX = 8
FY = 8
FZ = 128
COLS = FX * FY
LANES = 128
GROUP = 256
CHUNK = 2048
VMEM = 48 * 1024 * 1024
LARGE = 63 * 1024 * 1024

NT = (((1,), (1,)), ((), ()))
TN = (((0,), (0,)), ((), ()))


def iota(shape, dim):
    return lax.broadcasted_iota(jnp.int32, shape, dim)


def dot(a, b, dims=(((1,), (0,)), ((), ()))):
    return lax.dot_general(a, b, dims, preferred_element_type=jnp.float32)


def one_hot(mask):
    return jnp.where(mask, 1.0, 0.0).astype(jnp.bfloat16)


def equal(rows, row):
    numbers = iota((rows, row.shape[1]), 0).astype(jnp.float32).astype(jnp.bfloat16)
    return numbers == row.astype(jnp.float32).astype(jnp.bfloat16)


def ones(mask):
    return jnp.where(mask, jnp.bfloat16(1), jnp.bfloat16(0))


def fetch(sources, targets, sems):
    copies = [
        pltpu.make_async_copy(source, target, sems.at[i])
        for i, (source, target) in enumerate(zip(sources, targets))
    ]
    for copy in copies:
        copy.start()
    return copies


def is_even(axis):
    return lax.axis_index(axis) % 2 == 0


def exchange(block_a, block_b, axis):
    size = lax.axis_size(axis)
    blocks = {}
    for odd, block in ((1, block_b), (0, block_a)):
        pairs = [(i, (i + 1) % size if i % 2 == odd else (i - 1) % size) for i in range(size)]
        blocks[odd] = lax.ppermute(block, axis, pairs)
    return blocks[0], blocks[1]


def ordered(first, second, axis):
    even = is_even(axis)
    return jnp.where(even, second, first), jnp.where(even, first, second)


def leaving_row(index_ref, count_ref, parts):
    migr = index_ref.shape[1]
    lane = iota((1, migr), 1)
    odd = [jnp.where(is_even(axis), 0, 1) for axis in ("gx", "gy")]
    rows = []
    for row in (odd[0], 1 - odd[0], 2 + odd[1], 3 - odd[1]):
        rows.append(jnp.where(lane < count_ref[0, row], index_ref[pl.ds(row, 1), :], parts))
    return jnp.concatenate(rows, axis=1)


def arrived_blocks(refs):
    yb, xb, ya, xa = [ref[...].astype(jnp.float32) for ref in refs]
    return ordered(xa, xb, "gx") + ordered(ya, yb, "gy")


def small_rows(rows, leaving, slots):
    leave = 2 * rows
    cells = leave + leaving // GROUP
    return rows, leave, cells, cells + slots // GROUP


def pick_kernel(
    part_hbm, index_hbm, count_hbm, size_hbm, owner_hbm, offset_hbm, closure_hbm, damping_hbm, cell_hbm, *refs
):
    out_hbm, small_hbm, refs = refs[:4], refs[4], refs[5:]
    part_ref, index_ref, count_ref, size_ref, owner_ref, offset_ref = refs[:6]
    closure_ref, damping_ref, cell_ref, out_ref, small_ref, sems, out_sems = refs[6:]
    channels, parts = part_ref.shape
    migr = index_ref.shape[1]
    slots = cell_ref.shape[1]
    groups = parts // GROUP
    rows, width = closure_ref.shape
    closure_row, leave_row, cell_row, _ = small_rows(rows, 4 * migr, slots)
    copies = fetch(
        [index_hbm, count_hbm, part_hbm, size_hbm, owner_hbm, offset_hbm, closure_hbm, damping_hbm, cell_hbm],
        [index_ref, count_ref, part_ref, size_ref, owner_ref, offset_ref, closure_ref, damping_ref, cell_ref],
        sems,
    )
    copies[0].wait()
    copies[1].wait()
    leave = leaving_row(index_ref, count_ref, parts)
    high = leave // GROUP
    low = ones(equal(GROUP, leave % GROUP))
    for copy in copies[3:]:
        copy.wait()
    for row, ref in enumerate((size_ref, owner_ref, offset_ref)):
        small_ref[row : row + 1, :] = ref[...].astype(jnp.float32)
    small_ref[closure_row:leave_row, :width] = closure_ref[...]
    diagonal = iota((rows, rows), 0) == iota((rows, rows), 1)
    damping = jnp.sum(jnp.where(diagonal, damping_ref[...], 0.0), axis=1, keepdims=True)
    small_ref[closure_row:leave_row, width : width + 1] = damping
    for first, line in ((leave_row, leave), (cell_row, cell_ref[...])):
        for k in range(line.shape[1] // GROUP):
            part = line[:, k * GROUP : (k + 1) * GROUP]
            small_ref[first + k : first + k + 1, :] = part.astype(jnp.float32)
    stores = [pltpu.make_async_copy(small_ref, small_hbm, out_sems.at[4])]
    stores[0].start()
    copies[2].wait()
    table = jnp.concatenate(
        [part_ref[:, g * GROUP : (g + 1) * GROUP].astype(jnp.bfloat16) for g in range(groups)], axis=0
    )
    free = jnp.where(iota((channels, migr), 0) == 0, FREE, 0.0)
    for r in range(4):
        where = slice(r * migr, (r + 1) * migr)
        found = dot(table, low[:, where])
        picked = free
        for g in range(groups):
            picked = jnp.where(high[:, where] == g, found[g * channels : (g + 1) * channels], picked)
        out_ref[r] = picked.astype(jnp.bfloat16)
        stores.append(pltpu.make_async_copy(out_ref.at[r], out_hbm[r], out_sems.at[r]))
        stores[-1].start()
    for store in stores:
        store.wait()


def mix(closure, state):
    state = state.astype(jnp.float32)
    mixed = closure[:, 0:1] * state[0:1]
    for f in range(1, state.shape[0]):
        mixed = mixed + closure[:, f : f + 1] * state[f : f + 1]
    return mixed, state[0:1]


def side_by_side(ref, first, begin, width):
    lanes = ref.shape[1]
    first = first + begin // lanes
    rows = [ref[r : r + 1, :] for r in range(first, first + width // lanes)]
    return jnp.concatenate(rows, axis=1)


def spread(mixed, first, place):
    hit = equal(TILE, place)
    values = jnp.concatenate([mixed, first], axis=0).astype(jnp.bfloat16)
    return jnp.concatenate(
        [jnp.where(hit, values[r : r + 1], jnp.bfloat16(0)) for r in range(values.shape[0])], axis=0
    )


def deposit_kernel(
    capacity, rows, leaving, part_ref, small_ref, sum_ref, code_ref, slot_ref, mark_ref, live_ref
):
    channels, parts = part_ref.shape
    slots = code_ref.shape[1]
    tiles = slot_ref.shape[1]
    groups = parts // GROUP
    closure_row, leave_row, cell_row, _ = small_rows(rows, leaving, slots)
    closure = small_ref[closure_row:leave_row, :channels]

    leave = side_by_side(small_ref, leave_row, 0, leaving).astype(jnp.int32)
    halves = [leave[:, : leaving // 2], leave[:, leaving // 2 :]]
    high = jnp.concatenate([ones(equal(2 * groups, half // LANES)) for half in halves], axis=0)
    low = jnp.concatenate([ones(equal(LANES, half % LANES)) for half in halves], axis=0)
    hits = dot(high, low, NT)
    live_ref[...] = 1.0 - (hits[: 2 * groups, :LANES] + hits[2 * groups :, LANES:])

    sizes, owners, offset = [small_ref[r : r + 1, :] for r in range(3)]
    offset = offset.astype(jnp.int32)
    square = (tiles, tiles)
    below, across = iota(square, 0), iota(square, 1)
    inputs = [sizes, owners, (offset % FZ).astype(jnp.float32), jnp.zeros((5, tiles), jnp.float32)]
    inputs = jnp.concatenate(inputs, axis=0).astype(jnp.bfloat16)
    turned = dot(ones(below == across), inputs, NT)
    start = dot(ones(across < below), inputs, NT)[:, 0:1].astype(jnp.int32)
    height = turned[:, 2:3].astype(jnp.int32)
    code = iota((tiles, 1), 0) * TILE + (height - start) % TILE
    code_step = code - jnp.concatenate([jnp.zeros((1, 1), jnp.int32), code[: tiles - 1]], axis=0)
    earlier = ones((turned[:, 1:2] == owners) & (below < across))
    rank = dot(jnp.ones((8, tiles), jnp.bfloat16), earlier)[0:1]
    slot_ref[...] = (owners * capacity + rank).astype(jnp.int32)
    starts = jnp.broadcast_to(start.astype(jnp.int16), (tiles, CHUNK))
    steps = jnp.broadcast_to(code_step.astype(jnp.int16), (tiles, CHUNK))
    lines = iota(mark_ref.shape, 0)
    marks = jnp.where(lines == 0, offset // FZ, jnp.where(lines == 1, offset % FZ, 0))
    mark_ref[...] = marks.astype(jnp.float32).astype(jnp.bfloat16)

    def find(begin):
        cell = side_by_side(small_ref, cell_row, begin, CHUNK).astype(jnp.int32)
        found = jnp.where(cell.astype(jnp.int16) >= starts, steps, jnp.int16(0))
        while found.shape[0] > 16:
            half = found.shape[0] // 2
            found = found[:half] + found[half:]
        found = jnp.sum(found.astype(jnp.int32), axis=0, keepdims=True) & 0xFFFF
        return found // TILE, (found + cell) % TILE

    for begin in range(parts, slots, CHUNK):
        tile, place = find(begin)
        code_ref[:, begin : begin + CHUNK] = tile * TILE + place
    for begin in range(0, parts, CHUNK):
        tile, place = find(begin)
        code_ref[:, begin : begin + CHUNK] = tile * TILE + place
        live = side_by_side(live_ref, 0, begin, CHUNK)
        state = part_ref[:, begin : begin + CHUNK] * live
        mixed, first = mix(closure, state.astype(jnp.bfloat16))
        added = dot(spread(mixed, first, place), ones(equal(tiles, tile)), NT)
        total = added if begin == 0 else total + added
    sum_ref[...] = total


def pack_kernel(rows, sum_ref, code_ref, slot_ref, mark_ref, small_ref, *refs):
    state_refs, out_ref = refs[:4], refs[4]
    channels, tiles = state_refs[0].shape[0], slot_ref.shape[1]
    closure = small_ref[rows : 2 * rows, :channels]
    code = code_ref[:, code_ref.shape[1] - 4 * state_refs[0].shape[1] :]
    state = jnp.concatenate(arrived_blocks(state_refs), axis=1)
    state = jnp.where(state[0:1] < FREE, state, 0.0)
    mixed, first = mix(closure, state)
    total = sum_ref[...] + dot(spread(mixed, first, code % TILE), ones(equal(tiles, code // TILE)), NT)
    table = jnp.concatenate([total.astype(jnp.bfloat16), mark_ref[...]], axis=0)
    match = one_hot(iota((out_ref.shape[0], tiles), 0) == slot_ref[...])
    out_ref[...] = dot(match, table, NT).astype(jnp.bfloat16)


def place_kernel(tile_ref, gas_ref, xa_ref, xb_ref):
    even = is_even("gx")
    count, lanes = tile_ref.shape
    width = gas_ref.shape[1] // 2
    marks = tile_ref[:, lanes - LANES :].astype(jnp.float32)
    column = marks[:, width % LANES : width % LANES + 1]
    height = marks[:, width % LANES + 1 : width % LANES + 2]
    lane = iota((1, LANES), 1)
    hot = one_hot(column == lane.astype(jnp.float32))
    place = (iota((1, width), 1) % TILE).astype(jnp.float32)
    values = tile_ref[:, :width].astype(jnp.float32)
    for half, mask in enumerate((place >= height, place < height)):
        total = dot(hot, jnp.where(mask, values, 0.0).astype(jnp.bfloat16), TN)
        where = slice(half * width, (half + 1) * width)
        gas_ref[:, where] = total[:COLS]
        rows = slice(half * FY, (half + 1) * FY)
        low, high = total[:FY], total[COLS - FY : COLS]
        xa_ref[rows, :] = jnp.where(even, high, low).astype(jnp.bfloat16)
        xb_ref[rows, :] = jnp.where(even, low, high).astype(jnp.bfloat16)


def unfold(ref):
    edge = ref[...].astype(jnp.float32)
    half = edge.shape[0] // 2
    return jnp.concatenate([edge[:half], edge[half:]], axis=1)


def along_kernel(gas_ref, xb_ref, xa_ref, out_ref, ya_ref, yb_ref):
    before, after = ordered(unfold(xa_ref), unfold(xb_ref), "gx")
    blocks = [before] + [gas_ref[x * FY : (x + 1) * FY, :] for x in range(FX)] + [after]
    along = [blocks[x] + 2.0 * blocks[x + 1] + blocks[x + 2] for x in range(FX)]
    for x in range(FX):
        out_ref[x * FY : (x + 1) * FY, :] = along[x]
    width = ya_ref.shape[1]
    edges = []
    for row in (0, FY - 1):
        edge = jnp.concatenate([along[x][row : row + 1] for x in range(FX)], axis=0)
        edges.append(jnp.concatenate([edge[:, :width], edge[:, width:]], axis=0))
    even = is_even("gy")
    ya_ref[...] = jnp.where(even, edges[1], edges[0]).astype(jnp.bfloat16)
    yb_ref[...] = jnp.where(even, edges[0], edges[1]).astype(jnp.bfloat16)


def drag_kernel(mark_ref, along_ref, yb_ref, ya_ref, drag_ref, back_ref):
    rows = drag_ref.shape[0]
    width = along_ref.shape[1] // 2
    lanes = rows * TILE
    before, after = ordered(unfold(ya_ref), unfold(yb_ref), "gy")
    smooth = []
    for x in range(FX):
        block = along_ref[x * FY : (x + 1) * FY, :]
        padded = jnp.concatenate([before[x : x + 1], block, after[x : x + 1]], axis=0)
        smooth.append((padded[0:FY] + 2.0 * block + padded[2 : FY + 2]) / 16.0)
    smooth = jnp.concatenate(smooth, axis=0)
    halves = []
    for half in range(2):
        base = half * width
        density = smooth[:, base + lanes : base + lanes + TILE]
        scale = 1.0 / (1.0 + density * density)
        halves.append(smooth[:, base : base + lanes] * jnp.concatenate([scale] * rows, axis=1))
    for r in range(rows):
        where = slice(r * TILE, (r + 1) * TILE)
        both = jnp.concatenate([halves[0][:, where], halves[1][:, where]], axis=1)
        drag_ref[r] = both.reshape(FX, FY, FZ).astype(jnp.bfloat16)
    mark = width % LANES
    marks = mark_ref[:, mark_ref.shape[1] - LANES :].astype(jnp.float32)
    column, height = marks[:, mark : mark + 1], marks[:, mark + 1 : mark + 2]
    hot = one_hot(column == iota((1, COLS), 1).astype(jnp.float32))
    place = (iota((1, lanes), 1) % TILE).astype(jnp.float32)
    low = dot(hot, halves[0].astype(jnp.bfloat16))
    high = dot(hot, halves[1].astype(jnp.bfloat16))
    back_ref[...] = jnp.where(place >= height, low, high).astype(jnp.bfloat16)


def force_kernel(back_ref, slot_ref, code_ref, part_ref, small_ref, live_ref, drag_ref, *refs):
    state_refs, (out_hbm, drag_hbm, out_ref, table_ref, sems) = refs[:4], refs[4:]
    stores = [pltpu.make_async_copy(drag_ref, drag_hbm, sems.at[0])]
    stores[0].start()

    def store(where):
        stores.append(pltpu.make_async_copy(out_ref.at[:, where], out_hbm.at[:, where], sems.at[len(stores)]))
        stores[-1].start()

    rows, slots = out_ref.shape
    parts = part_ref.shape[1]
    tiles = slot_ref.shape[1]
    migr = (slots - parts) // 4
    match = one_hot(iota((back_ref.shape[0], tiles), 0) == slot_ref[...])
    table_ref[...] = dot(back_ref[...], match, TN).astype(jnp.bfloat16)
    channels = part_ref.shape[0]
    damping = small_ref[rows : 2 * rows, channels : channels + 1]

    def look(code):
        values = dot(table_ref[...], ones(equal(tiles, code // TILE))).astype(jnp.bfloat16)
        hit = equal(TILE, code % TILE)
        found = []
        for r in range(rows):
            picked = jnp.where(hit, values[r * TILE : (r + 1) * TILE], jnp.bfloat16(0))
            while picked.shape[0] > 16:
                half = picked.shape[0] // 2
                picked = picked[:half] + picked[half:]
            found.append(jnp.sum(picked.astype(jnp.float32), axis=0, keepdims=True))
        return jnp.concatenate(found, axis=0)

    for begin in range(0, parts, CHUNK):
        where = slice(begin, begin + CHUNK)
        live = side_by_side(live_ref, 0, begin, CHUNK)
        out_ref[:, where] = live * (look(code_ref[:, where]) - damping * part_ref[:rows, where])
        store(where)
    drag = look(code_ref[:, parts:])
    for row, arrived in enumerate(arrived_blocks(state_refs)):
        begin = parts + row * migr
        live = jnp.where(arrived[0:1] < FREE, 1.0, 0.0)
        force = drag[:, row * migr : (row + 1) * migr] - damping * arrived[:rows]
        out_ref[:, begin : begin + migr] = live * force
    store(slice(parts, slots))
    for copy in stores:
        copy.wait()


def call(kernel, shapes, *operands, limit=None, late=(), scratch=()):
    vmem, hbm = pl.BlockSpec(memory_space=pltpu.VMEM), pl.BlockSpec(memory_space=pltpu.HBM)
    return pl.pallas_call(
        kernel,
        out_shape=shapes,
        in_specs=[hbm if limit else vmem] * len(operands),
        out_specs=[hbm if limit or i in late else vmem for i in range(len(shapes))],
        scratch_shapes=scratch,
        compiler_params=pltpu.CompilerParams(vmem_limit_bytes=limit or VMEM),
    )(*operands)


def per_device(
    particles,
    migrant_index,
    migrant_count,
    migrated_slot_cell,
    source_tile_size,
    tile_owner,
    tile_offset,
    closure,
    damping,
):
    f32, bf16, i32 = jnp.float32, jnp.bfloat16, jnp.int32
    shape = jax.ShapeDtypeStruct
    channels, parts = particles.shape
    rows = closure.shape[0]
    migr = migrant_index.shape[1]
    slots = migrated_slot_cell.shape[0]
    tiles = source_tile_size.shape[1]
    devices = lax.axis_size("gx") * lax.axis_size("gy")
    capacity = max(2, 2 * tiles // devices)
    count = devices * capacity
    width = (rows + 1) * TILE
    lanes = (width + LANES) // LANES * LANES
    small_count = small_rows(rows, 4 * migr, slots)[-1]
    operands = (
        particles, migrant_index, migrant_count, source_tile_size, tile_owner.reshape(1, tiles),
        tile_offset.reshape(1, tiles), closure, damping.reshape(1, rows), migrated_slot_cell.reshape(1, slots),
    )
    *leaving, small = call(
        pick_kernel,
        [shape((channels, migr), bf16)] * 4 + [shape((small_count, GROUP), f32)],
        *operands, limit=LARGE,
        scratch=[(pltpu.SMEM if i == 2 else pltpu.VMEM)(x.shape, x.dtype) for i, x in enumerate(operands)]
        + [pltpu.VMEM((4, channels, migr), bf16), pltpu.VMEM((small_count, GROUP), f32),
           pltpu.SemaphoreType.DMA((9,)), pltpu.SemaphoreType.DMA((5,))],
    )
    (xa, xb), (ya, yb) = exchange(*leaving[:2], "gx"), exchange(*leaving[2:], "gy")
    arrived = yb, xb, ya, xa
    sums, code, slot, marks, live = call(
        functools.partial(deposit_kernel, capacity, rows, 4 * migr),
        [shape((width, tiles), f32), shape((1, slots), i32), shape((1, tiles), i32),
         shape((lanes - width, tiles), bf16), shape((parts // LANES, LANES), f32)],
        particles, small,
    )
    (payload,) = call(
        functools.partial(pack_kernel, rows), [shape((count, lanes), bf16)],
        sums, code, slot, marks, small, *arrived,
    )
    received = lax.all_to_all(
        payload.reshape(devices, capacity, lanes), ("gx", "gy"), split_axis=0, concat_axis=0, tiled=True
    ).reshape(count, lanes)
    grid, edge = shape((COLS, 2 * width), f32), shape((2 * FX, width), bf16)
    gas, xa, xb = call(place_kernel, [grid, edge, edge], received)
    xa, xb = exchange(xa, xb, "gx")
    along, ya, yb = call(along_kernel, [grid, edge, edge], gas, xb, xa)
    ya, yb = exchange(ya, yb, "gy")
    drag, back = call(
        drag_kernel,
        [shape((rows, FX, FY, FZ), bf16), shape((count, rows * TILE), bf16)],
        received, along, yb, ya,
    )
    returned = lax.all_to_all(
        back.reshape(devices, capacity, rows * TILE), ("gx", "gy"), split_axis=0, concat_axis=0, tiled=True
    ).reshape(count, rows * TILE)
    force, drag = call(
        force_kernel, [shape((rows, slots), f32), shape(drag.shape, bf16)],
        returned, slot, code, particles, small, live, drag, *arrived, late=(0, 1),
        scratch=[pltpu.VMEM((rows, slots), f32), pltpu.VMEM((rows * TILE, tiles), bf16),
                 pltpu.SemaphoreType.DMA((2 + parts // CHUNK,))],
    )
    return drag, force


def solution(mesh):
    both = ("gx", "gy")
    in_specs = (
        P(None, both),
        P(both, None),
        P(both, None),
        P(both),
        P(both, None),
        P(both, None),
        P(both),
        P(),
        P(),
    )
    out_specs = (P(None, "gx", "gy", None), P(None, both))
    return jax.shard_map(
        per_device, mesh=mesh, in_specs=in_specs, out_specs=out_specs, check_vma=False
    )
```
